32 devices in a mesh: rows: 8 (over y, x, core), tp: 4 (over z).
Axes of the slice: x: 2, y: 2, z: 4, core: 2. Of those that a mesh axis runs over, the one named last changes fastest.
Arguments:
- tokens: bfloat16 [16, 1024, 1024], P('rows', 'tp'), may hold values from -6 to 6
- w_query: bfloat16 [1024, 1024], P('rows', 'tp'), may hold values from -0.1875 to 0.1875
- w_key: bfloat16 [1024, 1024], P('rows', 'tp'), may hold values from -0.1875 to 0.1875
- w_value: bfloat16 [1024, 1024], P('rows', 'tp'), may hold values from -0.1875 to 0.1875
- w_attn_out: bfloat16 [1024, 1024], P('tp', 'rows'), may hold values from -0.75 to 0.75
- w_up: bfloat16 [1024, 4096], P('rows', 'tp'), may hold values from -0.1875 to 0.1875
- w_down: bfloat16 [4096, 1024], P('tp', 'rows'), may hold values from -0.09375 to 0.09375
- first_gain: float32 [1024], replicated, may hold values from 0.5 to 1.5
- first_shift: float32 [1024], replicated, may hold values from -3 to 3
- second_gain: float32 [1024], replicated, may hold values from 0.5 to 1.5
- second_shift: float32 [1024], replicated, may hold values from -3 to 3
- prefix_keys: bfloat16 [4, 100, 1024], P(None, None, 'tp'), may hold values from -6 to 6
- prefix_values: bfloat16 [4, 100, 1024], P(None, None, 'tp'), may hold values from -6 to 6
- example_lengths: int32 [16, 8], P('rows'), may hold values from 1 to 512, 1024 in all within a row
- task_ids: int32 [16], P('rows'), may hold values from 0 to 3
- prefix_lens: int32 [4], replicated, may hold values from 20 to 100, as said below
- slot_masks: int32 [4, 100], replicated, may hold values 0 or 1
- out_grad: bfloat16 [16, 1024, 1024], P('rows', 'tp'), may hold values from -6 to 6
Outputs:
- output: bfloat16 [16, 1024, 1024], P('rows', 'tp')
- tokens_grad: float32 [16, 1024, 1024], P('rows', 'tp')
- prefix_keys_grad: float32 [4, 100, 1024], P(None, None, 'tp')
- prefix_values_grad: float32 [4, 100, 1024], P(None, None, 'tp')
The draws below stay inside these ranges and needn't reach their ends.
Inputs may be any that keep to these rules, and one draw needn't show every extreme that they name: `prefix_lens`: each of 20, 64 and 100 is the prefix length of some task, and no other value occurs. `example_lengths`: the 8 lengths of a row sum to 1024.
All inputs are finite; a program needn't handle non-finite values.
Results may differ from the reference program's by a relative error of at most 0.014.
Values may be sent and summed in bfloat16 or wider, within the bound.
A program may use at most 192 MiB of HBM per device.

```python
import math
import jax
import jax.numpy as jnp
import numpy as np
from jax import lax

HD = 64
FF = 4096
D = 1024
PREFIX = 100
NTASK = 4
NEX = 8
LEN = 1024
ROWS = 16


def draw_prefix_lens(key, part):
    key = jax.random.fold_in(key, 17)
    table = jnp.array([20, 64, 100], dtype=jnp.int32)
    leading = jax.random.permutation(jax.random.fold_in(key, 1), 3).astype(jnp.int32)
    others = jax.random.randint(jax.random.fold_in(key, 2), (NTASK,), 0, 3, dtype=jnp.int32)
    picks = others.at[:3].set(leading)
    return table[picks]


def touch_ends(entries, rng, smallest, largest):
    longest = entries.shape.index(max(entries.shape))
    spots = []
    for shift in (0, 1):
        where = [jax.random.randint(jax.random.fold_in(rng, axis), (), 0, length) for axis, length in enumerate(entries.shape)]
        where[longest] = (where[longest] + shift) % entries.shape[longest]
        spots.append(tuple(where))
    return entries.at[spots[0]].set(smallest).at[spots[1]].set(largest)


def level_of(stream_key, dims, cuts, least, high):
    loudness, own = 1.0, jax.random.fold_in(stream_key, 6)
    for position, shards_of in cuts:
        heights = jnp.exp(jax.random.uniform(jax.random.fold_in(own, position), (shards_of,), jnp.float32, least / len(cuts), high / len(cuts)))
        loudness = loudness * jnp.repeat(heights, dims[position] // shards_of).reshape([-1 if axis == position else 1 for axis in range(len(dims))])
    return loudness


def length_profile(amount, total, bound, lean):
    loads = [(1 << 20) // math.isqrt(rank ** lean) + 1 for rank in range(2, amount + 1)]
    surplus, counts = total - bound - (amount - 1), [1] * (amount - 1)
    while surplus > 0:
        candidates = [i for i in range(amount - 1) if counts[i] < bound]
        whole, left = sum([loads[i] for i in candidates]), surplus
        for i in candidates:
            more = min(bound - counts[i], max(1, left * loads[i] // whole), surplus)
            counts[i] = counts[i] + more
            surplus = surplus - more
    return np.array([bound] + counts)


def uneven(own_key, number_of, total, reach, skew):
    if number_of == 2:
        one = jax.random.randint(own_key, (), max(1, total - reach), min(reach, total - 1) + 1)
        return jnp.stack([one, total - one])
    sizes = jnp.asarray(length_profile(number_of, total, reach, skew), jnp.int32)
    couples = (number_of - 1) // 2
    giver, receiver = sizes[1:1 + 2 * couples:2], sizes[2:2 + 2 * couples:2]
    margin = jnp.minimum(giver - 1, reach - receiver)
    shifted = jax.random.randint(jax.random.fold_in(own_key, 1), (couples,), 0, 1 << 20) % (margin + 1)
    sizes = sizes.at[1:1 + 2 * couples:2].set(giver - shifted).at[2:2 + 2 * couples:2].set(receiver + shifted)
    return sizes[jax.random.permutation(jax.random.fold_in(own_key, 2), number_of)]


def gaussian(key, extent, scale, most, split=(), kind=jnp.bfloat16):
    drawn = jax.random.normal(key, extent, jnp.float32) * scale
    if len(split) > 0:
        drawn = level_of(key, extent, split, -0.22, 0.18) * drawn
    return jnp.clip(drawn, min=-most, max=most).astype(kind)


def setup_inputs(seed: int = 0) -> dict:
    key_list = jax.random.split(jax.random.key(seed), 19)
    tokens = gaussian(key_list[0], (ROWS, LEN, D), 1.0, 6.0, ((0, 8), (1, 4)))
    w_query = gaussian(key_list[1], (D, D), D ** -0.5, 0.1875, ((0, 8), (1, 4)))
    w_key = gaussian(key_list[2], (D, D), D ** -0.5, 0.1875, ((0, 8), (1, 4)))
    w_value = gaussian(key_list[3], (D, D), D ** -0.5, 0.1875, ((0, 8), (1, 4)))
    w_attn_out = gaussian(key_list[4], (D, D), (D // 16) ** -0.5, 0.75, ((0, 4), (1, 8)))
    w_up = gaussian(key_list[5], (D, FF), D ** -0.5, 0.1875, ((0, 8), (1, 4)))
    w_down = gaussian(key_list[6], (FF, D), FF ** -0.5, 0.09375, ((0, 4), (1, 8)))
    first_gain = jnp.clip(1.0 + 0.1 * jax.random.normal(key_list[7], (D,), jnp.float32), 0.5, 1.5)
    first_shift = gaussian(key_list[8], (D,), 0.5, 3.0, (), jnp.float32)
    second_gain = jnp.clip(1.0 + 0.1 * jax.random.normal(key_list[9], (D,), jnp.float32), 0.5, 1.5)
    second_shift = gaussian(key_list[10], (D,), 0.5, 3.0, (), jnp.float32)
    prefix_keys = gaussian(key_list[11], (NTASK, PREFIX, D), 1.0, 6.0, ((2, 4),))
    prefix_values = gaussian(key_list[12], (NTASK, PREFIX, D), 1.0, 6.0, ((2, 4),))
    example_lengths = jax.vmap(lambda own: uneven(own, NEX, LEN, LEN // 2, 2))(jax.random.split(key_list[13], ROWS)).reshape((ROWS, NEX)).astype(jnp.int32)
    task_ids = touch_ends(jax.random.randint(key_list[14], (ROWS,), 0, NTASK), jax.random.fold_in(key_list[14], 1), 0, NTASK - 1).astype(jnp.int32)
    prefix_lens = draw_prefix_lens(jax.random.fold_in(key_list[18], 71), 0)
    slot_masks = touch_ends((jax.random.randint(key_list[16], (NTASK, PREFIX), 0, 4) < 3).astype(jnp.int32), jax.random.fold_in(key_list[16], 1), 0, 1)
    out_grad = gaussian(key_list[17], (ROWS, LEN, D), 1.0, 6.0, ((0, 8), (1, 4)))
    return {"tokens": tokens, "w_query": w_query, "w_key": w_key, "w_value": w_value, "w_attn_out": w_attn_out, "w_up": w_up, "w_down": w_down, "first_gain": first_gain, "first_shift": first_shift, "second_gain": second_gain, "second_shift": second_shift, "prefix_keys": prefix_keys, "prefix_values": prefix_values, "example_lengths": example_lengths, "task_ids": task_ids, "prefix_lens": prefix_lens, "slot_masks": slot_masks, "out_grad": out_grad}


@jax.custom_vjp
def low(v):
    return lax.optimization_barrier(v.astype(jnp.bfloat16)).astype(jnp.float32)

@jax.custom_vjp
def low_back(v):
    return v

def low_keep(v):
    return (low(v), None)

def low_pass(kept, grad):
    return (grad,)

def back_keep(v):
    return (v, None)

def back_low(kept, grad):
    return (low(grad),)
low.defvjp(low_keep, low_pass)
low_back.defvjp(back_keep, back_low)
highest = lax.Precision.HIGHEST

def layer_norm(z, gain, shift):
    mean = lax.optimization_barrier(jnp.mean(z, axis=-1, keepdims=True))
    centred = z - mean
    spread = lax.optimization_barrier(jnp.mean(centred * centred, axis=-1, keepdims=True))
    return centred * lax.rsqrt(spread + 1e-05) * gain + shift

def reference(tokens, w_query, w_key, w_value, w_attn_out, w_up, w_down, first_gain, first_shift, second_gain, second_shift, prefix_keys, prefix_values, example_lengths, task_ids, prefix_lens, slot_masks, out_grad):
    f32 = jnp.float32
    wq = w_query.astype(f32)
    wk = w_key.astype(f32)
    wv = w_value.astype(f32)
    wao = w_attn_out.astype(f32)
    wup = w_up.astype(f32)
    wdn = w_down.astype(f32)
    gain_one = first_gain.astype(f32)
    shift_one = first_shift.astype(f32)
    gain_two = second_gain.astype(f32)
    shift_two = second_shift.astype(f32)
    length = tokens.shape[1]
    heads = D // HD
    ends = jnp.cumsum(example_lengths, axis=1)
    places = jnp.arange(length, dtype=jnp.int32)
    segment = lax.optimization_barrier(jnp.sum((places[None, :, None] >= ends[:, None, :]).astype(jnp.int32), axis=-1))
    slots = jnp.arange(PREFIX, dtype=jnp.int32)
    valid_table = (slots[None, :] < prefix_lens[:, None]) & (slot_masks == 1)

    def forward(inputs, pre_keys, pre_values):

        def one_row(packed):
            x_row, seg_row, task = packed
            query = low_back(low(jnp.dot(x_row, wq, precision=highest)))
            key_seq = low_back(low(jnp.dot(x_row, wk, precision=highest)))
            value_seq = low_back(low(jnp.dot(x_row, wv, precision=highest)))
            keys = jnp.concatenate([pre_keys[task], key_seq], axis=0).reshape(PREFIX + length, heads, HD)
            values = jnp.concatenate([pre_values[task], value_seq], axis=0).reshape(PREFIX + length, heads, HD)
            scores = jnp.einsum('qhd,khd->hqk', query.reshape(length, heads, HD), keys, precision=highest)
            scores = low_back(0.125 * scores)
            allowed = jnp.concatenate([jnp.broadcast_to(valid_table[task][None, :], (length, PREFIX)), seg_row[:, None] == seg_row[None, :]], axis=1)
            scores = jnp.where(allowed[None], scores, -1e+30)
            probs = low(jax.nn.softmax(scores, axis=-1))
            mixed = jnp.einsum('hqk,khd->qhd', probs, values, precision=highest).reshape(length, D)
            mixed = low_back(low(mixed))
            first_sum = x_row + low_back(jnp.dot(mixed, wao, precision=highest))
            normed = low(layer_norm(first_sum, gain_one, shift_one))
            upper = low_back(jnp.dot(normed, wup, precision=highest))
            acted = low(jax.nn.gelu(upper, approximate=False))
            second_sum = normed + low_back(jnp.dot(acted, wdn, precision=highest))
            return layer_norm(second_sum, gain_two, shift_two)
        return lax.map(jax.checkpoint(one_row), (inputs, segment, task_ids))
    result, pull = jax.vjp(forward, tokens.astype(f32), prefix_keys.astype(f32), prefix_values.astype(f32))
    d_tokens, d_keys, d_values = pull(out_grad.astype(f32))
    return (result.astype(jnp.bfloat16), d_tokens, d_keys, d_values)
```

```python
import functools
import jax
import jax.numpy as jnp
from jax import lax
from jax.experimental import pallas as pl
from jax.experimental.pallas import tpu as pltpu
from jax.sharding import PartitionSpec as P


HD = 64
PAIR = 2 * HD
SLOTS = 128
QB = 256
KB = 256
NEG = -1e30
NT = (((1,), (1,)), ((), ()))


def mm(a, b):
    return jnp.dot(a, b, preferred_element_type=jnp.float32)


def mm_nt(a, b):
    return lax.dot_general(a, b, NT, preferred_element_type=jnp.float32)


def head_lanes(half):
    lane = lax.broadcasted_iota(jnp.int32, (1, PAIR), 1)
    return (lane >= half * HD) & (lane < (half + 1) * HD)


def only_head(a, half):
    return jnp.where(head_lanes(half), a, jnp.zeros_like(a))


def attend_block(q, keys, values, seg_col, seg_row, live_row):
    mixed = jnp.zeros((q.shape[0], PAIR), jnp.float32)
    totals = jnp.zeros((q.shape[0], PAIR), jnp.float32)
    lane = lax.broadcasted_iota(jnp.int32, (1, PAIR), 1)
    for half in range(2):
        qh = only_head(q, half) * jnp.asarray(0.125, jnp.bfloat16)
        scores = mm_nt(qh, keys)
        seq = jnp.where(seg_col == seg_row, scores[:, SLOTS:], NEG)
        pre = jnp.where(live_row > 0.5, scores[:, :SLOTS], NEG)
        top = jnp.maximum(
            jnp.max(seq, axis=1, keepdims=True), jnp.max(pre, axis=1, keepdims=True)
        )
        seq = jnp.exp(seq - top)
        pre = jnp.exp(pre - top)
        total = jnp.sum(seq, axis=1, keepdims=True) + jnp.sum(pre, axis=1, keepdims=True)
        scale = 1.0 / total
        low = jnp.concatenate([(pre * scale).astype(jnp.bfloat16), (seq * scale).astype(jnp.bfloat16)], axis=1)
        out = mm(low, values)
        mixed = jnp.where(head_lanes(half), out, mixed)
        totals = jnp.where(lane == half, top + jnp.log(total), totals)
    return mixed.astype(jnp.bfloat16), totals


def forward_kernel(q_ref, k_ref, v_ref, pk_ref, pv_ref, meta_ref, seg_ref, att_ref, lse_ref, keys, values):
    keys[0:SLOTS, :] = pk_ref[...]
    keys[SLOTS:, :] = k_ref[...]
    values[0:SLOTS, :] = pv_ref[...]
    values[SLOTS:, :] = v_ref[...]

    def block(b, carry):
        rows = pl.ds(pl.multiple_of(b * QB, QB), QB)
        mixed, totals = attend_block(
            q_ref[rows, :], keys[...], values[...], seg_ref[rows, 0:1],
            meta_ref[0:1, SLOTS:], meta_ref[0:1, :SLOTS],
        )
        att_ref[rows, :] = mixed
        lse_ref[0, :, rows] = jnp.transpose(totals)[0:8, :]
        return carry

    lax.fori_loop(0, q_ref.shape[0] // QB, block, 0)


def attend_forward(q, k, v, pk, pv, meta, seg_col):
    length, width = q.shape
    pairs = width // PAIR
    block = pl.BlockSpec((length, PAIR), lambda p: (0, p))
    pre = pl.BlockSpec((SLOTS, PAIR), lambda p: (0, p))
    whole = lambda a: pl.BlockSpec(a.shape, lambda p: (0,) * a.ndim)
    return pl.pallas_call(
        forward_kernel,
        grid=(pairs,),
        in_specs=[block, block, block, pre, pre, whole(meta), whole(seg_col)],
        out_specs=[block, pl.BlockSpec((1, 8, length), lambda p: (p, 0, 0))],
        out_shape=[
            jax.ShapeDtypeStruct((length, width), jnp.bfloat16),
            jax.ShapeDtypeStruct((pairs, 8, length), jnp.float32),
        ],
        scratch_shapes=[
            pltpu.VMEM((SLOTS + length, PAIR), jnp.bfloat16),
            pltpu.VMEM((SLOTS + length, PAIR), jnp.bfloat16),
        ],
        compiler_params=pltpu.CompilerParams(vmem_limit_bytes=48 * 2**20),
    )(q, k, v, pk, pv, meta, seg_col)


def backward_kernel(
    bounds_ref, q_ref, k_ref, v_ref, do_ref, att_ref, pk_ref, pv_ref, lse_ref, meta_ref, seg_ref, live_ref,
    dq_ref, dk_ref, dv_ref, dpk_ref, dpv_ref,
    dk_acc, dv_acc, dpk_acc, dpv_acc, k_t, pk_t,
):
    length = q_ref.shape[0]
    dk_acc[...] = jnp.zeros_like(dk_acc)
    dv_acc[...] = jnp.zeros_like(dv_acc)
    dpk_acc[...] = jnp.zeros_like(dpk_acc)
    dpv_acc[...] = jnp.zeros_like(dpv_acc)
    k_t[...] = jnp.transpose(k_ref[...])
    pk_t[...] = jnp.transpose(pk_ref[...])
    picks = lax.broadcasted_iota(jnp.int32, (8, PAIR), 0)
    lanes = lax.broadcasted_iota(jnp.int32, (8, PAIR), 1) // HD
    picker = jnp.where(picks == lanes, 1.0, 0.0)

    def block(b, carry):
        start = pl.multiple_of(b * QB, QB)
        rows = pl.ds(start, QB)
        q = q_ref[rows, :]
        do = do_ref[rows, :]
        prod = do.astype(jnp.float32) * att_ref[rows, :].astype(jnp.float32)
        inner = lax.dot_general(
            picker, prod, NT, preferred_element_type=jnp.float32, precision=lax.Precision.HIGHEST
        )
        seg_q = meta_ref[0:1, pl.ds(SLOTS + start, QB)]
        heads = []
        for half in range(2):
            qh = only_head(q, half) * jnp.asarray(0.125, jnp.bfloat16)
            dh = only_head(do, half)
            lse = lse_ref[0, half : half + 1, rows]
            delta = inner[half : half + 1, :]
            heads.append((qh, dh, lse, delta))

        def tile(kk, vv, kt, allowed, half):
            qh, dh, lse, delta = heads[half]
            s = mm_nt(kk, qh)
            p = jnp.exp(jnp.where(allowed, s, NEG) - lse)
            dp = mm_nt(vv, dh)
            ds = (p * (dp - delta)).astype(jnp.bfloat16)
            return mm(ds, qh), mm(p.astype(jnp.bfloat16), dh), mm(kt, ds)

        dqs = []
        for half in range(2):
            a, g, dq = tile(
                pk_ref[...], pv_ref[...], pk_t[half * HD : (half + 1) * HD, :], live_ref[:, 0:1] > 0.5, half
            )
            dpk_acc[...] += a
            dpv_acc[...] += g
            dqs.append(dq)

        def step(j, dqs):
            at = pl.multiple_of(j * KB, KB)
            krows = pl.ds(at, KB)
            allowed = seg_ref[krows, 0:1] == seg_q
            dk = dk_acc[krows, :]
            dv = dv_acc[krows, :]
            outs = []
            for half in range(2):
                a, g, dq = tile(
                    k_ref[krows, :], v_ref[krows, :], k_t[half * HD : (half + 1) * HD, krows], allowed, half
                )
                dk = dk + a
                dv = dv + g
                outs.append(dqs[half] + dq)
            dk_acc[krows, :] = dk
            dv_acc[krows, :] = dv
            return tuple(outs)

        dqs = lax.fori_loop(bounds_ref[0, b], bounds_ref[1, b], step, tuple(dqs))
        dq_ref[rows, :] = (jnp.transpose(jnp.concatenate(dqs, axis=0)) * 0.125).astype(jnp.bfloat16)
        return carry

    lax.fori_loop(0, length // QB, block, 0)
    dk_ref[...] = dk_acc[...].astype(jnp.bfloat16)
    dv_ref[...] = dv_acc[...].astype(jnp.bfloat16)
    dpk_ref[...] = dpk_acc[...]
    dpv_ref[...] = dpv_acc[...]


def attend_backward(bounds, q, k, v, do, att, pk, pv, lse, meta, seg_col, live_col):
    length, width = q.shape
    pairs = width // PAIR
    block = pl.BlockSpec((length, PAIR), lambda p, *_: (0, p))
    pre = pl.BlockSpec((SLOTS, PAIR), lambda p, *_: (0, p))
    whole = lambda a: pl.BlockSpec(a.shape, lambda p, *_: (0,) * a.ndim)
    low = jax.ShapeDtypeStruct((length, width), jnp.bfloat16)
    full = jax.ShapeDtypeStruct((SLOTS, width), jnp.float32)
    return pl.pallas_call(
        backward_kernel,
        grid_spec=pltpu.PrefetchScalarGridSpec(
            num_scalar_prefetch=1,
            grid=(pairs,),
            in_specs=[
                block, block, block, block, block, pre, pre,
                pl.BlockSpec((1, 8, length), lambda p, *_: (p, 0, 0)),
                whole(meta), whole(seg_col), whole(live_col),
            ],
            out_specs=[block, block, block, pre, pre],
            scratch_shapes=[
                pltpu.VMEM((length, PAIR), jnp.float32),
                pltpu.VMEM((length, PAIR), jnp.float32),
                pltpu.VMEM((SLOTS, PAIR), jnp.float32),
                pltpu.VMEM((SLOTS, PAIR), jnp.float32),
                pltpu.VMEM((PAIR, length), jnp.bfloat16),
                pltpu.VMEM((PAIR, SLOTS), jnp.bfloat16),
            ],
        ),
        out_shape=[low, low, low, full, full],
        compiler_params=pltpu.CompilerParams(vmem_limit_bytes=48 * 2**20),
    )(bounds, q, k, v, do, att, pk, pv, lse, meta, seg_col, live_col)


def block_bounds(seg):
    length = seg.shape[0]
    first = seg[::QB]
    last = seg[QB - 1 :: QB]
    low = jnp.sum((seg[None, :] < first[:, None]).astype(jnp.int32), axis=1)
    high = jnp.sum((seg[None, :] <= last[:, None]).astype(jnp.int32), axis=1)
    return jnp.stack([low // KB, (high + KB - 1) // KB])


MESH = pl.DeviceIdType.MESH
LINE = 4
LANES = 128


class Plan:
    def __init__(self, rows, tp):
        self.rows = rows
        self.tp = tp
        self.core_in_tp = tp > LINE
        self.shape = (rows // 8, 2, 4) if self.core_in_tp else (rows // 4, 2, 2)
        self.axes = (0, 1, 2) if self.core_in_tp else (0, 1)
        self.cores = 2 if self.core_in_tp else 1

    def here(self):
        r = lax.axis_index("rows")
        t = lax.axis_index("tp")
        a, b, c = self.shape
        coords = (r // (b * c), lax.rem(r // c, b), lax.rem(r, c))
        if self.core_in_tp:
            return coords, t // 2, lax.rem(t, 2)
        return coords, t, coords[2]

    def device(self, coords, line, core):
        a, b, c = self.shape
        if self.core_in_tp:
            return ((coords[0] * b + coords[1]) * c + coords[2], line * 2 + core)
        return ((coords[0] * b + coords[1]) * c + core, line)


def shifted(coords, axis, by, size):
    moved = list(coords)
    moved[axis] = lax.rem(coords[axis] + by, size)
    return tuple(moved)


def sibling(plan, coords, line, core):
    return plan.device(coords, line, 1 - core)


def greet(plan, coords, line, core):
    others = [
        plan.device(coords, lax.rem(line + by, LINE), side) for by in range(1, LINE) for side in range(2)
    ]
    others.append(sibling(plan, coords, line, core))
    for axis in plan.axes:
        for by in range(1, plan.shape[axis]):
            others.append(plan.device(shifted(coords, axis, by, plan.shape[axis]), line, core))
    barrier = pltpu.get_barrier_semaphore()
    for other in others:
        pl.semaphore_signal(barrier, inc=1, device_id=other, device_id_type=MESH)
    pl.semaphore_wait(barrier, len(others))


class Gather:
    def __init__(self, plan, place, source, whole, sems):
        self.plan = plan
        self.coords, self.line, self.core = place
        self.source = source
        self.whole = whole
        self.sems = sems
        self.count = source.shape[0] * (1 if plan.core_in_tp else 2)
        self.depth = source.shape[-2]
        self.orders = (plan.axes, plan.axes[::-1])

    def unit(self, i):
        if self.plan.core_in_tp:
            return (i, self.core)
        return (i // 2, lax.rem(i, 2))

    def remote(self, src, dst, send, recv, device):
        return pltpu.make_async_remote_copy(
            src_ref=src, dst_ref=dst, send_sem=send, recv_sem=recv, device_id=device, device_id_type=MESH
        )

    def own(self):
        lanes = pl.ds(pl.multiple_of(self.line * LANES, LANES), LANES)
        where = (slice(None),) + tuple(self.coords) + (slice(None), lanes)
        if self.plan.core_in_tp:
            pairs = [(self.source, self.whole.at[(slice(None), self.core) + where[1:]])]
        else:
            pairs = [
                (self.source.at[:, side], self.whole.at[(slice(None), side) + where[1:]]) for side in range(2)
            ]
        return pairs

    def line_copies(self, i):
        lanes = pl.ds(pl.multiple_of(self.line * LANES, LANES), LANES)
        unit = self.unit(i)
        src = self.source.at[i] if self.plan.core_in_tp else self.source.at[unit]
        dst = self.whole.at[unit + tuple(self.coords) + (slice(None), lanes)]
        for by in range(1, LINE):
            yield self.remote(
                src, dst, self.sems["line_send"].at[i, by - 1], self.sems["line_recv"].at[i, by - 1],
                self.plan.device(self.coords, lax.rem(self.line + by, LINE), self.core),
            )

    def axis_copies(self, i, step):
        rows = self.depth // 2
        for half in range(2):
            order = self.orders[half]
            axis = order[step]
            size = self.plan.shape[axis]
            index = [
                pl.ds(0, self.plan.shape[a]) if a in order[:step] else self.coords[a] for a in range(3)
            ]
            block = self.whole.at[self.unit(i) + tuple(index) + (pl.ds(half * rows, rows),)]
            for by in range(1, size):
                spot = (i, half, step, by - 1)
                yield self.remote(
                    block, block, self.sems["axis_send"].at[spot], self.sems["axis_recv"].at[spot],
                    self.plan.device(shifted(self.coords, axis, by, size), self.line, self.core),
                )

    def core_copy(self, i, side):
        if self.plan.core_in_tp:
            block = self.whole.at[i, side]
        else:
            block = self.whole.at[self.unit(i) + (slice(None), slice(None), side)]
        return self.remote(
            block, block, self.sems["core_send"].at[i], self.sems["core_recv"].at[i],
            sibling(self.plan, self.coords, self.line, self.core),
        )

    def core_roles(self, i):
        if self.plan.core_in_tp:
            wide = i >= 3
            return wide, wide
        side = lax.rem(i, 2)
        wide = i >= 6
        return wide | (side != self.core), wide | (side == self.core)

    def start_line(self, i):
        for copy in self.line_copies(i):
            copy.start()

    def start_axis(self, i, step):
        waits = self.line_copies(i) if step == 0 else self.axis_copies(i, step - 1)
        for copy in waits:
            copy.wait_recv()
        for copy in self.axis_copies(i, step):
            copy.start()

    def start_core(self, i):
        for copy in self.axis_copies(i, len(self.plan.axes) - 1):
            copy.wait_recv()
        sends, _ = self.core_roles(i)

        @pl.when(sends)
        def _():
            self.core_copy(i, self.core).start()

    def finish(self, i):
        _, gets = self.core_roles(i)

        @pl.when(gets)
        def _():
            self.core_copy(i, 1 - self.core).wait_recv()

    def drain(self, i):
        for copy in self.line_copies(i):
            copy.wait_send()
        for step in range(len(self.plan.axes)):
            for copy in self.axis_copies(i, step):
                copy.wait_send()
        sends, _ = self.core_roles(i)

        @pl.when(sends)
        def _():
            self.core_copy(i, self.core).wait_send()


def gather_semaphores(plan, count):
    steps = len(plan.axes)
    reach = max(plan.shape[a] for a in plan.axes) - 1
    shapes = {
        "line_send": (count, LINE - 1),
        "line_recv": (count, LINE - 1),
        "axis_send": (count, 2, steps, reach),
        "axis_recv": (count, 2, steps, reach),
        "core_send": (count,),
        "core_recv": (count,),
    }
    return {name: pltpu.SemaphoreType.DMA(shape) for name, shape in shapes.items()}


class Line:
    def __init__(self, plan, place, name, sems):
        self.plan = plan
        self.coords, self.line, self.core = place
        self.send_sems = sems[name + "_send"]
        self.recv_sems = sems[name + "_recv"]
        self.pieces = []

    def here(self, chip, side):
        return (chip == self.line) & (side == self.core)

    def send(self, src, dst, chip, side):
        at = len(self.pieces)
        far = pltpu.make_async_remote_copy(
            src_ref=src, dst_ref=dst, send_sem=self.send_sems.at[at],
            recv_sem=self.recv_sems.at[self.line, self.core],
            device_id=self.plan.device(self.coords, chip, side), device_id_type=MESH,
        )
        near = pltpu.make_async_copy(src, dst, self.send_sems.at[at])
        stays = self.here(chip, side)
        self.pieces.append((stays, far, near))
        pl.when(jnp.logical_not(stays))(far.start)
        pl.when(stays)(near.start)

    def settle(self):
        for stays, _, near in self.pieces:
            pl.when(stays)(near.wait)

    def drain(self):
        for stays, far, _ in self.pieces:
            pl.when(jnp.logical_not(stays))(far.wait_send)

    def receive(self, dst, chip, side):
        copy = pltpu.make_async_remote_copy(
            src_ref=dst, dst_ref=dst, send_sem=self.send_sems.at[0], recv_sem=self.recv_sems.at[chip, side],
            device_id=self.plan.device(self.coords, chip, side), device_id_type=MESH,
        )
        pl.when(jnp.logical_not(self.here(chip, side)))(copy.wait_recv)


def line_semaphores(name, count):
    return {
        name + "_send": pltpu.SemaphoreType.DMA((count,)),
        name + "_recv": pltpu.SemaphoreType.DMA((LINE, 2)),
    }


def gather_kernel(plan, names, source, tokens, grads, prefix, meta, whole, row, grad, pre, row_meta, *sems):
    sems = dict(zip(names, sems))
    place = plan.here()
    coords, line, core = place
    greet(plan, coords, line, core)
    rows_here = tokens.shape[0]
    spread = plan.core_in_tp
    base = 0 if spread else 2 * core
    slot = core if spread else 0
    holds = (line // 2 == core) if not spread else None
    other = sibling(plan, coords, line, core)

    def held(body):
        if holds is None:
            body()
        else:
            pl.when(holds)(body)

    lanes = pl.ds(pl.multiple_of(line * LANES, LANES), LANES)
    token_line = Line(plan, place, "token", sems)
    for j in range(rows_here):
        token_line.send(tokens.at[j], row.at[line, slot], base + j, core)
    gather = Gather(plan, place, source, whole, sems)
    own = [
        pltpu.make_async_copy(src, dst, sems["own"].at[i]) for i, (src, dst) in enumerate(gather.own())
    ]
    for copy in own:
        copy.start()
    lax.fori_loop(0, gather.count, lambda i, x: (gather.start_line(i), x)[1], 0)
    prefix_line = Line(plan, place, "prefix", sems)
    grad_line = Line(plan, place, "grad", sems)
    for j in range(rows_here):
        for side in range(2 // plan.cores):
            prefix_line.send(prefix.at[j, side], pre.at[:, :, lanes], base + j, core if spread else side)
    for j in range(rows_here):
        grad_line.send(grads.at[j], grad.at[lax.rem(line, 2), slot], base + j, line // 2)

    mine = line if spread else lax.rem(line, 2)
    meta_far = pltpu.make_async_remote_copy(
        src_ref=meta.at[mine], dst_ref=row_meta, send_sem=sems["meta"].at[0], recv_sem=sems["meta"].at[1],
        device_id=other, device_id_type=MESH,
    )
    meta_near = pltpu.make_async_copy(meta.at[mine], row_meta, sems["meta"].at[2])
    if spread:
        meta_near.start()
        meta_near.wait()
    else:
        @pl.when(holds)
        def _():
            meta_near.start()
            meta_far.start()
            meta_near.wait()
            meta_far.wait_send()

        @pl.when(jnp.logical_not(holds))
        def _():
            meta_far.wait_recv()

    for copy in own:
        copy.wait()

    token_line.settle()
    mine = row.at[:, slot]
    share = pltpu.make_async_remote_copy(
        src_ref=mine, dst_ref=mine, send_sem=sems["share"].at[0], recv_sem=sems["share"].at[1],
        device_id=other, device_id_type=MESH,
    )

    @held
    def _():
        for chip in range(LINE):
            token_line.receive(row.at[chip, slot], chip, core)
        share.start()
        share.wait_send()

    if spread:
        share.wait_recv()
    else:
        pl.when(jnp.logical_not(holds))(share.wait_recv)

    steps = len(plan.axes)
    lag = 2

    def tick(i, x):
        for step in range(steps + 1):
            at = i - lag * step

            def go(step=step, at=at):
                if step < steps:
                    gather.start_axis(at, step)
                else:
                    gather.start_core(at)

            pl.when((at >= 0) & (at < gather.count))(go)
        return x

    lax.fori_loop(0, gather.count + lag * steps, tick, 0)
    lax.fori_loop(0, gather.count, lambda i, x: (gather.finish(i), x)[1], 0)
    lax.fori_loop(0, gather.count, lambda i, x: (gather.drain(i), x)[1], 0)

    prefix_line.settle()
    grad_line.settle()
    for chip in range(LINE):
        prefix_line.receive(pre.at[:, :, pl.ds(chip * LANES, LANES)], chip, core if spread else line // 2)
    for part in range(2):
        for side in range(plan.cores):
            grad_line.receive(grad.at[part, side], 2 * core + part, side if spread else line // 2)
    token_line.drain()
    prefix_line.drain()
    grad_line.drain()


def gather_call(plan, source, tokens, grads, prefix, meta):
    count, depth = source.shape[0] * (source.shape[1] if not plan.core_in_tp else 1), source.shape[-2]
    held, places, width = tokens.shape
    sems = gather_semaphores(plan, count)
    for name, amount in (("token", held), ("prefix", held * 2), ("grad", held)):
        sems.update(line_semaphores(name, amount))
    for name in ("own", "meta", "share"):
        sems[name] = pltpu.SemaphoreType.DMA((4,))
    outs = [
        jax.ShapeDtypeStruct((12, 2) + plan.shape + (depth, LINE * LANES), jnp.bfloat16),
        jax.ShapeDtypeStruct((LINE, plan.cores, places, width), jnp.bfloat16),
        jax.ShapeDtypeStruct((2, plan.cores, places, width), jnp.bfloat16),
        jax.ShapeDtypeStruct((2, prefix.shape[3], LINE * LANES), jnp.bfloat16),
        jax.ShapeDtypeStruct(meta.shape[1:], jnp.float32),
    ]
    return pl.pallas_call(
        functools.partial(gather_kernel, plan, tuple(sems)),
        out_shape=outs,
        in_specs=[pl.BlockSpec(memory_space=pl.ANY)] * 5,
        out_specs=[pl.BlockSpec(memory_space=pl.ANY)] * 5,
        scratch_shapes=list(sems.values()),
        compiler_params=pltpu.CompilerParams(collective_id=0, has_side_effects=True),
    )(source, tokens, grads, prefix, meta)


def give_back_kernel(plan, names, parts, pieces, *sems):
    sems = dict(zip(names, sems))
    place = plan.here()
    coords, line, core = place
    greet(plan, coords, line, core)
    places = pieces.shape[2]
    back = Line(plan, place, "back", sems)
    for half in range(2):
        for side in range(plan.cores):
            start = (half * plan.cores + side) * places
            if plan.core_in_tp:
                slot, target = line, side
            else:
                slot, target = lax.rem(line, 2), line // 2
            back.send(parts.at[:, pl.ds(start, places)], pieces.at[:, slot], 2 * core + half, target)
    back.settle()
    for j in range(pieces.shape[1]):
        chip = j if plan.core_in_tp else 2 * core + j
        back.receive(pieces.at[:, j], chip, line // 2)
    back.drain()


def give_back(plan, parts, held, places):
    sems = line_semaphores("back", 4)
    return pl.pallas_call(
        functools.partial(give_back_kernel, plan, tuple(sems)),
        out_shape=jax.ShapeDtypeStruct((parts.shape[0], held, places, parts.shape[2]), parts.dtype),
        in_specs=[pl.BlockSpec(memory_space=pl.ANY)],
        out_specs=pl.BlockSpec(memory_space=pl.ANY),
        scratch_shapes=list(sems.values()),
        compiler_params=pltpu.CompilerParams(collective_id=1, has_side_effects=True),
    )(parts)


def layer_norm_parts(z):
    mean = jnp.mean(z, axis=-1, keepdims=True)
    centred = z - mean
    rstd = lax.rsqrt(jnp.mean(centred * centred, axis=-1, keepdims=True) + 1e-05)
    return centred * rstd, rstd


def layer_norm_grad(normal, rstd, gain, grad):
    g = grad * gain
    return rstd * (
        g
        - jnp.mean(g, axis=-1, keepdims=True)
        - normal * jnp.mean(g * normal, axis=-1, keepdims=True)
    )


def gelu_exact(v):
    return jax.nn.gelu(v, approximate=False)


def own_blocks(plan, w_query, w_key, w_value, w_attn_out, w_up, w_down):
    depth = w_query.shape[0]

    def cut(a):
        return jnp.transpose(a.reshape(depth, -1, LANES), (1, 0, 2))

    sides = 2 // plan.cores
    first = [cut(a) for a in (w_query, w_key, w_value, w_attn_out.T)]
    up, down = cut(w_up), cut(w_down.T)
    blocks = [a.reshape(1, sides, depth, LANES) for a in first]
    for j in range(up.shape[0] // sides):
        for a in (up, down):
            blocks.append(a[j * sides : (j + 1) * sides][None])
    joined = jnp.concatenate(blocks, axis=0)
    return joined[:, 0] if plan.core_in_tp else joined


def shards(
    plan, tokens, w_query, w_key, w_value, w_attn_out, w_up, w_down, first_gain, first_shift,
    second_gain, second_shift, prefix_keys, prefix_values, example_lengths, task_ids, prefix_lens,
    slot_masks, out_grad,
):
    f32, bf16 = jnp.float32, jnp.bfloat16
    held, places, width = tokens.shape
    tasks, slots, part = prefix_keys.shape
    length = places * plan.tp
    _, line, core = plan.here()
    half = length // 2

    ends = jnp.cumsum(example_lengths, axis=1)
    spots = jnp.arange(length, dtype=jnp.int32)
    segment = jnp.sum((spots[None, :, None] >= ends[:, None, :]).astype(jnp.int32), axis=-1)
    live = (jnp.arange(slots, dtype=jnp.int32)[None, :] < prefix_lens[:, None]) & (slot_masks == 1)
    onehot = task_ids[:, None] == jnp.arange(tasks, dtype=jnp.int32)[None, :]
    live_rows = jnp.any(onehot[:, :, None] & live[None], axis=1)
    meta = jnp.zeros((held, 8, SLOTS + length), f32)
    meta = meta.at[:, 0, :slots].set(live_rows.astype(f32))
    meta = meta.at[:, 0, SLOTS:].set(segment.astype(f32))
    meta = meta.at[:, 1, :tasks].set(onehot.astype(f32))
    picker = onehot.astype(bf16)
    prefix = jnp.stack([prefix_keys, prefix_values])
    prefix = jnp.einsum("rt,atpe->rape", picker, prefix, preferred_element_type=f32).astype(bf16)
    prefix = jnp.pad(prefix, ((0, 0), (0, 0), (0, SLOTS - slots), (0, 0)))
    sides = 2 // plan.cores
    prefix = jnp.transpose(prefix.reshape(held, 2, SLOTS, sides, LANES), (0, 3, 1, 2, 4))

    source = own_blocks(plan, w_query, w_key, w_value, w_attn_out, w_up, w_down)
    whole, row, grad, pre, row_meta = gather_call(plan, source, tokens, out_grad, prefix, meta)
    whole = whole.reshape(12, 2, width, LINE * LANES)
    x = row.reshape(length, width)
    cotangent = grad.reshape(half, width)

    def mine(a):
        return lax.dynamic_index_in_dim(a, core, 0, keepdims=False)

    def pick(a, which):
        return lax.dynamic_slice_in_dim(a, which * half, half, 0)

    def swap(a):
        if plan.core_in_tp:
            return lax.ppermute(a, "tp", [(i, i ^ 1) for i in range(plan.tp)])
        return lax.ppermute(a, "rows", [(i, i ^ 1) for i in range(plan.rows)])

    def paired(own, other):
        return jnp.where(core == 0, own, other), jnp.where(core == 0, other, own)

    w_q, w_k, w_v = (mine(whole[i]) for i in range(3))
    q, k, v = (jnp.dot(x, w, preferred_element_type=f32).astype(bf16) for w in (w_q, w_k, w_v))
    seg = row_meta[0, SLOTS:]
    seg_col = jnp.broadcast_to(seg[:, None], (length, LANES))
    live_col = jnp.broadcast_to(row_meta[0, :SLOTS][:, None], (SLOTS, LANES))
    att, lse = attend_forward(q, k, v, pre[0], pre[1], row_meta, seg_col)
    att_low, att_high = paired(pick(att, core), swap(pick(att, 1 - core)))
    first_sum = pick(x, core).astype(f32) + mm_nt(att_low, whole[3, 0]) + mm_nt(att_high, whole[3, 1])
    n_one, r_one = layer_norm_parts(first_sum)
    normed = (n_one * first_gain + first_shift).astype(bf16)
    up, down = whole[4::2].reshape(8, width, -1), whole[5::2].reshape(8, width, -1)
    upper = jnp.einsum("pd,udf->upf", normed, up, preferred_element_type=f32)
    acted, gelu_pull = jax.vjp(gelu_exact, upper)
    second_sum = normed.astype(f32) + jnp.einsum(
        "upf,udf->pd", acted.astype(bf16), down, preferred_element_type=f32
    )
    n_two, r_two = layer_norm_parts(second_sum)
    output = (n_two * second_gain + second_shift).astype(bf16)

    d_second = layer_norm_grad(n_two, r_two, second_gain, cotangent.astype(f32))
    d_acted = jnp.einsum("pd,udf->upf", d_second.astype(bf16), down, preferred_element_type=f32)
    d_upper = gelu_pull(d_acted)[0].astype(bf16)
    d_normed = d_second + jnp.einsum("upf,udf->pd", d_upper, up, preferred_element_type=f32)
    d_first = layer_norm_grad(n_one, r_one, first_gain, d_normed)
    d_att = jnp.einsum("pd,cde->cpe", d_first.astype(bf16), whole[3], preferred_element_type=f32).astype(bf16)
    d_att = jnp.concatenate(paired(mine(d_att), swap(lax.dynamic_index_in_dim(d_att, 1 - core, 0, keepdims=False))), axis=0)
    bounds = block_bounds(seg.astype(jnp.int32))
    dq, dk, dv, dpk, dpv = attend_backward(
        bounds, q, k, v, d_att, att, pre[0], pre[1], lse, row_meta, seg_col, live_col
    )
    shares = mm_nt(dq, w_q) + mm_nt(dk, w_k) + mm_nt(dv, w_v)
    other = swap(pick(shares, 1 - core).astype(bf16)).astype(f32)
    d_tokens = d_first + pick(shares, core) + other
    back = give_back(plan, jnp.stack([output, d_tokens.astype(bf16)]), held, places)

    d_pre = jnp.stack([dpk, dpv])[:, :slots].reshape(2, slots, LINE, LANES)
    side = (jnp.arange(2) == core).astype(f32)
    d_pre = row_meta[1, :tasks][None, :, None, None, None, None] * (
        d_pre[:, None, :, :, None, :] * side[None, None, None, None, :, None]
    )
    d_pre = d_pre.reshape(2, tasks, slots, width).astype(bf16)
    d_pre = lax.psum_scatter(d_pre, "tp", scatter_dimension=3, tiled=True)
    d_pre = lax.psum(d_pre, "rows").astype(f32)
    return back[0], back[1].astype(f32), d_pre[0], d_pre[1]


def solution(mesh):
    placed = (
        P("rows", "tp", None),
        P("rows", "tp"),
        P("rows", "tp"),
        P("rows", "tp"),
        P("tp", "rows"),
        P("rows", "tp"),
        P("tp", "rows"),
        P(),
        P(),
        P(),
        P(),
        P(None, None, "tp"),
        P(None, None, "tp"),
        P("rows", None),
        P("rows"),
        P(),
        P(),
        P("rows", "tp", None),
    )
    plan = Plan(mesh.shape["rows"], mesh.shape["tp"])
    return jax.shard_map(
        functools.partial(shards, plan),
        mesh=mesh,
        in_specs=placed,
        out_specs=(
            P("rows", "tp", None),
            P("rows", "tp", None),
            P(None, None, "tp"),
            P(None, None, "tp"),
        ),
        check_vma=False,
    )
```

```python
import functools
import math
import jax
import jax.numpy as jnp
from jax import lax
from jax.experimental import pallas as pl
from jax.experimental.pallas import tpu as pltpu
from jax.sharding import PartitionSpec as P

HD = 64
PAIR = 2 * HD
SLOTS = 128
QB = 256
KB = 256
NEG = -1e30
NT = (((1,), (1,)), ((), ()))


def mm(a, b):
    return jnp.dot(a, b, preferred_element_type=jnp.float32)


def mm_nt(a, b):
    return lax.dot_general(a, b, NT, preferred_element_type=jnp.float32)


def head_lanes(half):
    lane = lax.broadcasted_iota(jnp.int32, (1, PAIR), 1)
    return (lane >= half * HD) & (lane < (half + 1) * HD)


def only_head(a, half):
    return jnp.where(head_lanes(half), a, jnp.zeros_like(a))


def attend_block(q, keys, values, seg_col, seg_row, live_row):
    mixed = jnp.zeros((q.shape[0], PAIR), jnp.float32)
    totals = jnp.zeros((q.shape[0], PAIR), jnp.float32)
    lane = lax.broadcasted_iota(jnp.int32, (1, PAIR), 1)
    for half in range(2):
        qh = only_head(q, half) * jnp.asarray(0.125, jnp.bfloat16)
        scores = mm_nt(qh, keys)
        seq = jnp.where(seg_col == seg_row, scores[:, SLOTS:], NEG)
        pre = jnp.where(live_row > 0.5, scores[:, :SLOTS], NEG)
        top = jnp.maximum(
            jnp.max(seq, axis=1, keepdims=True), jnp.max(pre, axis=1, keepdims=True)
        )
        seq = jnp.exp(seq - top)
        pre = jnp.exp(pre - top)
        total = jnp.sum(seq, axis=1, keepdims=True) + jnp.sum(pre, axis=1, keepdims=True)
        scale = 1.0 / total
        low = jnp.concatenate([(pre * scale).astype(jnp.bfloat16), (seq * scale).astype(jnp.bfloat16)], axis=1)
        out = mm(low, values)
        mixed = jnp.where(head_lanes(half), out, mixed)
        totals = jnp.where(lane == half, top + jnp.log(total), totals)
    return mixed.astype(jnp.bfloat16), totals


def backward_kernel(
    bounds_ref, q_ref, k_ref, v_ref, do_ref, att_ref, pk_ref, pv_ref, lse_ref, meta_ref, seg_ref, live_ref,
    dq_ref, dk_ref, dv_ref, dpk_ref, dpv_ref,
    dk_acc, dv_acc, dpk_acc, dpv_acc, k_t, pk_t,
):
    length = q_ref.shape[0]
    dk_acc[...] = jnp.zeros_like(dk_acc)
    dv_acc[...] = jnp.zeros_like(dv_acc)
    dpk_acc[...] = jnp.zeros_like(dpk_acc)
    dpv_acc[...] = jnp.zeros_like(dpv_acc)
    k_t[...] = jnp.transpose(k_ref[...])
    pk_t[...] = jnp.transpose(pk_ref[...])
    picks = lax.broadcasted_iota(jnp.int32, (8, PAIR), 0)
    lanes = lax.broadcasted_iota(jnp.int32, (8, PAIR), 1) // HD
    picker = jnp.where(picks == lanes, 1.0, 0.0)

    def block(b, carry):
        start = pl.multiple_of(b * QB, QB)
        rows = pl.ds(start, QB)
        q = q_ref[rows, :]
        do = do_ref[rows, :]
        prod = do.astype(jnp.float32) * att_ref[rows, :].astype(jnp.float32)
        inner = lax.dot_general(
            picker, prod, NT, preferred_element_type=jnp.float32, precision=lax.Precision.HIGHEST
        )
        seg_q = meta_ref[0:1, pl.ds(SLOTS + start, QB)]
        heads = []
        for half in range(2):
            qh = only_head(q, half) * jnp.asarray(0.125, jnp.bfloat16)
            dh = only_head(do, half)
            lse = lse_ref[0, half : half + 1, rows]
            delta = inner[half : half + 1, :]
            heads.append((qh, dh, lse, delta))

        def tile(kk, vv, kt, allowed, half):
            qh, dh, lse, delta = heads[half]
            s = mm_nt(kk, qh)
            p = jnp.exp(jnp.where(allowed, s, NEG) - lse)
            dp = mm_nt(vv, dh)
            ds = (p * (dp - delta)).astype(jnp.bfloat16)
            return mm(ds, qh), mm(p.astype(jnp.bfloat16), dh), mm(kt, ds)

        dqs = []
        for half in range(2):
            a, g, dq = tile(
                pk_ref[...], pv_ref[...], pk_t[half * HD : (half + 1) * HD, :], live_ref[:, 0:1] > 0.5, half
            )
            dpk_acc[...] += a
            dpv_acc[...] += g
            dqs.append(dq)

        def step(j, dqs):
            at = pl.multiple_of(j * KB, KB)
            krows = pl.ds(at, KB)
            allowed = seg_ref[krows, 0:1] == seg_q
            dk = dk_acc[krows, :]
            dv = dv_acc[krows, :]
            outs = []
            for half in range(2):
                a, g, dq = tile(
                    k_ref[krows, :], v_ref[krows, :], k_t[half * HD : (half + 1) * HD, krows], allowed, half
                )
                dk = dk + a
                dv = dv + g
                outs.append(dqs[half] + dq)
            dk_acc[krows, :] = dk
            dv_acc[krows, :] = dv
            return tuple(outs)

        dqs = lax.fori_loop(bounds_ref[0, b], bounds_ref[1, b], step, tuple(dqs))
        dq_ref[rows, :] = (jnp.transpose(jnp.concatenate(dqs, axis=0)) * 0.125).astype(jnp.bfloat16)
        return carry

    lax.fori_loop(0, length // QB, block, 0)
    dk_ref[...] = dk_acc[...].astype(jnp.bfloat16)
    dv_ref[...] = dv_acc[...].astype(jnp.bfloat16)
    dpk_ref[...] = dpk_acc[...]
    dpv_ref[...] = dpv_acc[...]


def attend_backward(bounds, q, k, v, do, att, pk, pv, lse, meta, seg_col, live_col):
    length, width = q.shape
    pairs = width // PAIR
    block = pl.BlockSpec((length, PAIR), lambda p, *_: (0, p))
    pre = pl.BlockSpec((SLOTS, PAIR), lambda p, *_: (0, p))
    whole = lambda a: pl.BlockSpec(a.shape, lambda p, *_: (0,) * a.ndim)
    low = jax.ShapeDtypeStruct((length, width), jnp.bfloat16)
    full = jax.ShapeDtypeStruct((SLOTS, width), jnp.float32)
    return pl.pallas_call(
        backward_kernel,
        grid_spec=pltpu.PrefetchScalarGridSpec(
            num_scalar_prefetch=1,
            grid=(pairs,),
            in_specs=[
                block, block, block, block, block, pre, pre,
                pl.BlockSpec((1, 8, length), lambda p, *_: (p, 0, 0)),
                whole(meta), whole(seg_col), whole(live_col),
            ],
            out_specs=[block, block, block, pre, pre],
            scratch_shapes=[
                pltpu.VMEM((length, PAIR), jnp.float32),
                pltpu.VMEM((length, PAIR), jnp.float32),
                pltpu.VMEM((SLOTS, PAIR), jnp.float32),
                pltpu.VMEM((SLOTS, PAIR), jnp.float32),
                pltpu.VMEM((PAIR, length), jnp.bfloat16),
                pltpu.VMEM((PAIR, SLOTS), jnp.bfloat16),
            ],
        ),
        out_shape=[low, low, low, full, full],
        compiler_params=pltpu.CompilerParams(vmem_limit_bytes=48 * 2**20),
    )(bounds, q, k, v, do, att, pk, pv, lse, meta, seg_col, live_col)


def block_bounds(seg):
    length = seg.shape[0]
    first = seg[::QB]
    last = seg[QB - 1 :: QB]
    low = jnp.sum((seg[None, :] < first[:, None]).astype(jnp.int32), axis=1)
    high = jnp.sum((seg[None, :] <= last[:, None]).astype(jnp.int32), axis=1)
    return jnp.stack([low // KB, (high + KB - 1) // KB])


MESH = pl.DeviceIdType.MESH
LINE = 4
LANES = 128
WIDE = LINE * LANES
KINDS = 12
FIRST_UP = 4
CHUNK = 256


class Plan:
    def __init__(self, rows, tp):
        self.rows = rows
        self.tp = tp
        self.core_in_tp = tp > LINE
        self.shape = (rows // 8, 2, 4) if self.core_in_tp else (rows // 4, 2, 2)
        self.axes = (0, 1, 2) if self.core_in_tp else (0, 1)
        self.cores = 2 if self.core_in_tp else 1
        self.sides = 2 // self.cores

    def here(self):
        r = lax.axis_index("rows")
        t = lax.axis_index("tp")
        a, b, c = self.shape
        coords = (r // (b * c), lax.rem(r // c, b), lax.rem(r, c))
        if self.core_in_tp:
            return coords, t // 2, lax.rem(t, 2)
        return coords, t, coords[2]

    def device(self, coords, line, core):
        a, b, c = self.shape
        if self.core_in_tp:
            return ((coords[0] * b + coords[1]) * c + coords[2], line * 2 + core)
        return ((coords[0] * b + coords[1]) * c + core, line)

    def row_core(self, chip):
        return None if self.core_in_tp else chip // 2


def shifted(coords, axis, by, size):
    moved = list(coords)
    moved[axis] = lax.rem(coords[axis] + by, size)
    return tuple(moved)


def sibling(plan, place):
    coords, line, core = place
    return plan.device(coords, line, 1 - core)


def greet(plan, place):
    coords, line, core = place
    others = [
        plan.device(coords, lax.rem(line + by, LINE), side) for by in range(1, LINE) for side in range(2)
    ]
    others.append(sibling(plan, place))
    for axis in plan.axes:
        for by in range(1, plan.shape[axis]):
            others.append(plan.device(shifted(coords, axis, by, plan.shape[axis]), line, core))
    barrier = pltpu.get_barrier_semaphore()
    for other in others:
        pl.semaphore_signal(barrier, inc=1, device_id=other, device_id_type=MESH)
    pl.semaphore_wait(barrier, len(others))


def remote(src, dst, send, recv, device):
    return pltpu.make_async_remote_copy(
        src_ref=src, dst_ref=dst, send_sem=send, recv_sem=recv, device_id=device, device_id_type=MESH
    )


class Gather:
    def __init__(self, plan, place, source, whole, sems):
        self.plan = plan
        self.place = place
        self.coords, self.line, self.core = place
        self.source = source
        self.whole = whole
        self.sems = sems
        self.count = KINDS * plan.sides
        self.depth = source.shape[-2]
        self.orders = (plan.axes, plan.axes[::-1])
        self.lanes = pl.ds(pl.multiple_of(self.line * LANES, LANES), LANES)

    def unit(self, i):
        if self.plan.core_in_tp:
            return (i, self.core)
        return (i // 2, lax.rem(i, 2))

    def own_copies(self):
        where = tuple(self.coords) + (slice(None), self.lanes)
        for at in range(self.plan.sides):
            side = self.core if self.plan.core_in_tp else at
            yield pltpu.make_async_copy(
                self.source.at[:, at], self.whole.at[(slice(None), side) + where], self.sems["own"].at[at]
            )

    def line_copies(self, i):
        src = self.source.at[(i, 0) if self.plan.core_in_tp else self.unit(i)]
        dst = self.whole.at[self.unit(i) + tuple(self.coords) + (slice(None), self.lanes)]
        for by in range(1, LINE):
            yield remote(
                src, dst, self.sems["line_send"].at[i, by - 1], self.sems["line_recv"].at[i, by - 1],
                self.plan.device(self.coords, lax.rem(self.line + by, LINE), self.core),
            )

    def axis_copies(self, i, step):
        rows = self.depth // 2
        for half in range(2):
            order = self.orders[half]
            axis = order[step]
            size = self.plan.shape[axis]
            index = [
                pl.ds(0, self.plan.shape[a]) if a in order[:step] else self.coords[a] for a in range(3)
            ]
            block = self.whole.at[self.unit(i) + tuple(index) + (pl.ds(half * rows, rows),)]
            for by in range(1, size):
                spot = (i, half, step, by - 1)
                yield remote(
                    block, block, self.sems["axis_send"].at[spot], self.sems["axis_recv"].at[spot],
                    self.plan.device(shifted(self.coords, axis, by, size), self.line, self.core),
                )

    def core_copy(self, i, side):
        if self.plan.core_in_tp:
            block = self.whole.at[i, side]
        else:
            block = self.whole.at[self.unit(i) + (slice(None), slice(None), side)]
        return remote(
            block, block, self.sems["core_send"].at[i], self.sems["core_recv"].at[i], sibling(self.plan, self.place)
        )

    def core_roles(self, i):
        if self.plan.core_in_tp:
            wide = i >= 3
            return wide, wide
        side = lax.rem(i, 2)
        wide = i >= 6
        return wide | (side != self.core), wide | (side == self.core)

    def start_line(self, i):
        for copy in self.line_copies(i):
            copy.start()

    def start_axis(self, i, step):
        for copy in self.line_copies(i) if step == 0 else self.axis_copies(i, step - 1):
            copy.wait_recv()
        for copy in self.axis_copies(i, step):
            copy.start()

    def start_core(self, i):
        for copy in self.axis_copies(i, len(self.plan.axes) - 1):
            copy.wait_recv()
        sends, _ = self.core_roles(i)
        pl.when(sends)(lambda: self.core_copy(i, self.core).start())

    def finish(self, i):
        _, gets = self.core_roles(i)
        pl.when(gets)(lambda: self.core_copy(i, 1 - self.core).wait_recv())

    def drain(self, i):
        for copy in self.line_copies(i):
            copy.wait_send()
        for step in range(len(self.plan.axes)):
            for copy in self.axis_copies(i, step):
                copy.wait_send()
        sends, _ = self.core_roles(i)
        pl.when(sends)(lambda: self.core_copy(i, self.core).wait_send())

    def tick(self, i, ahead, lag):
        steps = len(self.plan.axes)

        def guarded(at, body):
            pl.when((at >= 0) & (at < self.count))(functools.partial(body, at))

        guarded(i + ahead, self.start_line)
        for step in range(steps):
            guarded(i - lag * step, lambda at, step=step: self.start_axis(at, step))
        guarded(i - lag * steps, self.start_core)

    def ticks(self, lag):
        return self.count + lag * len(self.plan.axes)


def gather_semaphores(plan):
    count = KINDS * plan.sides
    steps = len(plan.axes)
    reach = max(plan.shape[a] for a in plan.axes) - 1
    shapes = {
        "line_send": (count, LINE - 1),
        "line_recv": (count, LINE - 1),
        "axis_send": (count, 2, steps, reach),
        "axis_recv": (count, 2, steps, reach),
        "core_send": (count,),
        "core_recv": (count,),
        "own": (2,),
    }
    return {name: pltpu.SemaphoreType.DMA(shape) for name, shape in shapes.items()}


class Line:
    def __init__(self, plan, place, name, sems):
        self.plan = plan
        self.coords, self.line, self.core = place
        self.send_sems = sems[name + "_send"]
        self.recv_sems = sems[name + "_recv"]
        self.pieces = []

    def here(self, chip, side):
        return (chip == self.line) & (side == self.core)

    def send(self, src, dst, chip, side):
        at = len(self.pieces)
        far = remote(
            src, dst, self.send_sems.at[at], self.recv_sems.at[self.line, self.core],
            self.plan.device(self.coords, chip, side),
        )
        near = pltpu.make_async_copy(src, dst, self.send_sems.at[at])
        stays = self.here(chip, side)
        self.pieces.append((stays, far, near))
        pl.when(jnp.logical_not(stays))(far.start)
        pl.when(stays)(near.start)

    def settle(self):
        for stays, _, near in self.pieces:
            pl.when(stays)(near.wait)

    def drain(self):
        for stays, far, _ in self.pieces:
            pl.when(jnp.logical_not(stays))(far.wait_send)

    def receive(self, dst, chip, side):
        copy = remote(
            dst, dst, self.send_sems.at[0], self.recv_sems.at[chip, side],
            self.plan.device(self.coords, chip, side),
        )
        pl.when(jnp.logical_not(self.here(chip, side)))(copy.wait_recv)


def line_semaphores(name, count):
    return {
        name + "_send": pltpu.SemaphoreType.DMA((count,)),
        name + "_recv": pltpu.SemaphoreType.DMA((LINE, 2)),
    }


class Sibling:
    def __init__(self, plan, place, name, sems):
        self.sems = sems
        self.name = name
        self.device = sibling(plan, place)

    def copy(self, src, dst, at):
        return remote(src, dst, self.sems[self.name + "_send"].at[at], self.sems[self.name + "_recv"].at[at], self.device)


def sibling_semaphores(name, count):
    return {
        name + "_send": pltpu.SemaphoreType.DMA((count,)),
        name + "_recv": pltpu.SemaphoreType.DMA((count,)),
    }


def give_back_kernel(plan, names, parts, pieces, *sems):
    sems = dict(zip(names, sems))
    place = plan.here()
    coords, line, core = place
    greet(plan, place)
    places = pieces.shape[2]
    back = Line(plan, place, "back", sems)
    for half in range(2):
        for side in range(plan.cores):
            start = (half * plan.cores + side) * places
            if plan.core_in_tp:
                slot, target = line, side
            else:
                slot, target = lax.rem(line, 2), line // 2
            back.send(parts.at[:, pl.ds(start, places)], pieces.at[:, slot], 2 * core + half, target)
    back.settle()
    for j in range(pieces.shape[1]):
        chip = j if plan.core_in_tp else 2 * core + j
        back.receive(pieces.at[:, j], chip, line // 2)
    back.drain()


def give_back(plan, parts, held, places):
    sems = line_semaphores("back", 4)
    return pl.pallas_call(
        functools.partial(give_back_kernel, plan, tuple(sems)),
        out_shape=jax.ShapeDtypeStruct((parts.shape[0], held, places, parts.shape[2]), parts.dtype),
        in_specs=[pl.BlockSpec(memory_space=pl.ANY)],
        out_specs=pl.BlockSpec(memory_space=pl.ANY),
        scratch_shapes=list(sems.values()),
        compiler_params=pltpu.CompilerParams(collective_id=1, has_side_effects=True),
    )(parts)

def normalise(z):
    mean = jnp.mean(z, axis=1, keepdims=True)
    centred = z - mean
    rstd = lax.rsqrt(jnp.mean(centred * centred, axis=1, keepdims=True) + 1e-05)
    return centred * rstd, rstd


def normalise_grad(normal, rstd, gain, grad):
    g = grad * gain
    return rstd * (
        g - jnp.mean(g, axis=1, keepdims=True) - normal * jnp.mean(g * normal, axis=1, keepdims=True)
    )


def forward_inputs(plan, place, refs, scratch):
    coords, line, core = place
    source, prefix, meta = scratch["source"], scratch["prefix"], scratch["meta"]
    sides = plan.sides

    def put(kind, block, first):
        for side in range(sides):
            at = (first + side) * LANES
            source[kind, side] = block[:, at : at + LANES]

    put(0, refs["w_query"], 0)
    put(1, refs["w_key"], 0)
    put(2, refs["w_value"], 0)
    put(3, jnp.transpose(refs["w_attn_out"][...]), 0)
    down = jnp.transpose(refs["w_down"][...])
    for j in range((KINDS - FIRST_UP) // 2):
        put(FIRST_UP + 2 * j, refs["w_up"], j * sides)
        put(FIRST_UP + 2 * j + 1, down, j * sides)

    slots = refs["prefix_keys"].shape[1]
    prefix[...] = jnp.zeros_like(prefix)
    for j in range(refs["tokens"].shape[0]):
        task = refs["task_ids"][j]
        for which, name in enumerate(("prefix_keys", "prefix_values")):
            rows = refs[name][task]
            for side in range(sides):
                prefix[j, side, which, 0:slots, :] = rows[:, side * LANES : (side + 1) * LANES]

    mine = line if plan.core_in_tp else lax.rem(line, 2)
    task = refs["task_ids"][mine]
    meta[...] = jnp.zeros_like(meta)
    length = meta.shape[1] - SLOTS
    spots = lax.broadcasted_iota(jnp.int32, (1, length), 1)
    lane = lax.broadcasted_iota(jnp.int32, (1, SLOTS), 1)
    segment = jnp.zeros((1, length), jnp.float32)
    ends = jnp.zeros((1, SLOTS), jnp.float32)
    end = jnp.int32(0)
    for j in range(refs["lengths"].shape[1]):
        end = end + refs["lengths"][mine, j]
        segment = segment + jnp.where(spots >= end, 1.0, 0.0)
        ends = jnp.where(lane == j, end.astype(jnp.float32), ends)
    masks = refs["slot_masks"]
    used = jnp.zeros((1, slots), jnp.int32)
    limit = jnp.int32(0)
    for t in range(masks.shape[0]):
        used = jnp.where(task == t, masks[t : t + 1, :], used)
        limit = jnp.where(task == t, refs["prefix_lens"][t], limit)
    live = jnp.where((used == 1) & (lane[:, :slots] < limit), 1.0, 0.0)
    meta[0:1, 0:slots] = live
    meta[0:1, SLOTS:] = segment
    meta[1:2, 0:SLOTS] = jnp.where(lane == task, 1.0, 0.0)
    meta[2:3, 0:SLOTS] = ends


F_IN = (
    "task_ids", "lengths", "prefix_lens", "slot_masks", "tokens", "out_grad", "w_query", "w_key", "w_value",
    "w_attn_out", "w_up", "w_down", "gain_one", "shift_one", "gain_two", "shift_two", "prefix_keys",
    "prefix_values",
)
F_OUT = (
    "q_out", "k_out", "v_out", "att_out", "lse_out", "pre_out", "meta_out", "d_att_out", "d_first_out",
    "w_out", "pieces",
)
F_SCRATCH = (
    "source", "prefix", "meta", "whole", "row", "grad", "pre", "q", "k", "v", "att", "lse", "att_other",
    "keys", "values", "meta_cols", "normal_one", "rstd_one", "normed", "slope", "acc", "low", "out", "d_att",
    "d_att_away",
)
AHEAD = 3
LAG = 2


def forward_backward_kernel(plan, sem_names, *args):
    names = F_IN + F_OUT + F_SCRATCH + sem_names
    refs = dict(zip(names, args))
    sems = refs
    place = plan.here()
    coords, line, core = place
    bf16, f32 = jnp.bfloat16, jnp.float32
    spread = plan.core_in_tp
    tokens, row, grad, pre = refs["tokens"], refs["row"], refs["grad"], refs["pre"]
    whole, meta = refs["whole"], refs["meta"]
    q, k, v, att, lse = (refs[n] for n in ("q", "k", "v", "att", "lse"))
    held = tokens.shape[0]
    width = row.shape[-1]
    length = q.shape[0]
    half = length // 2
    base = 0 if spread else 2 * core
    slot = core if spread else 0
    holds = None if spread else line // 2 == core

    forward_inputs(plan, place, refs, refs)
    greet(plan, place)

    gather = Gather(plan, place, refs["source"], whole, sems)
    gather.start_line(0)
    gather.start_line(1)
    token_line = Line(plan, place, "token", sems)
    for j in range(held):
        token_line.send(tokens.at[j], row.at[line, slot], base + j, core)
    for copy in gather.own_copies():
        copy.start()
    for i in range(2, AHEAD):
        gather.start_line(i)
    prefix_line = Line(plan, place, "prefix", sems)
    for j in range(held):
        for side in range(plan.sides):
            prefix_line.send(
                refs["prefix"].at[j, side], pre.at[:, :, gather.lanes], base + j, core if spread else side
            )
    share = Sibling(plan, place, "share", sems)
    meta_copy = share.copy(meta, meta, 4)
    if not spread:
        pl.when(holds)(meta_copy.start)
    for copy in gather.own_copies():
        copy.wait()

    last = gather.ticks(LAG)

    def beat(i, x=0):
        gather.tick(i, AHEAD, LAG)
        return x

    steps = LAG * len(plan.axes) + 1
    done = min(last, steps)
    lax.fori_loop(0, done, beat, 0)

    token_line.settle()

    def share_token(chip):
        if spread:
            token_line.receive(row.at[chip, core], chip, core)
            share.copy(row.at[chip, core], row.at[chip, core], chip).start()
        else:
            @pl.when(holds)
            def _():
                token_line.receive(row.at[chip, 0], chip, core)
                share.copy(row.at[chip, 0], row.at[chip, 0], chip).start()

    for chip in range(LINE):
        share_token(chip)
    grad_line = Line(plan, place, "grad", sems)
    for j in range(held):
        grad_line.send(refs["out_grad"].at[j], grad.at[lax.rem(line, 2), slot], base + j, line // 2)
    for chip in range(LINE):
        if spread:
            share.copy(row.at[chip, 1 - core], row.at[chip, 1 - core], chip).wait_recv()
        else:
            pl.when(jnp.logical_not(holds))(share.copy(row.at[chip, 0], row.at[chip, 0], chip).wait_recv)
    if not spread:
        pl.when(jnp.logical_not(holds))(meta_copy.wait_recv)
    prefix_line.settle()
    for chip in range(LINE):
        prefix_line.receive(pre.at[:, :, pl.ds(chip * LANES, LANES)], chip, core if spread else line // 2)
    refs["meta_cols"][...] = jnp.transpose(meta[...])

    def publish(name, out, at):
        return pltpu.make_async_copy(refs[name], refs[out], sems["publish"].at[at])

    def ready(first, amount, done):
        until = min(last, first + amount - 1 + steps)
        if until > done:
            lax.fori_loop(done, until, beat, 0)
        for i in range(first, first + amount):
            gather.finish(i)
        return max(done, until)

    for kind, target in enumerate((q, k, v)):
        done = ready(kind * plan.sides, plan.sides, done)
        weight = whole.at[kind, core]

        def project(b, x, weight=weight, target=target):
            block = row[b].reshape(CHUNK, width)
            target[pl.ds(pl.multiple_of(b * CHUNK, CHUNK), CHUNK), :] = mm(
                block, weight[...].reshape(width, WIDE)
            ).astype(bf16)
            return x

        lax.fori_loop(0, LINE, project, 0)
    keep = [publish(n, n + "_out", at) for at, n in enumerate(("q", "k", "v", "pre", "meta"))]
    keep.append(pltpu.make_async_copy(whole.at[pl.ds(0, 3), core], refs["w_out"], sems["publish"].at[5]))
    for copy in keep:
        copy.start()

    att_share = Sibling(plan, place, "att", sems)
    here = pl.ds(pl.multiple_of(core * half, half), half)
    there = pl.ds(pl.multiple_of((1 - core) * half, half), half)
    keys, values = refs["keys"], refs["values"]
    blocks = length // QB

    def att_copy(p):
        lanes = pl.ds(pl.multiple_of(p * PAIR, PAIR), PAIR)
        return att_share.copy(att.at[there, lanes], refs["att_other"].at[:, lanes], p)

    def pair(p, x):
        lanes = pl.ds(pl.multiple_of(p * PAIR, PAIR), PAIR)
        keys[0:SLOTS, :] = pre[0, :, lanes]
        keys[SLOTS:, :] = k[:, lanes]
        values[0:SLOTS, :] = pre[1, :, lanes]
        values[SLOTS:, :] = v[:, lanes]

        def block(b, x):
            rows = pl.ds(pl.multiple_of(b * QB, QB), QB)
            mixed, totals = attend_block(
                q[rows, lanes], keys[...], values[...],
                refs["meta_cols"][pl.ds(pl.multiple_of(SLOTS + b * QB, SLOTS), QB), 0:1],
                meta[0:1, SLOTS:], meta[0:1, :SLOTS],
            )
            att[rows, lanes] = mixed
            lse[p, :, rows] = jnp.transpose(totals)[0:8, :]
            return x

        lax.fori_loop(0, blocks // 2, block, 0)
        beat(done + plan.sides * p)
        lax.fori_loop(blocks // 2, blocks, block, 0)
        if plan.sides > 1:
            beat(done + plan.sides * p + 1)
        att_copy(p).start()
        return x

    pairs = WIDE // PAIR
    lax.fori_loop(0, pairs, pair, 0)
    done = min(last, done + plan.sides * pairs)
    keep += [publish(n, n + "_out", 6 + at) for at, n in enumerate(("att", "lse"))]
    for copy in keep[-2:]:
        copy.start()
    for p in range(pairs):
        att_copy(p).wait_recv()

    done = ready(3 * plan.sides, plan.sides, done)
    normal_one, rstd_one, normed, acc = (refs[n] for n in ("normal_one", "rstd_one", "normed", "acc"))
    low, slope, out = refs["low"], refs["slope"], refs["out"]
    parts = half // CHUNK

    def weight(kind, side):
        return whole[kind, side].reshape(width, WIDE)

    def mix(b, x):
        rows = pl.ds(pl.multiple_of(b * CHUNK, CHUNK), CHUNK)
        own = att[pl.ds(pl.multiple_of(core * half + b * CHUNK, CHUNK), CHUNK), :]
        total = row[2 * core + b].reshape(CHUNK, width).astype(f32)
        total = total + mm_nt(own, weight(3, core)) + mm_nt(refs["att_other"][rows, :], weight(3, 1 - core))
        normal, rstd = normalise(total)
        normal_one[rows, :] = normal
        rstd_one[rows, :] = jnp.broadcast_to(rstd, (CHUNK, LANES))
        low_normed = (normal * refs["gain_one"][...] + refs["shift_one"][...]).astype(bf16)
        normed[rows, :] = low_normed
        acc[rows, :] = low_normed.astype(f32)
        return x

    lax.fori_loop(0, parts, mix, 0)

    def feed(n, x):
        j, side = n // 2, lax.rem(n, 2)
        kind = FIRST_UP + 2 * j

        def part(b, x):
            rows = pl.ds(pl.multiple_of(b * CHUNK, CHUNK), CHUNK)
            upper = mm(normed[rows, :], weight(kind, side))
            bell = (1.0 + lax.erf(upper * (0.5**0.5))) * 0.5
            acted = (upper * bell).astype(bf16)
            slope[n, rows, :] = (
                bell + upper * jnp.exp(upper * upper * -0.5) * (1.0 / (2.0 * math.pi) ** 0.5)
            ).astype(bf16)
            acc[rows, :] += mm_nt(acted, weight(kind + 1, side))
            return x

        lax.fori_loop(0, parts, part, 0)
        return x

    groups = (KINDS - FIRST_UP) // 2
    for j in range(groups):
        done = ready((FIRST_UP + 2 * j) * plan.sides, 2 * plan.sides, done)
        lax.fori_loop(2 * j, 2 * j + 2, feed, 0)

    grad_line.settle()
    for part in range(2):
        for side in range(plan.cores):
            grad_line.receive(grad.at[part, side], 2 * core + part, side if spread else line // 2)

    back = Line(plan, place, "back", sems)
    places = tokens.shape[1]

    def close(b, x):
        rows = pl.ds(pl.multiple_of(b * CHUNK, CHUNK), CHUNK)
        normal, rstd = normalise(acc[rows, :])
        out[rows, :] = (normal * refs["gain_two"][...] + refs["shift_two"][...]).astype(bf16)
        d_second = normalise_grad(
            normal, rstd, refs["gain_two"][...], grad[b].reshape(CHUNK, width).astype(f32)
        )
        acc[rows, :] = d_second
        low[rows, :] = d_second.astype(bf16)
        return x

    lax.fori_loop(0, parts, close, 0)
    for b in range(2):
        for side in range(plan.cores):
            spot, target = (line, side) if spread else (lax.rem(line, 2), line // 2)
            back.send(
                out.at[pl.ds((b * plan.cores + side) * places, places)], refs["pieces"].at[spot],
                2 * core + b, target,
            )

    def feed_back(n, x):
        j, side = n // 2, lax.rem(n, 2)
        kind = FIRST_UP + 2 * j

        def part(b, x):
            rows = pl.ds(pl.multiple_of(b * CHUNK, CHUNK), CHUNK)
            d_acted = mm(low[rows, :], weight(kind + 1, side))
            d_upper = (d_acted * slope[n, rows, :].astype(f32)).astype(bf16)
            acc[rows, :] += mm_nt(d_upper, weight(kind, side))
            return x

        lax.fori_loop(0, parts, part, 0)
        return x

    lax.fori_loop(0, 2 * groups, feed_back, 0)

    d_att, away = refs["d_att"], refs["d_att_away"]
    d_share = Sibling(plan, place, "d_att", sems)

    def d_copy(b):
        mine = pl.ds(pl.multiple_of(core * half + b * CHUNK, CHUNK), CHUNK)
        return d_share.copy(away.at[pl.ds(pl.multiple_of(b * CHUNK, CHUNK), CHUNK)], d_att.at[mine], b)

    def open_(b, x):
        rows = pl.ds(pl.multiple_of(b * CHUNK, CHUNK), CHUNK)
        d_first = normalise_grad(normal_one[rows, :], rstd_one[rows, 0:1], refs["gain_one"][...], acc[rows, :])
        acc[rows, :] = d_first
        d_low = d_first.astype(bf16)
        away[rows, :] = mm(d_low, weight(3, 1 - core)).astype(bf16)
        d_copy(b).start()
        mine = pl.ds(pl.multiple_of(core * half + b * CHUNK, CHUNK), CHUNK)
        d_att[mine, :] = mm(d_low, weight(3, core)).astype(bf16)
        return x

    lax.fori_loop(0, parts, open_, 0)
    keep.append(publish("acc", "d_first_out", 8))
    keep[-1].start()
    for b in range(parts):
        d_copy(b).wait_recv()
    keep.append(publish("d_att", "d_att_out", 9))
    keep[-1].start()

    lax.fori_loop(0, gather.count, lambda i, x: (gather.drain(i), x)[1], 0)
    token_line.drain()
    prefix_line.drain()
    grad_line.drain()
    for chip in range(LINE):
        if spread:
            share.copy(row.at[chip, core], row.at[chip, core], chip).wait_send()
        else:
            pl.when(holds)(share.copy(row.at[chip, 0], row.at[chip, 0], chip).wait_send)
    if not spread:
        pl.when(holds)(meta_copy.wait_send)
    for p in range(pairs):
        att_copy(p).wait_send()
    for b in range(parts):
        d_copy(b).wait_send()
    back.settle()
    for j in range(held):
        back.receive(refs["pieces"].at[j], j if spread else 2 * core + j, line // 2)
    back.drain()
    for copy in keep:
        copy.wait()


def forward_backward(plan, task_ids, lengths, prefix_lens, slot_masks, *rest):
    tokens, _, w_query = rest[:3]
    held, places, width = tokens.shape
    depth = w_query.shape[0]
    length = places * plan.tp
    half = length // 2
    pairs = WIDE // PAIR
    bf16, f32 = jnp.bfloat16, jnp.float32
    S = jax.ShapeDtypeStruct
    outs = {
        "q_out": S((length, WIDE), bf16),
        "k_out": S((length, WIDE), bf16),
        "v_out": S((length, WIDE), bf16),
        "att_out": S((length, WIDE), bf16),
        "lse_out": S((pairs, 8, length), f32),
        "pre_out": S((2, SLOTS, WIDE), bf16),
        "meta_out": S((8, SLOTS + length), f32),
        "d_att_out": S((length, WIDE), bf16),
        "d_first_out": S((half, width), f32),
        "w_out": S((3,) + plan.shape + (depth, WIDE), bf16),
        "pieces": S((held, places, width), bf16),
    }
    units = 2 * (KINDS - FIRST_UP) // 2
    scratch = {
        "source": ((KINDS, plan.sides, depth, LANES), bf16),
        "prefix": ((held, plan.sides, 2, SLOTS, LANES), bf16),
        "meta": ((8, SLOTS + length), f32),
        "whole": ((KINDS, 2) + plan.shape + (depth, WIDE), bf16),
        "row": ((LINE, plan.cores, places, width), bf16),
        "grad": ((2, plan.cores, places, width), bf16),
        "pre": ((2, SLOTS, WIDE), bf16),
        "q": ((length, WIDE), bf16),
        "k": ((length, WIDE), bf16),
        "v": ((length, WIDE), bf16),
        "att": ((length, WIDE), bf16),
        "lse": ((pairs, 8, length), f32),
        "att_other": ((half, WIDE), bf16),
        "keys": ((SLOTS + length, PAIR), bf16),
        "values": ((SLOTS + length, PAIR), bf16),
        "meta_cols": ((SLOTS + length, 8), f32),
        "normal_one": ((half, width), f32),
        "rstd_one": ((half, LANES), f32),
        "normed": ((half, width), bf16),
        "slope": ((units, half, WIDE), bf16),
        "acc": ((half, width), f32),
        "low": ((half, width), bf16),
        "out": ((half, width), bf16),
        "d_att": ((length, WIDE), bf16),
        "d_att_away": ((half, WIDE), bf16),
    }
    sems = gather_semaphores(plan)
    for name, amount in (("token", held), ("prefix", held * plan.sides), ("grad", held), ("back", 4)):
        sems.update(line_semaphores(name, amount))
    for name, amount in (("share", 5), ("att", pairs), ("d_att", half // CHUNK)):
        sems.update(sibling_semaphores(name, amount))
    sems["publish"] = pltpu.SemaphoreType.DMA((10,))
    smem = pl.BlockSpec(memory_space=pltpu.SMEM)
    vmem = pl.BlockSpec(memory_space=pltpu.VMEM)
    hbm = pl.BlockSpec(memory_space=pl.ANY)
    results = pl.pallas_call(
        functools.partial(forward_backward_kernel, plan, tuple(sems)),
        out_shape=[outs[n] for n in F_OUT],
        in_specs=[smem, smem, smem, vmem, hbm, hbm] + [vmem] * 12,
        out_specs=[hbm] * len(F_OUT),
        scratch_shapes=[pltpu.VMEM(*scratch[n]) for n in F_SCRATCH] + list(sems.values()),
        compiler_params=pltpu.CompilerParams(
            collective_id=0, has_side_effects=True, vmem_limit_bytes=62 * 2**20
        ),
    )(task_ids, lengths, prefix_lens, slot_masks, *rest)
    return dict(zip(F_OUT, results))


def shards(
    plan, tokens, w_query, w_key, w_value, w_attn_out, w_up, w_down, first_gain, first_shift,
    second_gain, second_shift, prefix_keys, prefix_values, example_lengths, task_ids, prefix_lens,
    slot_masks, out_grad,
):
    f32, bf16 = jnp.float32, jnp.bfloat16
    held, places, width = tokens.shape
    tasks, slots, part = prefix_keys.shape
    length = places * plan.tp
    _, line, core = plan.here()
    half = length // 2
    done = forward_backward(
        plan, task_ids, example_lengths, prefix_lens, slot_masks, tokens, out_grad, w_query, w_key, w_value,
        w_attn_out, w_up, w_down, first_gain[None], first_shift[None], second_gain[None], second_shift[None],
        prefix_keys, prefix_values,
    )
    q, k, v, att, lse, pre, row_meta, d_att, d_first = (
        done[n + "_out"] for n in ("q", "k", "v", "att", "lse", "pre", "meta", "d_att", "d_first")
    )
    w_q, w_k, w_v = (done["w_out"][i].reshape(width, WIDE) for i in range(3))

    def pick(a, which):
        return lax.dynamic_slice_in_dim(a, which * half, half, 0)

    def swap(a):
        if plan.core_in_tp:
            return lax.ppermute(a, "tp", [(i, i ^ 1) for i in range(plan.tp)])
        return lax.ppermute(a, "rows", [(i, i ^ 1) for i in range(plan.rows)])

    seg = row_meta[0, SLOTS:]
    seg_col = jnp.broadcast_to(seg[:, None], (length, LANES))
    live_col = jnp.broadcast_to(row_meta[0, :SLOTS][:, None], (SLOTS, LANES))
    bounds = block_bounds(seg.astype(jnp.int32))
    dq, dk, dv, dpk, dpv = attend_backward(
        bounds, q, k, v, d_att, att, pre[0], pre[1], lse, row_meta, seg_col, live_col
    )
    shares = mm_nt(dq, w_q) + mm_nt(dk, w_k) + mm_nt(dv, w_v)
    other = swap(pick(shares, 1 - core).astype(bf16)).astype(f32)
    d_tokens = d_first + pick(shares, core) + other
    back = give_back(plan, d_tokens.astype(bf16)[None], held, places)

    d_pre = jnp.stack([dpk, dpv])[:, :slots].reshape(2, slots, LINE, LANES)
    side = (jnp.arange(2) == core).astype(f32)
    d_pre = row_meta[1, :tasks][None, :, None, None, None, None] * (
        d_pre[:, None, :, :, None, :] * side[None, None, None, None, :, None]
    )
    d_pre = d_pre.reshape(2, tasks, slots, width).astype(bf16)
    d_pre = lax.psum_scatter(d_pre, "tp", scatter_dimension=3, tiled=True)
    d_pre = lax.psum(d_pre, "rows").astype(f32)
    return done["pieces"], back[0].astype(f32), d_pre[0], d_pre[1]


def solution(mesh):
    placed = (
        P("rows", "tp", None),
        P("rows", "tp"),
        P("rows", "tp"),
        P("rows", "tp"),
        P("tp", "rows"),
        P("rows", "tp"),
        P("tp", "rows"),
        P(),
        P(),
        P(),
        P(),
        P(None, None, "tp"),
        P(None, None, "tp"),
        P("rows", None),
        P("rows"),
        P(),
        P(),
        P("rows", "tp", None),
    )
    plan = Plan(mesh.shape["rows"], mesh.shape["tp"])
    return jax.shard_map(
        functools.partial(shards, plan),
        mesh=mesh,
        in_specs=placed,
        out_specs=(
            P("rows", "tp", None),
            P("rows", "tp", None),
            P(None, None, "tp"),
            P(None, None, "tp"),
        ),
        check_vma=False,
    )
```

```python
import functools
import math
from types import SimpleNamespace

import jax
import jax.numpy as jnp
from jax import lax
from jax.experimental import pallas as pl
from jax.experimental.pallas import tpu as pltpu
from jax.sharding import PartitionSpec as P

HD = 64
PAIR = 2 * HD
SLOTS = 128
QB = 256
KB = 256
NEG = -1e30
NT = (((1,), (1,)), ((), ()))


def mm(a, b):
    return jnp.dot(a, b, preferred_element_type=jnp.float32)


def mm_nt(a, b):
    return lax.dot_general(a, b, NT, preferred_element_type=jnp.float32)


def head_lanes(half):
    lane = lax.broadcasted_iota(jnp.int32, (1, PAIR), 1)
    return (lane >= half * HD) & (lane < (half + 1) * HD)


def only_head(a, half):
    return jnp.where(head_lanes(half), a, jnp.zeros_like(a))


def attend_block(q, keys, values, seg_col, seg_row, live_row):
    mixed = jnp.zeros((q.shape[0], PAIR), jnp.float32)
    totals = jnp.zeros((q.shape[0], PAIR), jnp.float32)
    lane = lax.broadcasted_iota(jnp.int32, (1, PAIR), 1)
    for half in range(2):
        qh = only_head(q, half) * jnp.asarray(0.125, jnp.bfloat16)
        scores = mm_nt(qh, keys)
        seq = jnp.where(seg_col == seg_row, scores[:, SLOTS:], NEG)
        pre = jnp.where(live_row > 0.5, scores[:, :SLOTS], NEG)
        top = jnp.maximum(
            jnp.max(seq, axis=1, keepdims=True), jnp.max(pre, axis=1, keepdims=True)
        )
        seq = jnp.exp(seq - top)
        pre = jnp.exp(pre - top)
        total = jnp.sum(seq, axis=1, keepdims=True) + jnp.sum(pre, axis=1, keepdims=True)
        scale = 1.0 / total
        low = jnp.concatenate([(pre * scale).astype(jnp.bfloat16), (seq * scale).astype(jnp.bfloat16)], axis=1)
        out = mm(low, values)
        mixed = jnp.where(head_lanes(half), out, mixed)
        totals = jnp.where(lane == half, top + jnp.log(total), totals)
    return mixed.astype(jnp.bfloat16), totals


def backward_kernel(
    examples, ends_ref, q_ref, k_ref, v_ref, do_ref, att_ref, pre_ref, lse_ref, meta_ref,
    dq_ref, dk_ref, dv_ref, dpre_ref,
    dk_acc, dv_acc, dpk_acc, dpv_acc, k_t, pk_t, columns,
):
    length = q_ref.shape[0]
    pk_ref, pv_ref = pre_ref.at[0], pre_ref.at[1]
    live_ref, seg_ref = columns.at[0:SLOTS], columns.at[SLOTS:]

    @pl.when(pl.program_id(0) == 0)
    def _():
        columns[...] = jnp.transpose(meta_ref[...])

    dk_acc[...] = jnp.zeros_like(dk_acc)
    dv_acc[...] = jnp.zeros_like(dv_acc)
    dpk_acc[...] = jnp.zeros_like(dpk_acc)
    dpv_acc[...] = jnp.zeros_like(dpv_acc)
    k_t[...] = jnp.transpose(k_ref[...])
    pk_t[...] = jnp.transpose(pk_ref[...])
    picks = lax.broadcasted_iota(jnp.int32, (8, PAIR), 0)
    lanes = lax.broadcasted_iota(jnp.int32, (8, PAIR), 1) // HD
    picker = jnp.where(picks == lanes, 1.0, 0.0)

    def bounds(start):
        low, high = jnp.int32(0), jnp.int32(length)
        for j in range(examples):
            end = ends_ref[2, j].astype(jnp.int32)
            low = jnp.where(end <= start, jnp.maximum(low, end), low)
            high = jnp.where(end >= start + QB, jnp.minimum(high, end), high)
        return low // KB, (high + KB - 1) // KB

    def block(b, carry):
        start = pl.multiple_of(b * QB, QB)
        rows = pl.ds(start, QB)
        q = q_ref[rows, :]
        do = do_ref[rows, :]
        prod = do.astype(jnp.float32) * att_ref[rows, :].astype(jnp.float32)
        inner = lax.dot_general(
            picker, prod, NT, preferred_element_type=jnp.float32, precision=lax.Precision.HIGHEST
        )
        seg_q = meta_ref[0:1, pl.ds(SLOTS + start, QB)]
        heads = []
        for half in range(2):
            qh = only_head(q, half) * jnp.asarray(0.125, jnp.bfloat16)
            dh = only_head(do, half)
            lse = lse_ref[0, half : half + 1, rows]
            delta = inner[half : half + 1, :]
            heads.append((qh, dh, lse, delta))

        def tile(kk, vv, kt, allowed, half):
            qh, dh, lse, delta = heads[half]
            s = mm_nt(kk, qh)
            p = jnp.exp(jnp.where(allowed, s, NEG) - lse)
            dp = mm_nt(vv, dh)
            ds = (p * (dp - delta)).astype(jnp.bfloat16)
            return mm(ds, qh), mm(p.astype(jnp.bfloat16), dh), mm(kt, ds)

        dqs = []
        for half in range(2):
            a, g, dq = tile(
                pk_ref[...], pv_ref[...], pk_t[half * HD : (half + 1) * HD, :], live_ref[:, 0:1] > 0.5, half
            )
            dpk_acc[...] += a
            dpv_acc[...] += g
            dqs.append(dq)

        def step(j, dqs):
            at = pl.multiple_of(j * KB, KB)
            krows = pl.ds(at, KB)
            allowed = seg_ref[krows, 0:1] == seg_q
            dk = dk_acc[krows, :]
            dv = dv_acc[krows, :]
            outs = []
            for half in range(2):
                a, g, dq = tile(
                    k_ref[krows, :], v_ref[krows, :], k_t[half * HD : (half + 1) * HD, krows], allowed, half
                )
                dk = dk + a
                dv = dv + g
                outs.append(dqs[half] + dq)
            dk_acc[krows, :] = dk
            dv_acc[krows, :] = dv
            return tuple(outs)

        dqs = lax.fori_loop(*bounds(start), step, tuple(dqs))
        dq_ref[rows, :] = (jnp.transpose(jnp.concatenate(dqs, axis=0)) * 0.125).astype(jnp.bfloat16)
        return carry

    lax.fori_loop(0, length // QB, block, 0)
    dk_ref[...] = dk_acc[...].astype(jnp.bfloat16)
    dv_ref[...] = dv_acc[...].astype(jnp.bfloat16)
    dpre_ref[0] = dpk_acc[...]
    dpre_ref[1] = dpv_acc[...]


def attend_backward(examples, q, k, v, do, att, pre, lse, meta):
    length, width = q.shape
    pairs = width // PAIR
    block = pl.BlockSpec((length, PAIR), lambda p: (0, p))
    pre_block = pl.BlockSpec((2, SLOTS, PAIR), lambda p: (0, 0, p))
    low = jax.ShapeDtypeStruct((length, width), jnp.bfloat16)
    return pl.pallas_call(
        functools.partial(backward_kernel, examples),
        grid=(pairs,),
        in_specs=[
            pl.BlockSpec((8, SLOTS), lambda p: (0, 0), memory_space=pltpu.SMEM),
            block, block, block, block, block, pre_block,
            pl.BlockSpec((1, 8, length), lambda p: (p, 0, 0)),
            pl.BlockSpec(meta.shape, lambda p: (0, 0)),
        ],
        out_specs=[block, block, block, pre_block],
        out_shape=[low, low, low, jax.ShapeDtypeStruct((2, SLOTS, width), jnp.float32)],
        scratch_shapes=[
            pltpu.VMEM((length, PAIR), jnp.float32),
            pltpu.VMEM((length, PAIR), jnp.float32),
            pltpu.VMEM((SLOTS, PAIR), jnp.float32),
            pltpu.VMEM((SLOTS, PAIR), jnp.float32),
            pltpu.VMEM((PAIR, length), jnp.bfloat16),
            pltpu.VMEM((PAIR, SLOTS), jnp.bfloat16),
            pltpu.VMEM((meta.shape[1], 8), jnp.float32),
        ],
        compiler_params=pltpu.CompilerParams(vmem_limit_bytes=48 * 2**20),
    )(meta, q, k, v, do, att, pre, lse, meta)


MESH = pl.DeviceIdType.MESH
LINE = 4
LANES = 128
WIDE = LINE * LANES
KINDS = 12
FIRST_UP = 4
CHUNK = 256


class Plan:
    def __init__(self, rows, tp):
        self.rows = rows
        self.tp = tp
        self.core_in_tp = tp > LINE
        self.shape = (rows // 8, 2, 4) if self.core_in_tp else (rows // 4, 2, 2)
        self.axes = (0, 1, 2) if self.core_in_tp else (0, 1)
        self.cores = 2 if self.core_in_tp else 1
        self.sides = 2 // self.cores

    def here(self):
        r = lax.axis_index("rows")
        t = lax.axis_index("tp")
        a, b, c = self.shape
        coords = (r // (b * c), lax.rem(r // c, b), lax.rem(r, c))
        if self.core_in_tp:
            return coords, t // 2, lax.rem(t, 2)
        return coords, t, coords[2]

    def device(self, coords, line, core):
        a, b, c = self.shape
        if self.core_in_tp:
            return ((coords[0] * b + coords[1]) * c + coords[2], line * 2 + core)
        return ((coords[0] * b + coords[1]) * c + core, line)

    def row_core(self, chip):
        return None if self.core_in_tp else chip // 2


def shifted(coords, axis, by, size):
    moved = list(coords)
    moved[axis] = lax.rem(coords[axis] + by, size)
    return tuple(moved)


def sibling(plan, place):
    coords, line, core = place
    return plan.device(coords, line, 1 - core)


def greet(plan, place):
    coords, line, core = place
    others = [
        plan.device(coords, lax.rem(line + by, LINE), side) for by in range(1, LINE) for side in range(2)
    ]
    others.append(sibling(plan, place))
    for axis in plan.axes:
        for by in range(1, plan.shape[axis]):
            others.append(plan.device(shifted(coords, axis, by, plan.shape[axis]), line, core))
    barrier = pltpu.get_barrier_semaphore()
    for other in others:
        pl.semaphore_signal(barrier, inc=1, device_id=other, device_id_type=MESH)
    pl.semaphore_wait(barrier, len(others))


def remote(src, dst, send, recv, device):
    return pltpu.make_async_remote_copy(
        src_ref=src, dst_ref=dst, send_sem=send, recv_sem=recv, device_id=device, device_id_type=MESH
    )


class Gather:
    def __init__(self, plan, place, source, whole, sems):
        self.plan = plan
        self.place = place
        self.coords, self.line, self.core = place
        self.source = source
        self.whole = whole
        self.sems = sems
        self.count = KINDS * plan.sides
        self.depth = source.shape[-2]
        self.orders = (plan.axes, plan.axes[::-1])
        self.lanes = pl.ds(pl.multiple_of(self.line * LANES, LANES), LANES)

    def unit(self, i):
        if self.plan.core_in_tp:
            return (i, self.core)
        return (i // 2, lax.rem(i, 2))

    def own_copies(self):
        where = tuple(self.coords) + (slice(None), self.lanes)
        for at in range(self.plan.sides):
            side = self.core if self.plan.core_in_tp else at
            yield pltpu.make_async_copy(
                self.source.at[:, at], self.whole.at[(slice(None), side) + where], self.sems.own.at[at]
            )

    def line_copies(self, i):
        src = self.source.at[(i, 0) if self.plan.core_in_tp else self.unit(i)]
        dst = self.whole.at[self.unit(i) + tuple(self.coords) + (slice(None), self.lanes)]
        for by in range(1, LINE):
            yield remote(
                src, dst, self.sems.line_send.at[i, by - 1], self.sems.line_recv.at[i, by - 1],
                self.plan.device(self.coords, lax.rem(self.line + by, LINE), self.core),
            )

    def axis_copies(self, i, step):
        rows = self.depth // 2
        for half in range(2):
            order = self.orders[half]
            axis = order[step]
            size = self.plan.shape[axis]
            index = [
                pl.ds(0, self.plan.shape[a]) if a in order[:step] else self.coords[a] for a in range(3)
            ]
            block = self.whole.at[self.unit(i) + tuple(index) + (pl.ds(half * rows, rows),)]
            for by in range(1, size):
                spot = (i, half, step, by - 1)
                yield remote(
                    block, block, self.sems.axis_send.at[spot], self.sems.axis_recv.at[spot],
                    self.plan.device(shifted(self.coords, axis, by, size), self.line, self.core),
                )

    def core_copy(self, i, side):
        if self.plan.core_in_tp:
            block = self.whole.at[i, side]
        else:
            block = self.whole.at[self.unit(i) + (slice(None), slice(None), side)]
        return remote(
            block, block, self.sems.core_send.at[i], self.sems.core_recv.at[i], sibling(self.plan, self.place)
        )

    def core_roles(self, i):
        if self.plan.core_in_tp:
            wide = i >= 3
            return wide, wide
        side = lax.rem(i, 2)
        wide = i >= 6
        return wide | (side != self.core), wide | (side == self.core)

    def start_line(self, i):
        for copy in self.line_copies(i):
            copy.start()

    def start_axis(self, i, step):
        for copy in self.line_copies(i) if step == 0 else self.axis_copies(i, step - 1):
            copy.wait_recv()
        for copy in self.axis_copies(i, step):
            copy.start()

    def start_core(self, i):
        for copy in self.axis_copies(i, len(self.plan.axes) - 1):
            copy.wait_recv()
        sends, _ = self.core_roles(i)
        pl.when(sends)(lambda: self.core_copy(i, self.core).start())

    def finish(self, i):
        _, gets = self.core_roles(i)
        pl.when(gets)(lambda: self.core_copy(i, 1 - self.core).wait_recv())

    def drain(self, i):
        for copy in self.line_copies(i):
            copy.wait_send()
        for step in range(len(self.plan.axes)):
            for copy in self.axis_copies(i, step):
                copy.wait_send()
        sends, _ = self.core_roles(i)
        pl.when(sends)(lambda: self.core_copy(i, self.core).wait_send())

    def tick(self, i, ahead, lag):
        steps = len(self.plan.axes)

        def guarded(at, body):
            pl.when((at >= 0) & (at < self.count))(functools.partial(body, at))

        guarded(i + ahead, self.start_line)
        for step in range(steps):
            guarded(i - lag * step, lambda at, step=step: self.start_axis(at, step))
        guarded(i - lag * steps, self.start_core)

    def ticks(self, lag):
        return self.count + lag * len(self.plan.axes)


def semaphores(*shape):
    return pltpu.SemaphoreType.DMA(shape)


def gather_semaphores(plan):
    count = KINDS * plan.sides
    steps = len(plan.axes)
    reach = max(plan.shape[a] for a in plan.axes) - 1
    return dict(
        line_send=semaphores(count, LINE - 1),
        line_recv=semaphores(count, LINE - 1),
        axis_send=semaphores(count, 2, steps, reach),
        axis_recv=semaphores(count, 2, steps, reach),
        core_send=semaphores(count),
        core_recv=semaphores(count),
        own=semaphores(2),
    )


class Line:
    def __init__(self, plan, place, send_sems, recv_sems):
        self.plan = plan
        self.coords, self.line, self.core = place
        self.send_sems = send_sems
        self.recv_sems = recv_sems
        self.pieces = []

    def here(self, chip, side):
        return (chip == self.line) & (side == self.core)

    def send(self, src, dst, chip, side):
        at = len(self.pieces)
        far = remote(
            src, dst, self.send_sems.at[at], self.recv_sems.at[self.line, self.core],
            self.plan.device(self.coords, chip, side),
        )
        near = pltpu.make_async_copy(src, dst, self.send_sems.at[at])
        stays = self.here(chip, side)
        self.pieces.append((stays, far, near))
        pl.when(jnp.logical_not(stays))(far.start)
        pl.when(stays)(near.start)

    def settle(self):
        for stays, _, near in self.pieces:
            pl.when(stays)(near.wait)

    def drain(self):
        for stays, far, _ in self.pieces:
            pl.when(jnp.logical_not(stays))(far.wait_send)

    def receive(self, dst, chip, side):
        copy = remote(
            dst, dst, self.send_sems.at[0], self.recv_sems.at[chip, side],
            self.plan.device(self.coords, chip, side),
        )
        pl.when(jnp.logical_not(self.here(chip, side)))(copy.wait_recv)


class Sibling:
    def __init__(self, plan, place, send_sems, recv_sems):
        self.send_sems = send_sems
        self.recv_sems = recv_sems
        self.device = sibling(plan, place)

    def copy(self, src, dst, at):
        return remote(src, dst, self.send_sems.at[at], self.recv_sems.at[at], self.device)


def normalise(z):
    mean = jnp.mean(z, axis=1, keepdims=True)
    centred = z - mean
    rstd = lax.rsqrt(jnp.mean(centred * centred, axis=1, keepdims=True) + 1e-05)
    return centred * rstd, rstd


def normalise_grad(normal, rstd, gain, grad):
    g = grad * gain
    return rstd * (
        g - jnp.mean(g, axis=1, keepdims=True) - normal * jnp.mean(g * normal, axis=1, keepdims=True)
    )


def forward_inputs(plan, place, refs, scratch):
    coords, line, core = place
    source, prefix, meta = scratch.source, scratch.prefix, scratch.meta
    sides = plan.sides

    def put(kind, block, first):
        for side in range(sides):
            at = (first + side) * LANES
            source[kind, side] = block[:, at : at + LANES]

    put(0, refs.w_query, 0)
    put(1, refs.w_key, 0)
    put(2, refs.w_value, 0)
    put(3, jnp.transpose(refs.w_attn_out[...]), 0)
    down = jnp.transpose(refs.w_down[...])
    for j in range((KINDS - FIRST_UP) // 2):
        put(FIRST_UP + 2 * j, refs.w_up, j * sides)
        put(FIRST_UP + 2 * j + 1, down, j * sides)

    slots = refs.prefix_keys.shape[1]
    prefix[...] = jnp.zeros_like(prefix)
    for j in range(refs.tokens.shape[0]):
        task = refs.task_ids[j]
        for which, table in enumerate((refs.prefix_keys, refs.prefix_values)):
            rows = table[task]
            for side in range(sides):
                prefix[j, side, which, 0:slots, :] = rows[:, side * LANES : (side + 1) * LANES]

    mine = line if plan.core_in_tp else lax.rem(line, 2)
    task = refs.task_ids[mine]
    meta[...] = jnp.zeros_like(meta)
    length = meta.shape[1] - SLOTS
    spots = lax.broadcasted_iota(jnp.int32, (1, length), 1)
    lane = lax.broadcasted_iota(jnp.int32, (1, SLOTS), 1)
    segment = jnp.zeros((1, length), jnp.float32)
    ends = jnp.zeros((1, SLOTS), jnp.float32)
    end = jnp.int32(0)
    for j in range(refs.lengths.shape[1]):
        end = end + refs.lengths[mine, j]
        segment = segment + jnp.where(spots >= end, 1.0, 0.0)
        ends = jnp.where(lane == j, end.astype(jnp.float32), ends)
    masks = refs.slot_masks
    used = jnp.zeros((1, slots), jnp.int32)
    limit = jnp.int32(0)
    for t in range(masks.shape[0]):
        used = jnp.where(task == t, masks[t : t + 1, :], used)
        limit = jnp.where(task == t, refs.prefix_lens[t], limit)
    live = jnp.where((used == 1) & (lane[:, :slots] < limit), 1.0, 0.0)
    meta[0:1, 0:slots] = live
    meta[0:1, SLOTS:] = segment
    meta[1:2, 0:SLOTS] = jnp.where(lane == task, 1.0, 0.0)
    meta[2:3, 0:SLOTS] = ends


AHEAD = 3
LAG = 2


def forward_backward_kernel(plan, names, *args):
    refs = SimpleNamespace(**dict(zip(names, args)))
    sems = refs
    place = plan.here()
    coords, line, core = place
    bf16, f32 = jnp.bfloat16, jnp.float32
    spread = plan.core_in_tp
    tokens, row, grad, pre = refs.tokens, refs.row, refs.grad, refs.pre
    whole, meta = refs.whole, refs.meta
    q, k, v, att, lse = refs.q, refs.k, refs.v, refs.att, refs.lse
    held = tokens.shape[0]
    width = row.shape[-1]
    length = q.shape[0]
    half = length // 2
    base = 0 if spread else 2 * core
    slot = core if spread else 0
    holds = None if spread else line // 2 == core

    forward_inputs(plan, place, refs, refs)
    greet(plan, place)

    gather = Gather(plan, place, refs.source, whole, sems)
    gather.start_line(0)
    gather.start_line(1)
    token_line = Line(plan, place, sems.token_send, sems.token_recv)
    for j in range(held):
        token_line.send(tokens.at[j], row.at[line, slot], base + j, core)
    for copy in gather.own_copies():
        copy.start()
    for i in range(2, AHEAD):
        gather.start_line(i)
    prefix_line = Line(plan, place, sems.prefix_send, sems.prefix_recv)
    for j in range(held):
        for side in range(plan.sides):
            prefix_line.send(
                refs.prefix.at[j, side], pre.at[:, :, gather.lanes], base + j, core if spread else side
            )
    share = Sibling(plan, place, sems.share_send, sems.share_recv)
    meta_copy = share.copy(meta, meta, 4)
    if not spread:
        pl.when(holds)(meta_copy.start)
    for copy in gather.own_copies():
        copy.wait()

    last = gather.ticks(LAG)

    def beat(i, x=0):
        gather.tick(i, AHEAD, LAG)
        return x

    steps = LAG * len(plan.axes) + 1
    done = min(last, steps)
    lax.fori_loop(0, done, beat, 0)

    token_line.settle()

    def share_token(chip):
        if spread:
            token_line.receive(row.at[chip, core], chip, core)
            share.copy(row.at[chip, core], row.at[chip, core], chip).start()
        else:
            @pl.when(holds)
            def _():
                token_line.receive(row.at[chip, 0], chip, core)
                share.copy(row.at[chip, 0], row.at[chip, 0], chip).start()

    for chip in range(LINE):
        share_token(chip)
    grad_line = Line(plan, place, sems.grad_send, sems.grad_recv)
    for j in range(held):
        grad_line.send(refs.out_grad.at[j], grad.at[lax.rem(line, 2), slot], base + j, line // 2)
    for chip in range(LINE):
        if spread:
            share.copy(row.at[chip, 1 - core], row.at[chip, 1 - core], chip).wait_recv()
        else:
            pl.when(jnp.logical_not(holds))(share.copy(row.at[chip, 0], row.at[chip, 0], chip).wait_recv)
    if not spread:
        pl.when(jnp.logical_not(holds))(meta_copy.wait_recv)
    prefix_line.settle()
    for chip in range(LINE):
        prefix_line.receive(pre.at[:, :, pl.ds(chip * LANES, LANES)], chip, core if spread else line // 2)
    refs.meta_cols[...] = jnp.transpose(meta[...])

    def publish(ref, out, at):
        return pltpu.make_async_copy(ref, out, sems.publish.at[at])

    def ready(first, amount, done):
        until = min(last, first + amount - 1 + steps)
        if until > done:
            lax.fori_loop(done, until, beat, 0)
        for i in range(first, first + amount):
            gather.finish(i)
        return max(done, until)

    for kind, target in enumerate((q, k, v)):
        done = ready(kind * plan.sides, plan.sides, done)
        weight = whole.at[kind, core]

        def project(b, x, weight=weight, target=target):
            block = row[b].reshape(CHUNK, width)
            target[pl.ds(pl.multiple_of(b * CHUNK, CHUNK), CHUNK), :] = mm(
                block, weight[...].reshape(width, WIDE)
            ).astype(bf16)
            return x

        lax.fori_loop(0, LINE, project, 0)
    kept = ((q, refs.q_out), (k, refs.k_out), (v, refs.v_out), (pre, refs.pre_out), (meta, refs.meta_out))
    keep = [publish(ref, out, at) for at, (ref, out) in enumerate(kept)]
    keep.append(pltpu.make_async_copy(whole.at[pl.ds(0, 3), core], refs.w_out, sems.publish.at[5]))
    for copy in keep:
        copy.start()

    att_share = Sibling(plan, place, sems.att_send, sems.att_recv)
    here = pl.ds(pl.multiple_of(core * half, half), half)
    there = pl.ds(pl.multiple_of((1 - core) * half, half), half)
    keys, values = refs.keys, refs.values
    blocks = length // QB

    def att_copy(p):
        lanes = pl.ds(pl.multiple_of(p * PAIR, PAIR), PAIR)
        return att_share.copy(att.at[there, lanes], refs.att_other.at[:, lanes], p)

    def pair(p, x):
        lanes = pl.ds(pl.multiple_of(p * PAIR, PAIR), PAIR)
        keys[0:SLOTS, :] = pre[0, :, lanes]
        keys[SLOTS:, :] = k[:, lanes]
        values[0:SLOTS, :] = pre[1, :, lanes]
        values[SLOTS:, :] = v[:, lanes]

        def block(b, x):
            rows = pl.ds(pl.multiple_of(b * QB, QB), QB)
            mixed, totals = attend_block(
                q[rows, lanes], keys[...], values[...],
                refs.meta_cols[pl.ds(pl.multiple_of(SLOTS + b * QB, SLOTS), QB), 0:1],
                meta[0:1, SLOTS:], meta[0:1, :SLOTS],
            )
            att[rows, lanes] = mixed
            lse[p, :, rows] = jnp.transpose(totals)[0:8, :]
            return x

        lax.fori_loop(0, blocks // 2, block, 0)
        beat(done + plan.sides * p)
        lax.fori_loop(blocks // 2, blocks, block, 0)
        if plan.sides > 1:
            beat(done + plan.sides * p + 1)
        att_copy(p).start()
        return x

    pairs = WIDE // PAIR
    lax.fori_loop(0, pairs, pair, 0)
    done = min(last, done + plan.sides * pairs)
    keep += [publish(att, refs.att_out, 6), publish(lse, refs.lse_out, 7)]
    for copy in keep[-2:]:
        copy.start()
    for p in range(pairs):
        att_copy(p).wait_recv()

    done = ready(3 * plan.sides, plan.sides, done)
    normal_one, rstd_one, normed, acc = refs.normal_one, refs.rstd_one, refs.normed, refs.acc
    low, slope, out = refs.low, refs.slope, refs.out
    parts = half // CHUNK

    def weight(kind, side):
        return whole[kind, side].reshape(width, WIDE)

    def mix(b, x):
        rows = pl.ds(pl.multiple_of(b * CHUNK, CHUNK), CHUNK)
        own = att[pl.ds(pl.multiple_of(core * half + b * CHUNK, CHUNK), CHUNK), :]
        total = row[2 * core + b].reshape(CHUNK, width).astype(f32)
        total = total + mm_nt(own, weight(3, core)) + mm_nt(refs.att_other[rows, :], weight(3, 1 - core))
        normal, rstd = normalise(total)
        normal_one[rows, :] = normal
        rstd_one[rows, :] = jnp.broadcast_to(rstd, (CHUNK, LANES))
        low_normed = (normal * refs.gain_one[...] + refs.shift_one[...]).astype(bf16)
        normed[rows, :] = low_normed
        acc[rows, :] = low_normed.astype(f32)
        return x

    lax.fori_loop(0, parts, mix, 0)

    def feed(n, x):
        j, side = n // 2, lax.rem(n, 2)
        kind = FIRST_UP + 2 * j

        def part(b, x):
            rows = pl.ds(pl.multiple_of(b * CHUNK, CHUNK), CHUNK)
            upper = mm(normed[rows, :], weight(kind, side))
            bell = (1.0 + lax.erf(upper * (0.5**0.5))) * 0.5
            acted = (upper * bell).astype(bf16)
            slope[n, rows, :] = (
                bell + upper * jnp.exp(upper * upper * -0.5) * (1.0 / (2.0 * math.pi) ** 0.5)
            ).astype(bf16)
            acc[rows, :] += mm_nt(acted, weight(kind + 1, side))
            return x

        lax.fori_loop(0, parts, part, 0)
        return x

    groups = (KINDS - FIRST_UP) // 2
    for j in range(groups):
        done = ready((FIRST_UP + 2 * j) * plan.sides, 2 * plan.sides, done)
        lax.fori_loop(2 * j, 2 * j + 2, feed, 0)

    grad_line.settle()
    for part in range(2):
        for side in range(plan.cores):
            grad_line.receive(grad.at[part, side], 2 * core + part, side if spread else line // 2)

    back = Line(plan, place, sems.back_send, sems.back_recv)
    places = tokens.shape[1]

    def close(b, x):
        rows = pl.ds(pl.multiple_of(b * CHUNK, CHUNK), CHUNK)
        normal, rstd = normalise(acc[rows, :])
        out[rows, :] = (normal * refs.gain_two[...] + refs.shift_two[...]).astype(bf16)
        d_second = normalise_grad(
            normal, rstd, refs.gain_two[...], grad[b].reshape(CHUNK, width).astype(f32)
        )
        acc[rows, :] = d_second
        low[rows, :] = d_second.astype(bf16)
        return x

    lax.fori_loop(0, parts, close, 0)
    for b in range(2):
        for side in range(plan.cores):
            spot, target = (line, side) if spread else (lax.rem(line, 2), line // 2)
            back.send(
                out.at[pl.ds((b * plan.cores + side) * places, places)], refs.pieces.at[spot],
                2 * core + b, target,
            )

    def feed_back(n, x):
        j, side = n // 2, lax.rem(n, 2)
        kind = FIRST_UP + 2 * j

        def part(b, x):
            rows = pl.ds(pl.multiple_of(b * CHUNK, CHUNK), CHUNK)
            d_acted = mm(low[rows, :], weight(kind + 1, side))
            d_upper = (d_acted * slope[n, rows, :].astype(f32)).astype(bf16)
            acc[rows, :] += mm_nt(d_upper, weight(kind, side))
            return x

        lax.fori_loop(0, parts, part, 0)
        return x

    lax.fori_loop(0, 2 * groups, feed_back, 0)

    d_att, away = refs.d_att, refs.d_att_away
    d_share = Sibling(plan, place, sems.d_send, sems.d_recv)

    def d_copy(b):
        mine = pl.ds(pl.multiple_of(core * half + b * CHUNK, CHUNK), CHUNK)
        return d_share.copy(away.at[pl.ds(pl.multiple_of(b * CHUNK, CHUNK), CHUNK)], d_att.at[mine], b)

    def open_(b, x):
        rows = pl.ds(pl.multiple_of(b * CHUNK, CHUNK), CHUNK)
        d_first = normalise_grad(normal_one[rows, :], rstd_one[rows, 0:1], refs.gain_one[...], acc[rows, :])
        acc[rows, :] = d_first
        d_low = d_first.astype(bf16)
        away[rows, :] = mm(d_low, weight(3, 1 - core)).astype(bf16)
        d_copy(b).start()
        mine = pl.ds(pl.multiple_of(core * half + b * CHUNK, CHUNK), CHUNK)
        d_att[mine, :] = mm(d_low, weight(3, core)).astype(bf16)
        return x

    lax.fori_loop(0, parts, open_, 0)
    keep.append(publish(acc, refs.d_first_out, 8))
    keep[-1].start()
    for b in range(parts):
        d_copy(b).wait_recv()
    keep.append(publish(d_att, refs.d_att_out, 9))
    keep[-1].start()

    lax.fori_loop(0, gather.count, lambda i, x: (gather.drain(i), x)[1], 0)
    token_line.drain()
    prefix_line.drain()
    grad_line.drain()
    for chip in range(LINE):
        if spread:
            share.copy(row.at[chip, core], row.at[chip, core], chip).wait_send()
        else:
            pl.when(holds)(share.copy(row.at[chip, 0], row.at[chip, 0], chip).wait_send)
    if not spread:
        pl.when(holds)(meta_copy.wait_send)
    for p in range(pairs):
        att_copy(p).wait_send()
    for b in range(parts):
        d_copy(b).wait_send()
    back.settle()
    for j in range(held):
        back.receive(refs.pieces.at[j], j if spread else 2 * core + j, line // 2)
    back.drain()
    for copy in keep:
        copy.wait()


def forward_backward(plan, given):
    held, places, width = given.tokens.shape
    depth = given.w_query.shape[0]
    length = places * plan.tp
    half = length // 2
    pairs = WIDE // PAIR
    bf16, f32 = jnp.bfloat16, jnp.float32
    S = jax.ShapeDtypeStruct
    outs = dict(
        q_out=S((length, WIDE), bf16),
        k_out=S((length, WIDE), bf16),
        v_out=S((length, WIDE), bf16),
        att_out=S((length, WIDE), bf16),
        lse_out=S((pairs, 8, length), f32),
        pre_out=S((2, SLOTS, WIDE), bf16),
        meta_out=S((8, SLOTS + length), f32),
        d_att_out=S((length, WIDE), bf16),
        d_first_out=S((half, width), f32),
        w_out=S((3,) + plan.shape + (depth, WIDE), bf16),
        pieces=S((held, places, width), bf16),
    )
    units = 2 * (KINDS - FIRST_UP) // 2
    scratch = dict(
        source=((KINDS, plan.sides, depth, LANES), bf16),
        prefix=((held, plan.sides, 2, SLOTS, LANES), bf16),
        meta=((8, SLOTS + length), f32),
        whole=((KINDS, 2) + plan.shape + (depth, WIDE), bf16),
        row=((LINE, plan.cores, places, width), bf16),
        grad=((2, plan.cores, places, width), bf16),
        pre=((2, SLOTS, WIDE), bf16),
        q=((length, WIDE), bf16),
        k=((length, WIDE), bf16),
        v=((length, WIDE), bf16),
        att=((length, WIDE), bf16),
        lse=((pairs, 8, length), f32),
        att_other=((half, WIDE), bf16),
        keys=((SLOTS + length, PAIR), bf16),
        values=((SLOTS + length, PAIR), bf16),
        meta_cols=((SLOTS + length, 8), f32),
        normal_one=((half, width), f32),
        rstd_one=((half, LANES), f32),
        normed=((half, width), bf16),
        slope=((units, half, WIDE), bf16),
        acc=((half, width), f32),
        low=((half, width), bf16),
        out=((half, width), bf16),
        d_att=((length, WIDE), bf16),
        d_att_away=((half, WIDE), bf16),
    )
    sems = gather_semaphores(plan)
    sems.update(
        token_send=semaphores(held),
        token_recv=semaphores(LINE, 2),
        prefix_send=semaphores(held * plan.sides),
        prefix_recv=semaphores(LINE, 2),
        grad_send=semaphores(held),
        grad_recv=semaphores(LINE, 2),
        back_send=semaphores(4),
        back_recv=semaphores(LINE, 2),
        share_send=semaphores(5),
        share_recv=semaphores(5),
        att_send=semaphores(pairs),
        att_recv=semaphores(pairs),
        d_send=semaphores(half // CHUNK),
        d_recv=semaphores(half // CHUNK),
        publish=semaphores(10),
    )
    smem = pl.BlockSpec(memory_space=pltpu.SMEM)
    vmem = pl.BlockSpec(memory_space=pltpu.VMEM)
    hbm = pl.BlockSpec(memory_space=pl.ANY)
    results = pl.pallas_call(
        functools.partial(forward_backward_kernel, plan, (*vars(given), *outs, *scratch, *sems)),
        out_shape=list(outs.values()),
        in_specs=[smem, smem, smem, vmem, hbm, hbm] + [vmem] * 12,
        out_specs=[hbm] * len(outs),
        scratch_shapes=[pltpu.VMEM(*spec) for spec in scratch.values()] + list(sems.values()),
        compiler_params=pltpu.CompilerParams(
            collective_id=0, has_side_effects=True, vmem_limit_bytes=62 * 2**20
        ),
    )(*vars(given).values())
    return SimpleNamespace(**dict(zip(outs, results)))


def finish_kernel(plan, names, *args):
    refs = SimpleNamespace(**dict(zip(names, args)))
    place = plan.here()
    coords, line, core = place
    bf16, f32 = jnp.bfloat16, jnp.float32
    spread = plan.core_in_tp
    width = refs.d_first.shape[1]
    half = refs.d_first.shape[0]
    held, places = refs.pieces.shape[:2]
    tasks, slots = refs.keys_grad.shape[:2]
    parts = half // CHUNK
    kept = refs.total.shape[2]

    for chip in range(LINE):
        lanes = slice(chip * LANES, (chip + 1) * LANES)
        for which in range(2):
            refs.terms[chip, which] = refs.d_pre[which, :, lanes].astype(bf16)
        refs.terms[chip, 0, SLOTS - 16 :, :] = jnp.broadcast_to(refs.meta[1:2, 0:SLOTS], (16, SLOTS)).astype(bf16)
    greet(plan, place)
    terms = Line(plan, place, refs.terms_send, refs.terms_recv)
    for chip in range(LINE):
        terms.send(refs.terms.at[chip], refs.row_terms.at[line], chip, core)

    swap = Sibling(plan, place, refs.swap_send, refs.swap_recv)
    back = Line(plan, place, refs.back_send, refs.back_recv)

    def share(which, b):
        rows = pl.ds(pl.multiple_of(which * half + b * CHUNK, CHUNK), CHUNK)
        total = mm_nt(refs.dq[rows, :], refs.w[0].reshape(width, WIDE))
        total = total + mm_nt(refs.dk[rows, :], refs.w[1].reshape(width, WIDE))
        return total + mm_nt(refs.dv[rows, :], refs.w[2].reshape(width, WIDE))

    def swap_copy(b):
        rows = pl.ds(b * CHUNK, CHUNK)
        return swap.copy(refs.away.at[rows], refs.other.at[rows], b)

    for b in range(parts):
        rows = pl.ds(b * CHUNK, CHUNK)
        refs.away[rows, :] = share(1 - core, b).astype(bf16)
        swap_copy(b).start()
        own = share(core, b) + refs.d_first[rows, :]
        swap_copy(b).wait_recv()
        refs.sums[rows, :] = (own + refs.other[rows, :].astype(f32)).astype(bf16)
        for side in range(plan.cores):
            spot, target = (line, side) if spread else (lax.rem(line, 2), line // 2)
            back.send(
                refs.sums.at[pl.ds(b * CHUNK + side * places, places)], refs.pieces.at[spot], 2 * core + b, target
            )

    terms.settle()
    total = refs.total
    total[...] = jnp.zeros_like(total)
    for chip in range(LINE):
        terms.receive(refs.row_terms.at[chip], chip, core)
        marks = refs.row_terms[chip, 0, SLOTS - 16 :, :].astype(f32)
        for task in range(tasks):
            for which in range(2):
                total[task, which] += refs.row_terms[chip, which, 0:kept, :].astype(f32) * marks[0:1, task : task + 1]
    for step, axis in enumerate(plan.axes):
        size = plan.shape[axis]
        refs.gone[step] = total[...].astype(bf16)
        copies = [
            remote(
                refs.gone.at[step], refs.come.at[step, by - 1], refs.axis_send.at[step, by - 1],
                refs.axis_recv.at[step, by - 1],
                plan.device(shifted(coords, axis, by, size), line, core),
            )
            for by in range(1, size)
        ]
        for copy in copies:
            copy.start()
        for by, copy in enumerate(copies):
            copy.wait_recv()
            total[...] += refs.come[step, by].astype(f32)
        for copy in copies:
            copy.wait_send()

    def put(block, lanes):
        for task in range(tasks):
            refs.keys_grad[task, :, lanes] = block[task, 0, 0:slots, :]
            refs.values_grad[task, :, lanes] = block[task, 1, 0:slots, :]

    if spread:
        put(total, slice(None))
    else:
        last = swap.copy(total, refs.total_other, parts)
        last.start()

        @pl.when(core == 0)
        def _():
            put(total, slice(0, LANES))

        @pl.when(core == 1)
        def _():
            put(total, slice(LANES, 2 * LANES))

        last.wait_recv()

        @pl.when(core == 0)
        def _():
            put(refs.total_other, slice(LANES, 2 * LANES))

        @pl.when(core == 1)
        def _():
            put(refs.total_other, slice(0, LANES))

        last.wait_send()

    back.settle()
    for j in range(held):
        back.receive(refs.pieces.at[j], j if spread else 2 * core + j, line // 2)
    back.drain()
    terms.drain()
    for b in range(parts):
        swap_copy(b).wait_send()


def finish(plan, held, places, tasks, slots, part, given):
    half, width = given.d_first.shape
    steps = len(plan.axes)
    reach = max(plan.shape[a] for a in plan.axes) - 1
    kept = -(-slots // 16) * 16
    bf16, f32 = jnp.bfloat16, jnp.float32
    outs = dict(
        pieces=jax.ShapeDtypeStruct((held, places, width), bf16),
        keys_grad=jax.ShapeDtypeStruct((tasks, slots, part), f32),
        values_grad=jax.ShapeDtypeStruct((tasks, slots, part), f32),
    )
    scratch = dict(
        terms=((LINE, 2, SLOTS, LANES), bf16),
        row_terms=((LINE, 2, SLOTS, LANES), bf16),
        away=((half, width), bf16),
        other=((half, width), bf16),
        sums=((half, width), bf16),
        total=((tasks, 2, kept, LANES), f32),
        total_other=((tasks, 2, kept, LANES), f32),
        gone=((steps, tasks, 2, kept, LANES), bf16),
        come=((steps, reach, tasks, 2, kept, LANES), bf16),
    )
    sems = dict(
        terms_send=semaphores(LINE),
        terms_recv=semaphores(LINE, 2),
        swap_send=semaphores(half // CHUNK + 1),
        swap_recv=semaphores(half // CHUNK + 1),
        back_send=semaphores(4),
        back_recv=semaphores(LINE, 2),
        axis_send=semaphores(steps, reach),
        axis_recv=semaphores(steps, reach),
    )
    vmem = pl.BlockSpec(memory_space=pltpu.VMEM)
    results = pl.pallas_call(
        functools.partial(finish_kernel, plan, (*vars(given), *outs, *scratch, *sems)),
        out_shape=list(outs.values()),
        in_specs=[vmem] * len(vars(given)),
        out_specs=[pl.BlockSpec(memory_space=pl.ANY), vmem, vmem],
        scratch_shapes=[pltpu.VMEM(*spec) for spec in scratch.values()] + list(sems.values()),
        compiler_params=pltpu.CompilerParams(
            collective_id=1, has_side_effects=True, vmem_limit_bytes=48 * 2**20
        ),
    )(*vars(given).values())
    return results


def shards(
    plan, tokens, w_query, w_key, w_value, w_attn_out, w_up, w_down, first_gain, first_shift,
    second_gain, second_shift, prefix_keys, prefix_values, example_lengths, task_ids, prefix_lens,
    slot_masks, out_grad,
):
    held, places, _ = tokens.shape
    done = forward_backward(
        plan,
        SimpleNamespace(
            task_ids=task_ids,
            lengths=example_lengths,
            prefix_lens=prefix_lens,
            slot_masks=slot_masks,
            tokens=tokens,
            out_grad=out_grad,
            w_query=w_query,
            w_key=w_key,
            w_value=w_value,
            w_attn_out=w_attn_out,
            w_up=w_up,
            w_down=w_down,
            gain_one=first_gain[None],
            shift_one=first_shift[None],
            gain_two=second_gain[None],
            shift_two=second_shift[None],
            prefix_keys=prefix_keys,
            prefix_values=prefix_values,
        ),
    )
    dq, dk, dv, d_pre = attend_backward(
        example_lengths.shape[1], done.q_out, done.k_out, done.v_out, done.d_att_out, done.att_out,
        done.pre_out, done.lse_out, done.meta_out,
    )
    d_tokens, keys_grad, values_grad = finish(
        plan, held, places, *prefix_keys.shape,
        SimpleNamespace(
            dq=dq, dk=dk, dv=dv, w=done.w_out, d_first=done.d_first_out, d_pre=d_pre, meta=done.meta_out
        ),
    )
    return done.pieces, d_tokens.astype(jnp.float32), keys_grad, values_grad


def solution(mesh):
    placed = (
        P("rows", "tp", None),
        P("rows", "tp"),
        P("rows", "tp"),
        P("rows", "tp"),
        P("tp", "rows"),
        P("rows", "tp"),
        P("tp", "rows"),
        P(),
        P(),
        P(),
        P(),
        P(None, None, "tp"),
        P(None, None, "tp"),
        P("rows", None),
        P("rows"),
        P(),
        P(),
        P("rows", "tp", None),
    )
    plan = Plan(mesh.shape["rows"], mesh.shape["tp"])
    return jax.shard_map(
        functools.partial(shards, plan),
        mesh=mesh,
        in_specs=placed,
        out_specs=(
            P("rows", "tp", None),
            P("rows", "tp", None),
            P(None, None, "tp"),
            P(None, None, "tp"),
        ),
        check_vma=False,
    )
```

```python
import functools
import itertools
import math
from types import SimpleNamespace

import jax
import jax.numpy as jnp
from jax import lax
from jax.experimental import pallas as pl
from jax.experimental.pallas import tpu as pltpu
from jax.sharding import PartitionSpec as P

HD = 64
PAIR = 2 * HD
SLOTS = 128
QB = 256
KB = 256
NEG = -1e30
NT = (((1,), (1,)), ((), ()))


def mm(a, b):
    return jnp.dot(a, b, preferred_element_type=jnp.float32)


def mm_nt(a, b):
    return lax.dot_general(a, b, NT, preferred_element_type=jnp.float32)


def head_lanes(half):
    lane = lax.broadcasted_iota(jnp.int32, (1, PAIR), 1)
    return (lane >= half * HD) & (lane < (half + 1) * HD)


def only_head(a, half):
    return jnp.where(head_lanes(half), a, jnp.zeros_like(a))


def attend_block(q, keys, values, seg_col, seg_row, live_row):
    mixed = jnp.zeros((q.shape[0], PAIR), jnp.float32)
    totals = jnp.zeros((q.shape[0], PAIR), jnp.float32)
    lane = lax.broadcasted_iota(jnp.int32, (1, PAIR), 1)
    for half in range(2):
        qh = only_head(q, half) * jnp.asarray(0.125, jnp.bfloat16)
        scores = mm_nt(qh, keys)
        seq = jnp.where(seg_col == seg_row, scores[:, SLOTS:], NEG)
        pre = jnp.where(live_row > 0.5, scores[:, :SLOTS], NEG)
        top = jnp.maximum(
            jnp.max(seq, axis=1, keepdims=True), jnp.max(pre, axis=1, keepdims=True)
        )
        seq = jnp.exp(seq - top)
        pre = jnp.exp(pre - top)
        total = jnp.sum(seq, axis=1, keepdims=True) + jnp.sum(pre, axis=1, keepdims=True)
        scale = 1.0 / total
        low = jnp.concatenate([(pre * scale).astype(jnp.bfloat16), (seq * scale).astype(jnp.bfloat16)], axis=1)
        out = mm(low, values)
        mixed = jnp.where(head_lanes(half), out, mixed)
        totals = jnp.where(lane == half, top + jnp.log(total), totals)
    return mixed.astype(jnp.bfloat16), totals


def backward_kernel(
    examples, ends_ref, q_ref, k_ref, v_ref, do_ref, att_ref, pre_ref, lse_ref, meta_ref,
    dq_ref, dk_ref, dv_ref, dpre_ref,
    dk_acc, dv_acc, dpk_acc, dpv_acc, k_t, pk_t, columns,
):
    length = q_ref.shape[0]
    pk_ref, pv_ref = pre_ref.at[0], pre_ref.at[1]
    live_ref, seg_ref = columns.at[0:SLOTS], columns.at[SLOTS:]

    @pl.when(pl.program_id(0) == 0)
    def _():
        columns[...] = jnp.transpose(meta_ref[...])

    dk_acc[...] = jnp.zeros_like(dk_acc)
    dv_acc[...] = jnp.zeros_like(dv_acc)
    dpk_acc[...] = jnp.zeros_like(dpk_acc)
    dpv_acc[...] = jnp.zeros_like(dpv_acc)
    k_t[...] = jnp.transpose(k_ref[...])
    pk_t[...] = jnp.transpose(pk_ref[...])
    picks = lax.broadcasted_iota(jnp.int32, (8, PAIR), 0)
    lanes = lax.broadcasted_iota(jnp.int32, (8, PAIR), 1) // HD
    picker = jnp.where(picks == lanes, 1.0, 0.0)

    def bounds(start):
        low, high = jnp.int32(0), jnp.int32(length)
        for j in range(examples):
            end = ends_ref[2, j].astype(jnp.int32)
            low = jnp.where(end <= start, jnp.maximum(low, end), low)
            high = jnp.where(end >= start + QB, jnp.minimum(high, end), high)
        return low // KB, (high + KB - 1) // KB

    def block(b, carry):
        start = pl.multiple_of(b * QB, QB)
        rows = pl.ds(start, QB)
        q = q_ref[rows, :]
        do = do_ref[rows, :]
        prod = do.astype(jnp.float32) * att_ref[rows, :].astype(jnp.float32)
        inner = lax.dot_general(
            picker, prod, NT, preferred_element_type=jnp.float32, precision=lax.Precision.HIGHEST
        )
        seg_q = meta_ref[0:1, pl.ds(SLOTS + start, QB)]
        heads = []
        for half in range(2):
            qh = only_head(q, half) * jnp.asarray(0.125, jnp.bfloat16)
            dh = only_head(do, half)
            lse = lse_ref[0, half : half + 1, rows]
            delta = inner[half : half + 1, :]
            heads.append((qh, dh, lse, delta))

        def tile(kk, vv, kt, allowed, half):
            qh, dh, lse, delta = heads[half]
            s = mm_nt(kk, qh)
            p = jnp.exp(jnp.where(allowed, s, NEG) - lse)
            dp = mm_nt(vv, dh)
            ds = (p * (dp - delta)).astype(jnp.bfloat16)
            return mm(ds, qh), mm(p.astype(jnp.bfloat16), dh), mm(kt, ds)

        dqs = []
        for half in range(2):
            a, g, dq = tile(
                pk_ref[...], pv_ref[...], pk_t[half * HD : (half + 1) * HD, :], live_ref[:, 0:1] > 0.5, half
            )
            dpk_acc[...] += a
            dpv_acc[...] += g
            dqs.append(dq)

        def step(j, dqs):
            at = pl.multiple_of(j * KB, KB)
            krows = pl.ds(at, KB)
            allowed = seg_ref[krows, 0:1] == seg_q
            dk = dk_acc[krows, :]
            dv = dv_acc[krows, :]
            outs = []
            for half in range(2):
                a, g, dq = tile(
                    k_ref[krows, :], v_ref[krows, :], k_t[half * HD : (half + 1) * HD, krows], allowed, half
                )
                dk = dk + a
                dv = dv + g
                outs.append(dqs[half] + dq)
            dk_acc[krows, :] = dk
            dv_acc[krows, :] = dv
            return tuple(outs)

        dqs = lax.fori_loop(*bounds(start), step, tuple(dqs))
        dq_ref[rows, :] = (jnp.transpose(jnp.concatenate(dqs, axis=0)) * 0.125).astype(jnp.bfloat16)
        return carry

    lax.fori_loop(0, length // QB, block, 0)
    dk_ref[...] = dk_acc[...].astype(jnp.bfloat16)
    dv_ref[...] = dv_acc[...].astype(jnp.bfloat16)
    dpre_ref[0] = dpk_acc[...]
    dpre_ref[1] = dpv_acc[...]


def attend_backward(examples, q, k, v, do, att, pre, lse, meta):
    length, width = q.shape
    pairs = width // PAIR
    block = pl.BlockSpec((length, PAIR), lambda p: (0, p))
    pre_block = pl.BlockSpec((2, SLOTS, PAIR), lambda p: (0, 0, p))
    low = jax.ShapeDtypeStruct((length, width), jnp.bfloat16)
    return pl.pallas_call(
        functools.partial(backward_kernel, examples),
        grid=(pairs,),
        in_specs=[
            pl.BlockSpec((8, SLOTS), lambda p: (0, 0), memory_space=pltpu.SMEM),
            block, block, block, block, block, pre_block,
            pl.BlockSpec((1, 8, length), lambda p: (p, 0, 0)),
            pl.BlockSpec(meta.shape, lambda p: (0, 0)),
        ],
        out_specs=[block, block, block, pre_block],
        out_shape=[low, low, low, jax.ShapeDtypeStruct((2, SLOTS, width), jnp.float32)],
        scratch_shapes=[
            pltpu.VMEM((length, PAIR), jnp.float32),
            pltpu.VMEM((length, PAIR), jnp.float32),
            pltpu.VMEM((SLOTS, PAIR), jnp.float32),
            pltpu.VMEM((SLOTS, PAIR), jnp.float32),
            pltpu.VMEM((PAIR, length), jnp.bfloat16),
            pltpu.VMEM((PAIR, SLOTS), jnp.bfloat16),
            pltpu.VMEM((meta.shape[1], 8), jnp.float32),
        ],
        compiler_params=pltpu.CompilerParams(vmem_limit_bytes=48 * 2**20),
        cost_estimate=pl.CostEstimate(
            flops=40 * length * length * width, bytes_accessed=16 * length * width, transcendentals=0
        ),
    )(meta, q, k, v, do, att, pre, lse, meta)


MESH = pl.DeviceIdType.MESH
LINE = 4
LANES = 128
WIDE = LINE * LANES
KINDS = 12
FIRST_UP = 4
GROUPS = (KINDS - FIRST_UP) // 2
CHUNK = 256


class Plan:
    def __init__(self, rows, tp):
        self.rows = rows
        self.tp = tp
        self.core_in_tp = tp > LINE
        self.shape = (rows // 8, 2, 4) if self.core_in_tp else (rows // 4, 2, 2)
        self.axes = (0, 1, 2) if self.core_in_tp else (0, 1)
        self.cores = 2 if self.core_in_tp else 1
        self.sides = 2 // self.cores

    def here(self):
        r = lax.axis_index("rows")
        t = lax.axis_index("tp")
        a, b, c = self.shape
        coords = (r // (b * c), lax.rem(r // c, b), lax.rem(r, c))
        if self.core_in_tp:
            return coords, t // 2, lax.rem(t, 2)
        return coords, t, coords[2]

    def device(self, coords, line, core):
        a, b, c = self.shape
        if self.core_in_tp:
            return ((coords[0] * b + coords[1]) * c + coords[2], line * 2 + core)
        return ((coords[0] * b + coords[1]) * c + core, line)

    def row_core(self, chip):
        return None if self.core_in_tp else chip // 2


def shifted(coords, axis, by, size):
    moved = list(coords)
    moved[axis] = lax.rem(coords[axis] + by, size)
    return tuple(moved)


def sibling(plan, place):
    coords, line, core = place
    return plan.device(coords, line, 1 - core)


def greet(plan, place):
    coords, line, core = place
    others = [
        plan.device(coords, lax.rem(line + by, LINE), side) for by in range(1, LINE) for side in range(2)
    ]
    others.append(sibling(plan, place))
    for axis in plan.axes:
        for by in range(1, plan.shape[axis]):
            others.append(plan.device(shifted(coords, axis, by, plan.shape[axis]), line, core))
    barrier = pltpu.get_barrier_semaphore()
    for other in others:
        pl.semaphore_signal(barrier, inc=1, device_id=other, device_id_type=MESH)
    pl.semaphore_wait(barrier, len(others))


def remote(src, dst, send, recv, device):
    return pltpu.make_async_remote_copy(
        src_ref=src, dst_ref=dst, send_sem=send, recv_sem=recv, device_id=device, device_id_type=MESH
    )


class Gather:
    def __init__(self, plan, place, source, whole, sems):
        self.plan = plan
        self.place = place
        self.coords, self.line, self.core = place
        self.source = source
        self.whole = whole
        self.sems = sems
        self.count = KINDS * plan.sides
        self.depth = source.shape[-2]
        self.orders = (plan.axes, plan.axes[::-1])
        self.lanes = pl.ds(pl.multiple_of(self.line * LANES, LANES), LANES)

    def unit(self, i):
        if self.plan.core_in_tp:
            return (i, self.core)
        return (i // 2, lax.rem(i, 2))

    def own_copies(self):
        where = tuple(self.coords) + (slice(None), self.lanes)
        for at in range(self.plan.sides):
            side = self.core if self.plan.core_in_tp else at
            yield pltpu.make_async_copy(
                self.source.at[:, at], self.whole.at[(slice(None), side) + where], self.sems.own.at[at]
            )

    def block(self, i, chip):
        lanes = pl.ds(pl.multiple_of(chip * LANES, LANES), LANES)
        return self.whole.at[self.unit(i) + tuple(self.coords) + (slice(None), lanes)]

    def line_copies(self, i):
        src = self.source.at[(i, 0) if self.plan.core_in_tp else self.unit(i)]
        for at, by in enumerate((1, -1, 2, -2)):
            chip = self.line + by
            there = (chip >= 0) & (chip < LINE)
            yield there, remote(
                src, self.block(i, self.line), self.sems.line_send.at[i, at], self.sems.line_recv.at[i, self.line],
                self.plan.device(self.coords, jnp.clip(chip, 0, LINE - 1), self.core),
            )

    def pass_copies(self, i):
        for middle, first, target in ((2, 0, 3), (1, 3, 0)):
            block = self.block(i, first)
            yield self.line == middle, remote(
                block, block, self.sems.line_send.at[i, 4], self.sems.line_recv.at[i, first],
                self.plan.device(self.coords, target, self.core),
            )

    def line_arrived(self, i, chip):
        block = self.block(i, chip)
        remote(
            block, block, self.sems.line_send.at[i, 0], self.sems.line_recv.at[i, chip],
            self.plan.device(self.coords, chip, self.core),
        ).wait_recv()

    def axis_copies(self, i, step):
        rows = self.depth // 2
        for half in range(2):
            order = self.orders[half]
            axis = order[step]
            size = self.plan.shape[axis]
            index = [
                pl.ds(0, self.plan.shape[a]) if a in order[:step] else self.coords[a] for a in range(3)
            ]
            block = self.whole.at[self.unit(i) + tuple(index) + (pl.ds(half * rows, rows),)]
            for by in range(1, size):
                spot = (i, half, step, by - 1)
                yield remote(
                    block, block, self.sems.axis_send.at[spot], self.sems.axis_recv.at[spot],
                    self.plan.device(shifted(self.coords, axis, by, size), self.line, self.core),
                )

    def core_copy(self, i, side):
        if self.plan.core_in_tp:
            block = self.whole.at[i, side]
        else:
            block = self.whole.at[self.unit(i) + (slice(None), slice(None), side)]
        return remote(
            block, block, self.sems.core_send.at[i], self.sems.core_recv.at[i], sibling(self.plan, self.place)
        )

    def core_roles(self, i):
        if self.plan.core_in_tp:
            wide = i >= 3
            return wide, wide
        side = lax.rem(i, 2)
        wide = i >= 6
        return wide | (side != self.core), wide | (side == self.core)

    def start_line(self, i):
        for there, copy in self.line_copies(i):
            pl.when(there)(copy.start)

    def pass_on(self, i):
        for (here, copy), first in zip(self.pass_copies(i), (0, 3)):

            @pl.when(here)
            def _(copy=copy, first=first):
                self.line_arrived(i, first)
                copy.start()

    def start_axis(self, i, step):
        if step == 0:
            for chip in range(LINE):
                passed = ((chip == 0) & (self.line == 2)) | ((chip == 3) & (self.line == 1))
                pl.when((self.line != chip) & jnp.logical_not(passed))(functools.partial(self.line_arrived, i, chip))
        else:
            for copy in self.axis_copies(i, step - 1):
                copy.wait_recv()
        for copy in self.axis_copies(i, step):
            copy.start()

    def start_core(self, i):
        for copy in self.axis_copies(i, len(self.plan.axes) - 1):
            copy.wait_recv()
        sends, _ = self.core_roles(i)
        pl.when(sends)(lambda: self.core_copy(i, self.core).start())

    def finish(self, i):
        _, gets = self.core_roles(i)
        pl.when(gets)(lambda: self.core_copy(i, 1 - self.core).wait_recv())

    def drain(self, i):
        for there, copy in (*self.line_copies(i), *self.pass_copies(i)):
            pl.when(there)(copy.wait_send)
        for step in range(len(self.plan.axes)):
            for copy in self.axis_copies(i, step):
                copy.wait_send()
        sends, _ = self.core_roles(i)
        pl.when(sends)(lambda: self.core_copy(i, self.core).wait_send())

    def tick(self, i, ahead, lag):
        steps = len(self.plan.axes)

        def guarded(at, body):
            pl.when((at >= 0) & (at < self.count))(functools.partial(body, at))

        guarded(i + ahead, self.start_line)
        guarded(i + 1, self.pass_on)
        for step in range(steps):
            guarded(i - lag * step, lambda at, step=step: self.start_axis(at, step))
        guarded(i - lag * steps, self.start_core)

    def ticks(self, lag):
        return self.count + lag * len(self.plan.axes)


def semaphores(*shape):
    return pltpu.SemaphoreType.DMA(shape)


def gather_semaphores(plan):
    count = KINDS * plan.sides
    steps = len(plan.axes)
    reach = max(plan.shape[a] for a in plan.axes) - 1
    return dict(
        line_send=semaphores(count, 5),
        line_recv=semaphores(count, LINE),
        axis_send=semaphores(count, 2, steps, reach),
        axis_recv=semaphores(count, 2, steps, reach),
        core_send=semaphores(count),
        core_recv=semaphores(count),
        own=semaphores(2),
    )


class Line:
    def __init__(self, plan, place, send_sems, recv_sems):
        self.plan = plan
        self.coords, self.line, self.core = place
        self.send_sems = send_sems
        self.recv_sems = recv_sems
        self.pieces = []

    def here(self, chip, side):
        return (chip == self.line) & (side == self.core)

    def add(self, src, dst, chip, side):
        at = len(self.pieces)
        device = self.plan.device(self.coords, chip, side)

        def far(src, dst):
            return remote(src, dst, self.send_sems.at[at], self.recv_sems.at[self.line, self.core], device)

        near = pltpu.make_async_copy(src, dst, self.send_sems.at[at])
        self.pieces.append((self.here(chip, side), src, dst, far, near))

    def start(self, part=0, parts=1):
        for stays, src, dst, far, near in self.pieces:
            rows = src.shape[0] // parts
            cut = pl.ds(pl.multiple_of(part * rows, rows), rows) if parts > 1 else slice(None)
            pl.when(jnp.logical_not(stays))(far(src.at[cut], dst.at[cut]).start)
            pl.when(stays & (part == 0))(near.start)

    def send(self, src, dst, chip, side):
        self.add(src, dst, chip, side)
        stays, src, dst, far, near = self.pieces[-1]
        pl.when(jnp.logical_not(stays))(far(src, dst).start)
        pl.when(stays)(near.start)

    def settle(self):
        for stays, *_, near in self.pieces:
            pl.when(stays)(near.wait)

    def drain(self):
        for stays, src, dst, far, _ in self.pieces:
            pl.when(jnp.logical_not(stays))(far(src, dst).wait_send)

    def receive(self, dst, chip, side):
        copy = remote(
            dst, dst, self.send_sems.at[0], self.recv_sems.at[chip, side],
            self.plan.device(self.coords, chip, side),
        )
        pl.when(jnp.logical_not(self.here(chip, side)))(copy.wait_recv)


class Sibling:
    def __init__(self, plan, place, send_sems, recv_sems):
        self.send_sems = send_sems
        self.recv_sems = recv_sems
        self.device = sibling(plan, place)

    def copy(self, src, dst, at):
        return remote(src, dst, self.send_sems.at[at], self.recv_sems.at[at], self.device)


def normalise(z):
    mean = jnp.mean(z, axis=1, keepdims=True)
    centred = z - mean
    rstd = lax.rsqrt(jnp.mean(centred * centred, axis=1, keepdims=True) + 1e-05)
    return centred * rstd, rstd


def normalise_grad(normal, rstd, gain, grad):
    g = grad * gain
    return rstd * (
        g - jnp.mean(g, axis=1, keepdims=True) - normal * jnp.mean(g * normal, axis=1, keepdims=True)
    )


def up_kind(j):
    return FIRST_UP + j + jnp.maximum(j - 1, 0) if not isinstance(j, int) else FIRST_UP + j + max(j - 1, 0)


def down_kind(j):
    return jnp.minimum(FIRST_UP + 2 + 2 * j, KINDS - 1) if not isinstance(j, int) else min(FIRST_UP + 2 + 2 * j, KINDS - 1)


def forward_inputs(plan, place, refs, scratch):
    coords, line, core = place
    source, prefix, meta = scratch.source, scratch.prefix, scratch.meta
    sides = plan.sides

    def put(kind, block, first):
        for side in range(sides):
            at = (first + side) * LANES
            source[kind, side] = block[:, at : at + LANES]

    put(0, refs.w_query, 0)
    put(1, refs.w_key, 0)
    put(2, refs.w_value, 0)
    put(3, jnp.transpose(refs.w_attn_out[...]), 0)
    down = jnp.transpose(refs.w_down[...])
    for j in range(GROUPS):
        put(up_kind(j), refs.w_up, j * sides)
        put(down_kind(j), down, j * sides)

    slots = refs.prefix_keys.shape[1]
    prefix[...] = jnp.zeros_like(prefix)
    for j in range(refs.tokens.shape[0]):
        task = refs.task_ids[j]
        for which, table in enumerate((refs.prefix_keys, refs.prefix_values)):
            rows = table[task]
            for side in range(sides):
                prefix[j, side, which, 0:slots, :] = rows[:, side * LANES : (side + 1) * LANES]

    mine = line if plan.core_in_tp else lax.rem(line, 2)
    task = refs.task_ids[mine]
    meta[...] = jnp.zeros_like(meta)
    length = meta.shape[1] - SLOTS
    spots = lax.broadcasted_iota(jnp.int32, (1, length), 1)
    lane = lax.broadcasted_iota(jnp.int32, (1, SLOTS), 1)
    segment = jnp.zeros((1, length), jnp.float32)
    ends = jnp.zeros((1, SLOTS), jnp.float32)
    end = jnp.int32(0)
    for j in range(refs.lengths.shape[1]):
        end = end + refs.lengths[mine, j]
        segment = segment + jnp.where(spots >= end, 1.0, 0.0)
        ends = jnp.where(lane == j, end.astype(jnp.float32), ends)
    masks = refs.slot_masks
    used = jnp.zeros((1, slots), jnp.int32)
    limit = jnp.int32(0)
    for t in range(masks.shape[0]):
        used = jnp.where(task == t, masks[t : t + 1, :], used)
        limit = jnp.where(task == t, refs.prefix_lens[t], limit)
    live = jnp.where((used == 1) & (lane[:, :slots] < limit), 1.0, 0.0)
    meta[0:1, 0:slots] = live
    meta[0:1, SLOTS:] = segment
    meta[1:2, 0:SLOTS] = jnp.where(lane == task, 1.0, 0.0)
    meta[2:3, 0:SLOTS] = ends


AHEAD = 3
LAG = 2
CUTS = 8
TOKENS = 4
ATT_BEATS = 2
GRADS = 14


def forward_backward_kernel(plan, names, *args):
    refs = SimpleNamespace(**dict(zip(names, args)))
    sems = refs
    place = plan.here()
    coords, line, core = place
    bf16, f32 = jnp.bfloat16, jnp.float32
    spread = plan.core_in_tp
    tokens, row, grad, pre = refs.tokens, refs.row, refs.grad, refs.pre
    whole, meta = refs.whole, refs.meta
    q, k, v, att, lse = refs.q, refs.k, refs.v, refs.att, refs.lse
    held = tokens.shape[0]
    width = row.shape[-1]
    length = q.shape[0]
    half = length // 2
    base = 0 if spread else 2 * core
    slot = core if spread else 0
    holds = None if spread else line // 2 == core

    forward_inputs(plan, place, refs, refs)
    greet(plan, place)

    gather = Gather(plan, place, refs.source, whole, sems)
    gather.start_line(0)
    gather.start_line(1)
    token_line = Line(plan, place, sems.token_send, sems.token_recv)
    for j in range(held):
        token_line.add(tokens.at[j], row.at[line, slot], base + j, core)
    grad_line = Line(plan, place, sems.grad_send, sems.grad_recv)
    for j in range(held):
        grad_line.add(refs.out_grad.at[j], grad.at[lax.rem(line, 2), slot], base + j, line // 2)
    for copy in gather.own_copies():
        copy.start()
    for i in range(2, AHEAD):
        gather.start_line(i)
    share = Sibling(plan, place, sems.share_send, sems.share_recv)
    meta_copy = share.copy(meta, meta, 4)
    if not spread:
        pl.when(holds)(meta_copy.start)
    for copy in gather.own_copies():
        copy.wait()

    last = gather.ticks(LAG)

    grads = min(GRADS, last - CUTS)

    def beat(i, x=0):
        gather.tick(i, AHEAD, LAG)
        pl.when((i >= TOKENS) & (i < TOKENS + CUTS))(lambda: token_line.start(i - TOKENS, CUTS))
        pl.when((i >= grads) & (i < grads + CUTS))(lambda: grad_line.start(i - grads, CUTS))
        return x

    gather.pass_on(0)
    steps = LAG * len(plan.axes) + 1
    done = TOKENS + CUTS
    lax.fori_loop(0, done, beat, 0)
    prefix_line = Line(plan, place, sems.prefix_send, sems.prefix_recv)
    for j in range(held):
        for side in range(plan.sides):
            prefix_line.send(
                refs.prefix.at[j, side], pre.at[:, :, gather.lanes], base + j, core if spread else side
            )

    token_line.settle()

    def share_token(chip):
        if spread:
            token_line.receive(row.at[chip, core], chip, core)
            share.copy(row.at[chip, core], row.at[chip, core], chip).start()
        else:
            @pl.when(holds)
            def _():
                token_line.receive(row.at[chip, 0], chip, core)
                share.copy(row.at[chip, 0], row.at[chip, 0], chip).start()

    for chip in range(LINE):
        share_token(chip)
    for chip in range(LINE):
        if spread:
            share.copy(row.at[chip, 1 - core], row.at[chip, 1 - core], chip).wait_recv()
        else:
            pl.when(jnp.logical_not(holds))(share.copy(row.at[chip, 0], row.at[chip, 0], chip).wait_recv)
    if not spread:
        pl.when(jnp.logical_not(holds))(meta_copy.wait_recv)
    prefix_line.settle()
    for chip in range(LINE):
        prefix_line.receive(pre.at[:, :, pl.ds(chip * LANES, LANES)], chip, core if spread else line // 2)
    refs.meta_cols[...] = jnp.transpose(meta[...])

    def publish(ref, out, at):
        return pltpu.make_async_copy(ref, out, sems.publish.at[at])

    def ready(first, amount, done):
        until = min(last, first + amount - 1 + steps)
        if until > done:
            lax.fori_loop(done, until, beat, 0)
        for i in range(first, first + amount):
            gather.finish(i)
        return max(done, until)

    for kind, target in enumerate((q, k, v)):
        done = ready(kind * plan.sides, plan.sides, done)
        weight = whole.at[kind, core]

        def project(b, x, weight=weight, target=target):
            block = row[b].reshape(CHUNK, width)
            target[pl.ds(pl.multiple_of(b * CHUNK, CHUNK), CHUNK), :] = mm(
                block, weight[...].reshape(width, WIDE)
            ).astype(bf16)
            return x

        lax.fori_loop(0, LINE, project, 0)
        beat(done)
        done = done + 1
    kept = ((q, refs.q_out), (k, refs.k_out), (v, refs.v_out), (pre, refs.pre_out), (meta, refs.meta_out))
    keep = [publish(ref, out, at) for at, (ref, out) in enumerate(kept)]
    keep.append(pltpu.make_async_copy(whole.at[pl.ds(0, 3), core], refs.w_out, sems.publish.at[5]))
    for copy in keep:
        copy.start()


    att_share = Sibling(plan, place, sems.att_send, sems.att_recv)
    here = pl.ds(pl.multiple_of(core * half, half), half)
    there = pl.ds(pl.multiple_of((1 - core) * half, half), half)
    keys, values = refs.keys, refs.values
    blocks = length // QB

    def att_copy(p):
        lanes = pl.ds(pl.multiple_of(p * PAIR, PAIR), PAIR)
        return att_share.copy(att.at[there, lanes], refs.att_other.at[:, lanes], p)

    def pair(p, x):
        lanes = pl.ds(pl.multiple_of(p * PAIR, PAIR), PAIR)
        keys[0:SLOTS, :] = pre[0, :, lanes]
        keys[SLOTS:, :] = k[:, lanes]
        values[0:SLOTS, :] = pre[1, :, lanes]
        values[SLOTS:, :] = v[:, lanes]

        def block(b, x):
            rows = pl.ds(pl.multiple_of(b * QB, QB), QB)
            mixed, totals = attend_block(
                q[rows, lanes], keys[...], values[...],
                refs.meta_cols[pl.ds(pl.multiple_of(SLOTS + b * QB, SLOTS), QB), 0:1],
                meta[0:1, SLOTS:], meta[0:1, :SLOTS],
            )
            att[rows, lanes] = mixed
            lse[p, :, rows] = jnp.transpose(totals)[0:8, :]
            return x

        lax.fori_loop(0, blocks // 2, block, 0)
        beat(done + ATT_BEATS * p)
        lax.fori_loop(blocks // 2, blocks, block, 0)
        if ATT_BEATS > 1:
            beat(done + ATT_BEATS * p + 1)
        att_copy(p).start()
        return x

    pairs = WIDE // PAIR
    lax.fori_loop(0, pairs, pair, 0)
    done = done + ATT_BEATS * pairs
    keep += [publish(att, refs.att_out, 6), publish(lse, refs.lse_out, 7)]
    for copy in keep[-2:]:
        copy.start()
    for p in range(pairs):
        att_copy(p).wait_recv()

    done = ready(3 * plan.sides, plan.sides, done)
    normal_one, rstd_one, normed, acc = refs.normal_one, refs.rstd_one, refs.normed, refs.acc
    low, slope, out = refs.low, refs.slope, refs.out
    parts = half // CHUNK

    def weight(kind, side):
        return whole[kind, side].reshape(width, WIDE)

    def mix(b, x):
        rows = pl.ds(pl.multiple_of(b * CHUNK, CHUNK), CHUNK)
        own = att[pl.ds(pl.multiple_of(core * half + b * CHUNK, CHUNK), CHUNK), :]
        total = row[2 * core + b].reshape(CHUNK, width).astype(f32)
        total = total + mm_nt(own, weight(3, core)) + mm_nt(refs.att_other[rows, :], weight(3, 1 - core))
        normal, rstd = normalise(total)
        normal_one[rows, :] = normal
        rstd_one[rows, :] = jnp.broadcast_to(rstd, (CHUNK, LANES))
        low_normed = (normal * refs.gain_one[...] + refs.shift_one[...]).astype(bf16)
        normed[rows, :] = low_normed
        acc[rows, :] = low_normed.astype(f32)
        beat(done + b)
        return x

    lax.fori_loop(0, parts, mix, 0)
    done = done + parts

    acted = refs.acted
    chunks = [slice(b * CHUNK, (b + 1) * CHUNK) for b in range(parts)]

    def act(j, done):
        def unit(side, x):
            for rows in chunks:
                upper = mm(normed[rows, :], weight(up_kind(j), side))
                bell = (1.0 + lax.erf(upper * (0.5**0.5))) * 0.5
                acted[2 * j + side, rows, :] = (upper * bell).astype(bf16)
                slope[2 * j + side, rows, :] = (
                    bell + upper * jnp.exp(upper * upper * -0.5) * (1.0 / (2.0 * math.pi) ** 0.5)
                ).astype(bf16)
            if done < last:
                beat(done + side)
            return x

        lax.fori_loop(0, 2, unit, 0)

    def add(j, done):
        def unit(side, x):
            for rows in chunks:
                acc[rows, :] += mm_nt(acted[2 * j + side, rows, :], weight(down_kind(j), side))
            return x

        lax.fori_loop(0, 2, unit, 0)

    steps_of = sorted([(up_kind(j), act, j) for j in range(GROUPS)] + [(down_kind(j), add, j) for j in range(GROUPS)], key=lambda s: s[0])
    for kind, body, j in steps_of:
        done = ready(kind * plan.sides, plan.sides, done)
        body(j, done)
        done = done + 2 if body is act else done

    grad_line.settle()
    for part in range(2):
        for side in range(plan.cores):
            grad_line.receive(grad.at[part, side], 2 * core + part, side if spread else line // 2)

    def close(b, x):
        rows = pl.ds(pl.multiple_of(b * CHUNK, CHUNK), CHUNK)
        normal, rstd = normalise(acc[rows, :])
        out[rows, :] = (normal * refs.gain_two[...] + refs.shift_two[...]).astype(bf16)
        d_second = normalise_grad(
            normal, rstd, refs.gain_two[...], grad[b].reshape(CHUNK, width).astype(f32)
        )
        acc[rows, :] = d_second
        low[rows, :] = d_second.astype(bf16)
        return x

    lax.fori_loop(0, parts, close, 0)
    keep.append(publish(out, refs.out_out, 10))
    keep[-1].start()

    def feed_back(n, x):
        j, side = n // 2, lax.rem(n, 2)
        for rows in chunks:
            d_acted = mm(low[rows, :], weight(down_kind(j), side))
            d_upper = (d_acted * slope[n, rows, :].astype(f32)).astype(bf16)
            acc[rows, :] += mm_nt(d_upper, weight(up_kind(j), side))
        return x

    lax.fori_loop(0, 2 * GROUPS, feed_back, 0)

    d_att, away = refs.d_att, refs.d_att_away
    d_share = Sibling(plan, place, sems.d_send, sems.d_recv)

    def d_copy(b):
        mine = pl.ds(pl.multiple_of(core * half + b * CHUNK, CHUNK), CHUNK)
        return d_share.copy(away.at[pl.ds(pl.multiple_of(b * CHUNK, CHUNK), CHUNK)], d_att.at[mine], b)

    def open_(b, x):
        rows = pl.ds(pl.multiple_of(b * CHUNK, CHUNK), CHUNK)
        d_first = normalise_grad(normal_one[rows, :], rstd_one[rows, 0:1], refs.gain_one[...], acc[rows, :])
        acc[rows, :] = d_first
        d_low = d_first.astype(bf16)
        away[rows, :] = mm(d_low, weight(3, 1 - core)).astype(bf16)
        d_copy(b).start()
        mine = pl.ds(pl.multiple_of(core * half + b * CHUNK, CHUNK), CHUNK)
        d_att[mine, :] = mm(d_low, weight(3, core)).astype(bf16)
        return x

    lax.fori_loop(0, parts, open_, 0)
    keep.append(publish(acc, refs.d_first_out, 8))
    keep[-1].start()
    for b in range(parts):
        d_copy(b).wait_recv()
    keep.append(publish(d_att, refs.d_att_out, 9))
    keep[-1].start()

    lax.fori_loop(0, gather.count, lambda i, x: (gather.drain(i), x)[1], 0)
    token_line.drain()
    prefix_line.drain()
    grad_line.drain()
    for chip in range(LINE):
        if spread:
            share.copy(row.at[chip, core], row.at[chip, core], chip).wait_send()
        else:
            pl.when(holds)(share.copy(row.at[chip, 0], row.at[chip, 0], chip).wait_send)
    if not spread:
        pl.when(holds)(meta_copy.wait_send)
    for p in range(pairs):
        att_copy(p).wait_send()
    for b in range(parts):
        d_copy(b).wait_send()
    for copy in keep:
        copy.wait()


def forward_backward(plan, given):
    held, places, width = given.tokens.shape
    depth = given.w_query.shape[0]
    length = places * plan.tp
    half = length // 2
    pairs = WIDE // PAIR
    bf16, f32 = jnp.bfloat16, jnp.float32
    S = jax.ShapeDtypeStruct
    outs = dict(
        q_out=S((length, WIDE), bf16),
        k_out=S((length, WIDE), bf16),
        v_out=S((length, WIDE), bf16),
        att_out=S((length, WIDE), bf16),
        lse_out=S((pairs, 8, length), f32),
        pre_out=S((2, SLOTS, WIDE), bf16),
        meta_out=S((8, SLOTS + length), f32),
        d_att_out=S((length, WIDE), bf16),
        d_first_out=S((half, width), f32),
        w_out=S((3,) + plan.shape + (depth, WIDE), bf16),
        out_out=S((half, width), bf16),
    )
    scratch = dict(
        source=((KINDS, plan.sides, depth, LANES), bf16),
        prefix=((held, plan.sides, 2, SLOTS, LANES), bf16),
        meta=((8, SLOTS + length), f32),
        whole=((KINDS, 2) + plan.shape + (depth, WIDE), bf16),
        row=((LINE, plan.cores, places, width), bf16),
        grad=((2, plan.cores, places, width), bf16),
        pre=((2, SLOTS, WIDE), bf16),
        q=((length, WIDE), bf16),
        k=((length, WIDE), bf16),
        v=((length, WIDE), bf16),
        att=((length, WIDE), bf16),
        lse=((pairs, 8, length), f32),
        att_other=((half, WIDE), bf16),
        keys=((SLOTS + length, PAIR), bf16),
        values=((SLOTS + length, PAIR), bf16),
        meta_cols=((SLOTS + length, 8), f32),
        normal_one=((half, width), f32),
        rstd_one=((half, LANES), f32),
        normed=((half, width), bf16),
        slope=((2 * GROUPS, half, WIDE), bf16),
        acted=((2 * GROUPS, half, WIDE), bf16),
        acc=((half, width), f32),
        low=((half, width), bf16),
        out=((half, width), bf16),
        d_att=((length, WIDE), bf16),
        d_att_away=((half, WIDE), bf16),
    )
    sems = gather_semaphores(plan)
    sems.update(
        token_send=semaphores(held),
        token_recv=semaphores(LINE, 2),
        prefix_send=semaphores(held * plan.sides),
        prefix_recv=semaphores(LINE, 2),
        grad_send=semaphores(held),
        grad_recv=semaphores(LINE, 2),
        share_send=semaphores(5),
        share_recv=semaphores(5),
        att_send=semaphores(pairs),
        att_recv=semaphores(pairs),
        d_send=semaphores(half // CHUNK),
        d_recv=semaphores(half // CHUNK),
        publish=semaphores(11),
    )
    smem = pl.BlockSpec(memory_space=pltpu.SMEM)
    vmem = pl.BlockSpec(memory_space=pltpu.VMEM)
    hbm = pl.BlockSpec(memory_space=pl.ANY)
    results = pl.pallas_call(
        functools.partial(forward_backward_kernel, plan, (*vars(given), *outs, *scratch, *sems)),
        out_shape=list(outs.values()),
        in_specs=[smem, smem, smem, vmem, hbm, hbm] + [vmem] * 12,
        out_specs=[hbm] * len(outs),
        scratch_shapes=[pltpu.VMEM(*spec) for spec in scratch.values()] + list(sems.values()),
        compiler_params=pltpu.CompilerParams(
            collective_id=0, has_side_effects=True, vmem_limit_bytes=62 * 2**20
        ),
    )(*vars(given).values())
    return SimpleNamespace(**dict(zip(outs, results)))


def finish_kernel(plan, names, *args):
    refs = SimpleNamespace(**dict(zip(names, args)))
    place = plan.here()
    coords, line, core = place
    bf16, f32 = jnp.bfloat16, jnp.float32
    spread = plan.core_in_tp
    width = refs.d_first.shape[1]
    half = refs.d_first.shape[0]
    held, places = refs.pieces.shape[:2]
    tasks, slots = refs.keys_grad.shape[:2]
    parts = half // CHUNK
    kept = refs.total.shape[2]

    for chip in range(LINE):
        lanes = slice(chip * LANES, (chip + 1) * LANES)
        for which in range(2):
            refs.terms[chip, which] = refs.d_pre[which, :, lanes].astype(bf16)
        refs.terms[chip, 0, SLOTS - 16 :, :] = jnp.broadcast_to(refs.meta[1:2, 0:SLOTS], (16, SLOTS)).astype(bf16)
    greet(plan, place)
    terms = Line(plan, place, refs.terms_send, refs.terms_recv)
    for chip in range(LINE):
        terms.send(refs.terms.at[chip], refs.row_terms.at[line], chip, core)

    swap = Sibling(plan, place, refs.swap_send, refs.swap_recv)
    back = Line(plan, place, refs.back_send, refs.back_recv)

    def share(which, b):
        rows = pl.ds(pl.multiple_of(which * half + b * CHUNK, CHUNK), CHUNK)
        total = mm_nt(refs.dq[rows, :], refs.w[0].reshape(width, WIDE))
        total = total + mm_nt(refs.dk[rows, :], refs.w[1].reshape(width, WIDE))
        return total + mm_nt(refs.dv[rows, :], refs.w[2].reshape(width, WIDE))

    def swap_copy(b):
        rows = pl.ds(b * CHUNK, CHUNK)
        return swap.copy(refs.away.at[rows], refs.other.at[rows], b)

    for b in range(parts):
        rows = pl.ds(b * CHUNK, CHUNK)
        refs.away[rows, :] = share(1 - core, b).astype(bf16)
        swap_copy(b).start()
        own = share(core, b) + refs.d_first[rows, :]
        swap_copy(b).wait_recv()
        refs.sums[rows, :] = (own + refs.other[rows, :].astype(f32)).astype(bf16)
        for side in range(plan.cores):
            spot, target = (line, side) if spread else (lax.rem(line, 2), line // 2)
            back.send(
                refs.sums.at[pl.ds(b * CHUNK + side * places, places)], refs.pieces.at[spot], 2 * core + b, target
            )

    terms.settle()
    total = refs.total
    total[...] = jnp.zeros_like(total)
    for chip in range(LINE):
        terms.receive(refs.row_terms.at[chip], chip, core)
        marks = refs.row_terms[chip, 0, SLOTS - 16 :, :].astype(f32)
        for task in range(tasks):
            for which in range(2):
                total[task, which] += refs.row_terms[chip, which, 0:kept, :].astype(f32) * marks[0:1, task : task + 1]
    for step, axis in enumerate(plan.axes):
        size = plan.shape[axis]
        refs.gone[step] = total[...].astype(bf16)
        copies = [
            remote(
                refs.gone.at[step], refs.come.at[step, by - 1], refs.axis_send.at[step, by - 1],
                refs.axis_recv.at[step, by - 1],
                plan.device(shifted(coords, axis, by, size), line, core),
            )
            for by in range(1, size)
        ]
        for copy in copies:
            copy.start()
        for by, copy in enumerate(copies):
            copy.wait_recv()
            total[...] += refs.come[step, by].astype(f32)
        for copy in copies:
            copy.wait_send()

    def put(block, lanes):
        for task in range(tasks):
            refs.keys_grad[task, :, lanes] = block[task, 0, 0:slots, :]
            refs.values_grad[task, :, lanes] = block[task, 1, 0:slots, :]

    if spread:
        put(total, slice(None))
    else:
        last = swap.copy(total, refs.total_other, parts)
        last.start()

        @pl.when(core == 0)
        def _():
            put(total, slice(0, LANES))

        @pl.when(core == 1)
        def _():
            put(total, slice(LANES, 2 * LANES))

        last.wait_recv()

        @pl.when(core == 0)
        def _():
            put(refs.total_other, slice(LANES, 2 * LANES))

        @pl.when(core == 1)
        def _():
            put(refs.total_other, slice(0, LANES))

        last.wait_send()

    back.settle()
    for j in range(held):
        back.receive(refs.pieces.at[j], j if spread else 2 * core + j, line // 2)
    back.drain()
    terms.drain()
    for b in range(parts):
        swap_copy(b).wait_send()


def finish(plan, held, places, tasks, slots, part, given):
    half, width = given.d_first.shape
    steps = len(plan.axes)
    reach = max(plan.shape[a] for a in plan.axes) - 1
    kept = -(-slots // 16) * 16
    bf16, f32 = jnp.bfloat16, jnp.float32
    outs = dict(
        pieces=jax.ShapeDtypeStruct((held, places, width), bf16),
        keys_grad=jax.ShapeDtypeStruct((tasks, slots, part), f32),
        values_grad=jax.ShapeDtypeStruct((tasks, slots, part), f32),
    )
    scratch = dict(
        terms=((LINE, 2, SLOTS, LANES), bf16),
        row_terms=((LINE, 2, SLOTS, LANES), bf16),
        away=((half, width), bf16),
        other=((half, width), bf16),
        sums=((half, width), bf16),
        total=((tasks, 2, kept, LANES), f32),
        total_other=((tasks, 2, kept, LANES), f32),
        gone=((steps, tasks, 2, kept, LANES), bf16),
        come=((steps, reach, tasks, 2, kept, LANES), bf16),
    )
    sems = dict(
        terms_send=semaphores(LINE),
        terms_recv=semaphores(LINE, 2),
        swap_send=semaphores(half // CHUNK + 1),
        swap_recv=semaphores(half // CHUNK + 1),
        back_send=semaphores(4),
        back_recv=semaphores(LINE, 2),
        axis_send=semaphores(steps, reach),
        axis_recv=semaphores(steps, reach),
    )
    vmem = pl.BlockSpec(memory_space=pltpu.VMEM)
    results = pl.pallas_call(
        functools.partial(finish_kernel, plan, (*vars(given), *outs, *scratch, *sems)),
        out_shape=list(outs.values()),
        in_specs=[vmem] * len(vars(given)),
        out_specs=[pl.BlockSpec(memory_space=pl.ANY), vmem, vmem],
        scratch_shapes=[pltpu.VMEM(*spec) for spec in scratch.values()] + list(sems.values()),
        compiler_params=pltpu.CompilerParams(
            collective_id=1, has_side_effects=True, vmem_limit_bytes=48 * 2**20
        ),
    )(*vars(given).values())
    return results


def hand_out(plan, part, held, places):
    _, line, core = plan.here()
    count = 2 * plan.cores
    piece = lax.rem(line, 2) * plan.cores + (core if plan.core_in_tp else 0)
    pieces = part.reshape(count, places, -1)
    a, b, c = plan.shape
    got = []
    for k in range(count):
        pairs = []
        for place in itertools.product(range(a), range(b), range(c), range(LINE), range(2)):
            coords, chip, side = place[:3], place[3], place[4]
            if not plan.core_in_tp and coords[2] != side:
                continue
            which = (chip % count) ^ k
            target = which % 2 if plan.core_in_tp else chip // 2
            ends = plan.device(coords, chip, side), plan.device(coords, 2 * side + which // plan.cores, target)
            pairs.append(tuple(r * plan.tp + t for r, t in ends))
        mine = lax.dynamic_index_in_dim(pieces, lax.rem(line, count) ^ k, 0, keepdims=False)
        got.append(lax.ppermute(mine, ("rows", "tp"), pairs))
    slots = []
    for j in range(held):
        slot = got[0]
        for k in range(1, count):
            slot = jnp.where(piece ^ j == k, got[k], slot)
        slots.append(slot)
    return jnp.stack(slots)


def shards(
    plan, tokens, w_query, w_key, w_value, w_attn_out, w_up, w_down, first_gain, first_shift,
    second_gain, second_shift, prefix_keys, prefix_values, example_lengths, task_ids, prefix_lens,
    slot_masks, out_grad,
):
    held, places, _ = tokens.shape
    done = forward_backward(
        plan,
        SimpleNamespace(
            task_ids=task_ids,
            lengths=example_lengths,
            prefix_lens=prefix_lens,
            slot_masks=slot_masks,
            tokens=tokens,
            out_grad=out_grad,
            w_query=w_query,
            w_key=w_key,
            w_value=w_value,
            w_attn_out=w_attn_out,
            w_up=w_up,
            w_down=w_down,
            gain_one=first_gain[None],
            shift_one=first_shift[None],
            gain_two=second_gain[None],
            shift_two=second_shift[None],
            prefix_keys=prefix_keys,
            prefix_values=prefix_values,
        ),
    )
    output = hand_out(plan, done.out_out, held, places)
    dq, dk, dv, d_pre = attend_backward(
        example_lengths.shape[1], done.q_out, done.k_out, done.v_out, done.d_att_out, done.att_out,
        done.pre_out, done.lse_out, done.meta_out,
    )
    d_tokens, keys_grad, values_grad = finish(
        plan, held, places, *prefix_keys.shape,
        SimpleNamespace(
            dq=dq, dk=dk, dv=dv, w=done.w_out, d_first=done.d_first_out, d_pre=d_pre, meta=done.meta_out
        ),
    )
    return output, d_tokens.astype(jnp.float32), keys_grad, values_grad


def solution(mesh):
    placed = (
        P("rows", "tp", None),
        P("rows", "tp"),
        P("rows", "tp"),
        P("rows", "tp"),
        P("tp", "rows"),
        P("rows", "tp"),
        P("tp", "rows"),
        P(),
        P(),
        P(),
        P(),
        P(None, None, "tp"),
        P(None, None, "tp"),
        P("rows", None),
        P("rows"),
        P(),
        P(),
        P("rows", "tp", None),
    )
    plan = Plan(mesh.shape["rows"], mesh.shape["tp"])
    return jax.shard_map(
        functools.partial(shards, plan),
        mesh=mesh,
        in_specs=placed,
        out_specs=(
            P("rows", "tp", None),
            P("rows", "tp", None),
            P(None, None, "tp"),
            P(None, None, "tp"),
        ),
        check_vma=False,
    )
```

```python
import functools
import math
from types import SimpleNamespace

import jax
import jax.numpy as jnp
from jax import lax
from jax.experimental import pallas as pl
from jax.experimental.pallas import tpu as pltpu
from jax.sharding import PartitionSpec as P

HD = 64
PAIR = 2 * HD
SLOTS = 128
QB = 256
KB = 256
REACH = 512
NEG = -1e30
NT = (((1,), (1,)), ((), ()))


def mm(a, b):
    return jnp.dot(a, b, preferred_element_type=jnp.float32)


def mm_nt(a, b):
    return lax.dot_general(a, b, NT, preferred_element_type=jnp.float32)


def head_lanes(half):
    lane = lax.broadcasted_iota(jnp.int32, (1, PAIR), 1)
    return (lane >= half * HD) & (lane < (half + 1) * HD)


def only_head(a, half):
    return jnp.where(head_lanes(half), a, jnp.zeros_like(a))


def attend_block(q, keys, values, seg_col, seg_row, live_row):
    mixed = jnp.zeros((q.shape[0], PAIR), jnp.float32)
    totals = jnp.zeros((q.shape[0], PAIR), jnp.float32)
    lane = lax.broadcasted_iota(jnp.int32, (1, PAIR), 1)
    for half in range(2):
        qh = only_head(q, half) * jnp.asarray(0.125, jnp.bfloat16)
        scores = mm_nt(qh, keys)
        seq = jnp.where(seg_col == seg_row, scores[:, SLOTS:], NEG)
        pre = jnp.where(live_row > 0.5, scores[:, :SLOTS], NEG)
        top = jnp.maximum(
            jnp.max(seq, axis=1, keepdims=True), jnp.max(pre, axis=1, keepdims=True)
        )
        seq = jnp.exp(seq - top)
        pre = jnp.exp(pre - top)
        total = jnp.sum(seq, axis=1, keepdims=True) + jnp.sum(pre, axis=1, keepdims=True)
        scale = 1.0 / total
        low = jnp.concatenate([(pre * scale).astype(jnp.bfloat16), (seq * scale).astype(jnp.bfloat16)], axis=1)
        out = mm(low, values)
        mixed = jnp.where(head_lanes(half), out, mixed)
        totals = jnp.where(lane == half, top + jnp.log(total), totals)
    return mixed.astype(jnp.bfloat16), totals


def inner_rows(do, att):
    picks = lax.broadcasted_iota(jnp.int32, (8, PAIR), 0)
    lanes = lax.broadcasted_iota(jnp.int32, (8, PAIR), 1) // HD
    picker = jnp.where(picks == lanes, 1.0, 0.0).astype(jnp.bfloat16)
    prod = do.astype(jnp.float32) * att.astype(jnp.float32)
    high = prod.astype(jnp.bfloat16)
    return mm_nt(picker, high) + mm_nt(picker, (prod - high.astype(jnp.float32)).astype(jnp.bfloat16))


def gradient_tile(keys, values, q, do, rows, allowed):
    back = jnp.transpose(keys)
    d_keys = jnp.zeros(keys.shape, jnp.float32)
    d_values = jnp.zeros(keys.shape, jnp.float32)
    d_query = []
    scaled = q * jnp.asarray(0.125, jnp.bfloat16)
    for half in range(2):
        qh, dh = only_head(scaled, half), only_head(do, half)
        scores = jnp.where(allowed, mm_nt(keys, qh), NEG)
        probs = jnp.exp(scores - rows[half : half + 1, :])
        d_scores = (probs * (mm_nt(values, dh) - rows[2 + half : 3 + half, :])).astype(jnp.bfloat16)
        d_keys = d_keys + mm(d_scores, qh)
        d_values = d_values + mm(probs.astype(jnp.bfloat16), dh)
        d_query.append(mm(back[half * HD : (half + 1) * HD, :], d_scores))
    return d_keys, d_values, jnp.concatenate(d_query, axis=0)


MESH = pl.DeviceIdType.MESH
LINE = 4
LANES = 128
WIDE = LINE * LANES
KINDS = 12
FIRST_UP = 4
GROUPS = (KINDS - FIRST_UP) // 2
CHUNK = 256


class Plan:
    def __init__(self, rows, tp):
        self.rows = rows
        self.tp = tp
        self.core_in_tp = tp > LINE
        self.shape = (rows // 8, 2, 4) if self.core_in_tp else (rows // 4, 2, 2)
        self.axes = (0, 1, 2) if self.core_in_tp else (0, 1)
        self.cores = 2 if self.core_in_tp else 1
        self.sides = 2 // self.cores

    def here(self):
        r = lax.axis_index("rows")
        t = lax.axis_index("tp")
        a, b, c = self.shape
        coords = (r // (b * c), lax.rem(r // c, b), lax.rem(r, c))
        if self.core_in_tp:
            return coords, t // 2, lax.rem(t, 2)
        return coords, t, coords[2]

    def device(self, coords, line, core):
        a, b, c = self.shape
        if self.core_in_tp:
            return ((coords[0] * b + coords[1]) * c + coords[2], line * 2 + core)
        return ((coords[0] * b + coords[1]) * c + core, line)

    def row_core(self, chip):
        return None if self.core_in_tp else chip // 2


def shifted(coords, axis, by, size):
    moved = list(coords)
    moved[axis] = lax.rem(coords[axis] + by, size)
    return tuple(moved)


def sibling(plan, place):
    coords, line, core = place
    return plan.device(coords, line, 1 - core)


def greet(plan, place):
    coords, line, core = place
    others = [
        plan.device(coords, lax.rem(line + by, LINE), side) for by in range(1, LINE) for side in range(2)
    ]
    others.append(sibling(plan, place))
    for axis in plan.axes:
        for by in range(1, plan.shape[axis]):
            others.append(plan.device(shifted(coords, axis, by, plan.shape[axis]), line, core))
    barrier = pltpu.get_barrier_semaphore()
    for other in others:
        pl.semaphore_signal(barrier, inc=1, device_id=other, device_id_type=MESH)
    pl.semaphore_wait(barrier, len(others))


def remote(src, dst, send, recv, device):
    return pltpu.make_async_remote_copy(
        src_ref=src, dst_ref=dst, send_sem=send, recv_sem=recv, device_id=device, device_id_type=MESH
    )


class Gather:
    def __init__(self, plan, place, source, whole, sems):
        self.plan = plan
        self.place = place
        self.coords, self.line, self.core = place
        self.source = source
        self.whole = whole
        self.sems = sems
        self.count = KINDS * plan.sides
        self.depth = source.shape[-2]
        self.orders = (plan.axes, plan.axes[::-1])
        self.lanes = pl.ds(pl.multiple_of(self.line * LANES, LANES), LANES)

    def unit(self, i):
        if self.plan.core_in_tp:
            return (i, self.core)
        return (i // 2, lax.rem(i, 2))

    def own_copies(self):
        where = tuple(self.coords) + (slice(None), self.lanes)
        for at in range(self.plan.sides):
            side = self.core if self.plan.core_in_tp else at
            yield pltpu.make_async_copy(
                self.source.at[:, at], self.whole.at[(slice(None), side) + where], self.sems.own.at[at]
            )

    def block(self, i, chip):
        lanes = pl.ds(pl.multiple_of(chip * LANES, LANES), LANES)
        return self.whole.at[self.unit(i) + tuple(self.coords) + (slice(None), lanes)]

    def line_copies(self, i):
        src = self.source.at[(i, 0) if self.plan.core_in_tp else self.unit(i)]
        for at, by in enumerate((1, -1, 2, -2)):
            chip = self.line + by
            there = (chip >= 0) & (chip < LINE)
            yield there, remote(
                src, self.block(i, self.line), self.sems.line_send.at[i, at], self.sems.line_recv.at[i, self.line],
                self.plan.device(self.coords, jnp.clip(chip, 0, LINE - 1), self.core),
            )

    def pass_copies(self, i):
        for middle, first, target in ((2, 0, 3), (1, 3, 0)):
            block = self.block(i, first)
            yield self.line == middle, remote(
                block, block, self.sems.line_send.at[i, 4], self.sems.line_recv.at[i, first],
                self.plan.device(self.coords, target, self.core),
            )

    def line_arrived(self, i, chip):
        block = self.block(i, chip)
        remote(
            block, block, self.sems.line_send.at[i, 0], self.sems.line_recv.at[i, chip],
            self.plan.device(self.coords, chip, self.core),
        ).wait_recv()

    def axis_copies(self, i, step):
        rows = self.depth // 2
        for half in range(2):
            order = self.orders[half]
            axis = order[step]
            size = self.plan.shape[axis]
            index = [
                pl.ds(0, self.plan.shape[a]) if a in order[:step] else self.coords[a] for a in range(3)
            ]
            block = self.whole.at[self.unit(i) + tuple(index) + (pl.ds(half * rows, rows),)]
            for by in range(1, size):
                spot = (i, half, step, by - 1)
                yield remote(
                    block, block, self.sems.axis_send.at[spot], self.sems.axis_recv.at[spot],
                    self.plan.device(shifted(self.coords, axis, by, size), self.line, self.core),
                )

    def core_copy(self, i, side):
        if self.plan.core_in_tp:
            block = self.whole.at[i, side]
        else:
            block = self.whole.at[self.unit(i) + (slice(None), slice(None), side)]
        return remote(
            block, block, self.sems.core_send.at[i], self.sems.core_recv.at[i], sibling(self.plan, self.place)
        )

    def core_roles(self, i):
        if self.plan.core_in_tp:
            wide = i >= 3
            return wide, wide
        side = lax.rem(i, 2)
        wide = i >= 6
        return wide | (side != self.core), wide | (side == self.core)

    def start_line(self, i):
        for there, copy in self.line_copies(i):
            pl.when(there)(copy.start)

    def pass_on(self, i):
        for (here, copy), first in zip(self.pass_copies(i), (0, 3)):

            @pl.when(here)
            def _(copy=copy, first=first):
                self.line_arrived(i, first)
                copy.start()

    def start_axis(self, i, step):
        if step == 0:
            for chip in range(LINE):
                passed = ((chip == 0) & (self.line == 2)) | ((chip == 3) & (self.line == 1))
                pl.when((self.line != chip) & jnp.logical_not(passed))(functools.partial(self.line_arrived, i, chip))
        else:
            for copy in self.axis_copies(i, step - 1):
                copy.wait_recv()
        for copy in self.axis_copies(i, step):
            copy.start()

    def start_core(self, i):
        for copy in self.axis_copies(i, len(self.plan.axes) - 1):
            copy.wait_recv()
        sends, _ = self.core_roles(i)
        pl.when(sends)(lambda: self.core_copy(i, self.core).start())

    def finish(self, i):
        _, gets = self.core_roles(i)
        pl.when(gets)(lambda: self.core_copy(i, 1 - self.core).wait_recv())

    def drain(self, i):
        for there, copy in (*self.line_copies(i), *self.pass_copies(i)):
            pl.when(there)(copy.wait_send)
        for step in range(len(self.plan.axes)):
            for copy in self.axis_copies(i, step):
                copy.wait_send()
        sends, _ = self.core_roles(i)
        pl.when(sends)(lambda: self.core_copy(i, self.core).wait_send())

    def tick(self, i, ahead, lag):
        steps = len(self.plan.axes)

        def guarded(at, body):
            pl.when((at >= 0) & (at < self.count))(functools.partial(body, at))

        guarded(i + ahead, self.start_line)
        guarded(i + 1, self.pass_on)
        for step in range(steps):
            guarded(i - lag * step, lambda at, step=step: self.start_axis(at, step))
        guarded(i - lag * steps, self.start_core)

    def ticks(self, lag):
        return self.count + lag * len(self.plan.axes)


def semaphores(*shape):
    return pltpu.SemaphoreType.DMA(shape)


def gather_semaphores(plan):
    count = KINDS * plan.sides
    steps = len(plan.axes)
    reach = max(plan.shape[a] for a in plan.axes) - 1
    return dict(
        line_send=semaphores(count, 5),
        line_recv=semaphores(count, LINE),
        axis_send=semaphores(count, 2, steps, reach),
        axis_recv=semaphores(count, 2, steps, reach),
        core_send=semaphores(count),
        core_recv=semaphores(count),
        own=semaphores(2),
    )


class Line:
    def __init__(self, plan, place, send_sems, recv_sems):
        self.plan = plan
        self.coords, self.line, self.core = place
        self.send_sems = send_sems
        self.recv_sems = recv_sems
        self.pieces = []

    def here(self, chip, side):
        return (chip == self.line) & (side == self.core)

    def add(self, src, dst, chip, side):
        at = len(self.pieces)
        device = self.plan.device(self.coords, chip, side)

        def far(src, dst):
            return remote(src, dst, self.send_sems.at[at], self.recv_sems.at[self.line, self.core], device)

        near = pltpu.make_async_copy(src, dst, self.send_sems.at[at])
        self.pieces.append((self.here(chip, side), src, dst, far, near))

    def start(self, part=0, parts=1):
        for stays, src, dst, far, near in self.pieces:
            rows = src.shape[0] // parts
            cut = pl.ds(pl.multiple_of(part * rows, rows), rows) if parts > 1 else slice(None)
            pl.when(jnp.logical_not(stays))(far(src.at[cut], dst.at[cut]).start)
            pl.when(stays & (part == 0))(near.start)

    def send(self, src, dst, chip, side):
        self.add(src, dst, chip, side)
        stays, src, dst, far, near = self.pieces[-1]
        pl.when(jnp.logical_not(stays))(far(src, dst).start)
        pl.when(stays)(near.start)

    def settle(self):
        for stays, *_, near in self.pieces:
            pl.when(stays)(near.wait)

    def drain(self):
        for stays, src, dst, far, _ in self.pieces:
            pl.when(jnp.logical_not(stays))(far(src, dst).wait_send)

    def receive(self, dst, chip, side):
        copy = remote(
            dst, dst, self.send_sems.at[0], self.recv_sems.at[chip, side],
            self.plan.device(self.coords, chip, side),
        )
        pl.when(jnp.logical_not(self.here(chip, side)))(copy.wait_recv)


class Sibling:
    def __init__(self, plan, place, send_sems, recv_sems):
        self.send_sems = send_sems
        self.recv_sems = recv_sems
        self.device = sibling(plan, place)

    def copy(self, src, dst, at):
        return remote(src, dst, self.send_sems.at[at], self.recv_sems.at[at], self.device)


class PrefixSum:
    def __init__(self, plan, place, refs):
        self.plan = plan
        self.place = place
        self.refs = refs
        self.coords, self.line, self.core = place
        self.terms = Line(plan, place, refs.terms_send, refs.terms_recv)
        self.last = Sibling(plan, place, refs.total_send, refs.total_recv)

    def start(self):
        refs = self.refs
        for chip in range(LINE):
            lanes = slice(chip * LANES, (chip + 1) * LANES)
            for which in range(2):
                refs.terms[chip, which] = refs.d_pre[which, :, lanes].astype(jnp.bfloat16)
            refs.terms[chip, 0, SLOTS - 16 :, :] = jnp.broadcast_to(refs.meta[1:2, 0:SLOTS], (16, SLOTS)).astype(
                jnp.bfloat16
            )
        for chip in range(LINE):
            self.terms.send(refs.terms.at[chip], refs.row_terms.at[self.line], chip, self.core)

    def copies(self, step):
        refs = self.refs
        axis = self.plan.axes[step]
        size = self.plan.shape[axis]
        return [
            remote(
                refs.gone.at[step], refs.come.at[step, by - 1], refs.sum_send.at[step, by - 1],
                refs.sum_recv.at[step, by - 1],
                self.plan.device(shifted(self.coords, axis, by, size), self.line, self.core),
            )
            for by in range(1, size)
        ]

    def send(self, step):
        self.refs.gone[step] = self.refs.total[...].astype(jnp.bfloat16)
        for copy in self.copies(step):
            copy.start()

    def line_sum(self):
        refs = self.refs
        total = refs.total
        tasks, _, kept = total.shape[:3]
        self.terms.settle()
        for chip in range(LINE):
            self.terms.receive(refs.row_terms.at[chip], chip, self.core)
            marks = refs.row_terms[chip, 0, SLOTS - 16 :, :].astype(jnp.float32)
            for task in range(tasks):
                for which in range(2):
                    more = refs.row_terms[chip, which, 0:kept, :].astype(jnp.float32) * marks[0:1, task : task + 1]
                    total[task, which] = more if chip == 0 else total[task, which] + more

    def receive(self, step):
        for by, copy in enumerate(self.copies(step)):
            copy.wait_recv()
            self.refs.total[...] += self.refs.come[step, by].astype(jnp.float32)

    def go_on(self, beat):
        steps = len(self.plan.axes)
        if beat == 0:
            self.line_sum()
        elif beat <= steps:
            self.receive(beat - 1)
        if beat < steps:
            self.send(beat)
        elif beat == steps and not self.plan.core_in_tp:
            self.last.copy(self.refs.total, self.refs.total_other, 0).start()

    def put(self, block, lanes):
        refs = self.refs
        tasks, slots = refs.keys_grad.shape[:2]
        for task in range(tasks):
            refs.keys_grad[task, :, lanes] = block[task, 0, 0:slots, :]
            refs.values_grad[task, :, lanes] = block[task, 1, 0:slots, :]

    def finish(self, beats):
        refs = self.refs
        steps = len(self.plan.axes)
        for beat in range(beats, steps + 1):
            self.go_on(beat)
        if self.plan.core_in_tp:
            self.put(refs.total, slice(None))
        else:
            self.last.copy(refs.total, refs.total_other, 0).wait_recv()
            sides = slice(0, LANES), slice(LANES, 2 * LANES)
            for side in range(2):

                @pl.when(self.core == side)
                def _(side=side):
                    self.put(refs.total, sides[side])
                    self.put(refs.total_other, sides[1 - side])

            self.last.copy(refs.total, refs.total_other, 0).wait_send()
        self.terms.drain()
        for step in range(steps):
            for copy in self.copies(step):
                copy.wait_send()


def normalise(z):
    mean = jnp.mean(z, axis=1, keepdims=True)
    centred = z - mean
    rstd = lax.rsqrt(jnp.mean(centred * centred, axis=1, keepdims=True) + 1e-05)
    return centred * rstd, rstd


def normalise_grad(normal, rstd, gain, grad):
    g = grad * gain
    return rstd * (
        g - jnp.mean(g, axis=1, keepdims=True) - normal * jnp.mean(g * normal, axis=1, keepdims=True)
    )


def up_kind(j):
    return FIRST_UP + j + jnp.maximum(j - 1, 0) if not isinstance(j, int) else FIRST_UP + j + max(j - 1, 0)


def down_kind(j):
    return jnp.minimum(FIRST_UP + 2 + 2 * j, KINDS - 1) if not isinstance(j, int) else min(FIRST_UP + 2 + 2 * j, KINDS - 1)


def forward_inputs(plan, place, refs, scratch):
    coords, line, core = place
    source, prefix, meta = scratch.source, scratch.prefix, scratch.meta
    sides = plan.sides

    def put(kind, block, first):
        for side in range(sides):
            at = (first + side) * LANES
            source[kind, side] = block[:, at : at + LANES]

    put(0, refs.w_query, 0)
    put(1, refs.w_key, 0)
    put(2, refs.w_value, 0)
    put(3, jnp.transpose(refs.w_attn_out[...]), 0)
    down = jnp.transpose(refs.w_down[...])
    for j in range(GROUPS):
        put(up_kind(j), refs.w_up, j * sides)
        put(down_kind(j), down, j * sides)

    slots = refs.prefix_keys.shape[1]
    prefix[...] = jnp.zeros_like(prefix)
    for j in range(refs.tokens.shape[0]):
        task = refs.task_ids[j]
        for which, table in enumerate((refs.prefix_keys, refs.prefix_values)):
            rows = table[task]
            for side in range(sides):
                prefix[j, side, which, 0:slots, :] = rows[:, side * LANES : (side + 1) * LANES]

    mine = line if plan.core_in_tp else lax.rem(line, 2)
    task = refs.task_ids[mine]
    meta[...] = jnp.zeros_like(meta)
    length = meta.shape[1] - SLOTS
    spots = lax.broadcasted_iota(jnp.int32, (1, length), 1)
    lane = lax.broadcasted_iota(jnp.int32, (1, SLOTS), 1)
    segment = jnp.zeros((1, length), jnp.float32)
    ends = jnp.zeros((1, SLOTS), jnp.float32)
    end = jnp.int32(0)
    for j in range(refs.lengths.shape[1]):
        end = end + refs.lengths[mine, j]
        segment = segment + jnp.where(spots >= end, 1.0, 0.0)
        ends = jnp.where(lane == j, end.astype(jnp.float32), ends)
    masks = refs.slot_masks
    used = jnp.zeros((1, slots), jnp.int32)
    limit = jnp.int32(0)
    for t in range(masks.shape[0]):
        used = jnp.where(task == t, masks[t : t + 1, :], used)
        limit = jnp.where(task == t, refs.prefix_lens[t], limit)
    live = jnp.where((used == 1) & (lane[:, :slots] < limit), 1.0, 0.0)
    meta[0:1, 0:slots] = live
    meta[0:1, SLOTS:] = segment
    meta[1:2, 0:SLOTS] = jnp.where(lane == task, 1.0, 0.0)
    meta[2:3, 0:SLOTS] = ends


AHEAD = 3
LAG = 2
CUTS = 8
TOKENS = 4
ATT_BEATS = 2
GRADS = 14


def forward_backward_kernel(plan, names, *args):
    refs = SimpleNamespace(**dict(zip(names, args)))
    sems = refs
    place = plan.here()
    coords, line, core = place
    bf16, f32 = jnp.bfloat16, jnp.float32
    spread = plan.core_in_tp
    tokens, row, grad, pre = refs.tokens, refs.row, refs.grad, refs.pre
    whole, meta = refs.whole, refs.meta
    q, k, v, att, lse = refs.q, refs.k, refs.v, refs.att, refs.lse
    held = tokens.shape[0]
    width = row.shape[-1]
    length = q.shape[0]
    half = length // 2
    base = 0 if spread else 2 * core
    slot = core if spread else 0
    holds = None if spread else line // 2 == core

    forward_inputs(plan, place, refs, refs)
    greet(plan, place)

    gather = Gather(plan, place, refs.source, whole, sems)
    gather.start_line(0)
    gather.start_line(1)
    token_line = Line(plan, place, sems.token_send, sems.token_recv)
    for j in range(held):
        token_line.add(tokens.at[j], row.at[line, slot], base + j, core)
    grad_line = Line(plan, place, sems.grad_send, sems.grad_recv)
    for j in range(held):
        grad_line.add(refs.out_grad.at[j], grad.at[lax.rem(line, 2), slot], base + j, line // 2)
    for copy in gather.own_copies():
        copy.start()
    for i in range(2, AHEAD):
        gather.start_line(i)
    share = Sibling(plan, place, sems.share_send, sems.share_recv)
    meta_copy = share.copy(meta, meta, 4)
    if not spread:
        pl.when(holds)(meta_copy.start)
    for copy in gather.own_copies():
        copy.wait()

    last = gather.ticks(LAG)

    grads = min(GRADS, last - CUTS)

    def beat(i, x=0):
        gather.tick(i, AHEAD, LAG)
        pl.when((i >= TOKENS) & (i < TOKENS + CUTS))(lambda: token_line.start(i - TOKENS, CUTS))
        pl.when((i >= grads) & (i < grads + CUTS))(lambda: grad_line.start(i - grads, CUTS))
        return x

    gather.pass_on(0)
    steps = LAG * len(plan.axes) + 1
    done = TOKENS + CUTS
    lax.fori_loop(0, done, beat, 0)
    prefix_line = Line(plan, place, sems.prefix_send, sems.prefix_recv)
    for j in range(held):
        for side in range(plan.sides):
            prefix_line.send(
                refs.prefix.at[j, side], pre.at[:, :, gather.lanes], base + j, core if spread else side
            )

    token_line.settle()

    def share_token(chip):
        if spread:
            token_line.receive(row.at[chip, core], chip, core)
            share.copy(row.at[chip, core], row.at[chip, core], chip).start()
        else:
            @pl.when(holds)
            def _():
                token_line.receive(row.at[chip, 0], chip, core)
                share.copy(row.at[chip, 0], row.at[chip, 0], chip).start()

    for chip in range(LINE):
        share_token(chip)
    for chip in range(LINE):
        if spread:
            share.copy(row.at[chip, 1 - core], row.at[chip, 1 - core], chip).wait_recv()
        else:
            pl.when(jnp.logical_not(holds))(share.copy(row.at[chip, 0], row.at[chip, 0], chip).wait_recv)
    if not spread:
        pl.when(jnp.logical_not(holds))(meta_copy.wait_recv)
    prefix_line.settle()
    for chip in range(LINE):
        prefix_line.receive(pre.at[:, :, pl.ds(chip * LANES, LANES)], chip, core if spread else line // 2)
    refs.meta_cols[...] = jnp.transpose(meta[...])

    def ready(first, amount, done):
        until = min(last, first + amount - 1 + steps)
        if until > done:
            lax.fori_loop(done, until, beat, 0)
        for i in range(first, first + amount):
            gather.finish(i)
        return max(done, until)

    for kind, target in enumerate((q, k, v)):
        done = ready(kind * plan.sides, plan.sides, done)
        weight = whole.at[kind, core]

        def project(b, x, weight=weight, target=target):
            block = row[b].reshape(CHUNK, width)
            target[pl.ds(pl.multiple_of(b * CHUNK, CHUNK), CHUNK), :] = mm(
                block, weight[...].reshape(width, WIDE)
            ).astype(bf16)
            return x

        lax.fori_loop(0, LINE, project, 0)
        beat(done)
        done = done + 1
    att_share = Sibling(plan, place, sems.att_send, sems.att_recv)
    here = pl.ds(pl.multiple_of(core * half, half), half)
    there = pl.ds(pl.multiple_of((1 - core) * half, half), half)
    keys, values = refs.keys, refs.values
    blocks = length // QB

    def pair_lanes(p):
        return pl.ds(pl.multiple_of(p * PAIR, PAIR), PAIR)

    def att_copy(p):
        lanes = pair_lanes(p)
        return att_share.copy(att.at[there, lanes], refs.att_other.at[:, lanes], p)

    def pair(p, x):
        lanes = pl.ds(pl.multiple_of(p * PAIR, PAIR), PAIR)
        keys[0:SLOTS, :] = pre[0, :, lanes]
        keys[SLOTS:, :] = k[:, lanes]
        values[0:SLOTS, :] = pre[1, :, lanes]
        values[SLOTS:, :] = v[:, lanes]

        def block(b, x):
            rows = pl.ds(pl.multiple_of(b * QB, QB), QB)
            mixed, totals = attend_block(
                q[rows, lanes], keys[...], values[...],
                refs.meta_cols[pl.ds(pl.multiple_of(SLOTS + b * QB, SLOTS), QB), 0:1],
                meta[0:1, SLOTS:], meta[0:1, :SLOTS],
            )
            att[rows, lanes] = mixed
            lse[p, :, rows] = jnp.transpose(totals)[0:8, :]
            return x

        lax.fori_loop(0, blocks // 2, block, 0)
        beat(done + ATT_BEATS * p)
        lax.fori_loop(blocks // 2, blocks, block, 0)
        if ATT_BEATS > 1:
            beat(done + ATT_BEATS * p + 1)
        att_copy(p).start()
        return x

    pairs = WIDE // PAIR
    lax.fori_loop(0, pairs, pair, 0)
    done = done + ATT_BEATS * pairs
    for p in range(pairs):
        att_copy(p).wait_recv()

    done = ready(3 * plan.sides, plan.sides, done)
    normal_one, rstd_one, normed, acc = refs.normal_one, refs.rstd_one, refs.normed, refs.acc
    low, slope, out = refs.low, refs.slope, refs.out
    parts = half // CHUNK

    def weight(kind, side):
        return whole[kind, side].reshape(width, WIDE)

    def mix(b, x):
        rows = pl.ds(pl.multiple_of(b * CHUNK, CHUNK), CHUNK)
        own = att[pl.ds(pl.multiple_of(core * half + b * CHUNK, CHUNK), CHUNK), :]
        total = row[2 * core + b].reshape(CHUNK, width).astype(f32)
        total = total + mm_nt(own, weight(3, core)) + mm_nt(refs.att_other[rows, :], weight(3, 1 - core))
        normal, rstd = normalise(total)
        normal_one[rows, :] = normal
        rstd_one[rows, :] = jnp.broadcast_to(rstd, (CHUNK, LANES))
        low_normed = (normal * refs.gain_one[...] + refs.shift_one[...]).astype(bf16)
        normed[rows, :] = low_normed
        acc[rows, :] = low_normed.astype(f32)
        beat(done + b)
        return x

    lax.fori_loop(0, parts, mix, 0)
    done = done + parts

    acted = refs.acted
    chunks = [slice(b * CHUNK, (b + 1) * CHUNK) for b in range(parts)]

    def act(j, done):
        def unit(side, x):
            for rows in chunks:
                upper = mm(normed[rows, :], weight(up_kind(j), side))
                bell = (1.0 + lax.erf(upper * (0.5**0.5))) * 0.5
                acted[2 * j + side, rows, :] = (upper * bell).astype(bf16)
                slope[2 * j + side, rows, :] = (
                    bell + upper * jnp.exp(upper * upper * -0.5) * (1.0 / (2.0 * math.pi) ** 0.5)
                ).astype(bf16)
            if done < last:
                beat(done + side)
            return x

        lax.fori_loop(0, 2, unit, 0)

    def add(j, done):
        def unit(side, x):
            for rows in chunks:
                acc[rows, :] += mm_nt(acted[2 * j + side, rows, :], weight(down_kind(j), side))
            return x

        lax.fori_loop(0, 2, unit, 0)

    steps_of = sorted([(up_kind(j), act, j) for j in range(GROUPS)] + [(down_kind(j), add, j) for j in range(GROUPS)], key=lambda s: s[0])
    for kind, body, j in steps_of:
        done = ready(kind * plan.sides, plan.sides, done)
        body(j, done)
        done = done + 2 if body is act else done

    grad_line.settle()
    for part in range(2):
        for side in range(plan.cores):
            grad_line.receive(grad.at[part, side], 2 * core + part, side if spread else line // 2)

    def close(b, x):
        rows = pl.ds(pl.multiple_of(b * CHUNK, CHUNK), CHUNK)
        normal, rstd = normalise(acc[rows, :])
        out[rows, :] = (normal * refs.gain_two[...] + refs.shift_two[...]).astype(bf16)
        d_second = normalise_grad(
            normal, rstd, refs.gain_two[...], grad[b].reshape(CHUNK, width).astype(f32)
        )
        acc[rows, :] = d_second
        low[rows, :] = d_second.astype(bf16)
        return x

    lax.fori_loop(0, parts, close, 0)
    places = tokens.shape[1]
    out_back = Line(plan, place, sems.out_send, sems.out_recv)
    for b in range(2):
        for side in range(plan.cores):
            spot, target = (line, side) if spread else (lax.rem(line, 2), line // 2)
            out_back.send(
                out.at[pl.ds((b * plan.cores + side) * places, places)], refs.pieces.at[spot],
                2 * core + b, target,
            )

    def feed_back(n, x):
        j, side = n // 2, lax.rem(n, 2)
        for rows in chunks:
            d_acted = mm(low[rows, :], weight(down_kind(j), side))
            d_upper = (d_acted * slope[n, rows, :].astype(f32)).astype(bf16)
            acc[rows, :] += mm_nt(d_upper, weight(up_kind(j), side))
        return x

    lax.fori_loop(0, 2 * GROUPS, feed_back, 0)

    d_att, away = refs.d_att, refs.d_att_away
    d_share = Sibling(plan, place, sems.d_send, sems.d_recv)

    def d_copy(b):
        mine = pl.ds(pl.multiple_of(core * half + b * CHUNK, CHUNK), CHUNK)
        return d_share.copy(away.at[pl.ds(pl.multiple_of(b * CHUNK, CHUNK), CHUNK)], d_att.at[mine], b)

    def open_(b, x):
        rows = pl.ds(pl.multiple_of(b * CHUNK, CHUNK), CHUNK)
        d_first = normalise_grad(normal_one[rows, :], rstd_one[rows, 0:1], refs.gain_one[...], acc[rows, :])
        acc[rows, :] = d_first
        d_low = d_first.astype(bf16)
        away[rows, :] = mm(d_low, weight(3, 1 - core)).astype(bf16)
        d_copy(b).start()
        mine = pl.ds(pl.multiple_of(core * half + b * CHUNK, CHUNK), CHUNK)
        d_att[mine, :] = mm(d_low, weight(3, core)).astype(bf16)
        return x

    lax.fori_loop(0, parts, open_, 0)
    for b in range(parts):
        d_copy(b).wait_recv()

    def pair_inner(p, x):
        lanes = pair_lanes(p)
        lse[p, 2:4, :] = inner_rows(d_att[:, lanes], att[:, lanes])[0:2]
        return x

    lax.fori_loop(0, pairs, pair_inner, 0)
    columns, dq_acc = refs.meta_cols, normal_one
    d_queries, d_keys, d_values = (
        acted.at[pl.ds(n * length // half, length // half)] for n in range(3)
    )
    d_pre = refs.d_pre

    def prefix_pair(p, x):
        lanes = pair_lanes(p)
        live = columns[0:SLOTS, 0:1] > 0.5
        a, g, dq = gradient_tile(pre[0, :, lanes], pre[1, :, lanes], q[:, lanes], d_att[:, lanes], lse[p], live)
        d_pre[0, :, lanes] = a
        d_pre[1, :, lanes] = g
        dq_acc[lanes, :] = dq
        return x

    lax.fori_loop(0, pairs, prefix_pair, 0)
    prefix_sum = PrefixSum(plan, place, refs)
    prefix_sum.start()

    def key_block(kb, first, count):
        rows = pl.ds(pl.multiple_of(kb * KB, KB), KB)
        span = pl.ds(pl.multiple_of(first * KB, KB), count * KB)
        seg_k = columns[pl.ds(pl.multiple_of(SLOTS + kb * KB, SLOTS), KB), 0:1]
        part, at = kb * KB // half, pl.ds(pl.multiple_of(lax.rem(kb * KB, half), KB), KB)

        def one(p, x):
            lanes = pair_lanes(p)
            allowed = seg_k == meta[0:1, pl.ds(pl.multiple_of(SLOTS + first * KB, SLOTS), count * KB)]
            a, g, dq = gradient_tile(
                k[rows, lanes], v[rows, lanes], q[span, lanes], d_att[span, lanes], lse[p, :, span], allowed
            )
            d_keys[part, at, lanes] = a.astype(bf16)
            d_values[part, at, lanes] = g.astype(bf16)
            dq_acc[lanes, span] += dq
            return x

        lax.fori_loop(0, pairs, one, 0)

    swap = Sibling(plan, place, sems.swap_send, sems.swap_recv)
    spare = row
    own_blocks = half // KB
    for chip in range(LINE):
        if spread:
            share.copy(row.at[chip, core], row.at[chip, core], chip).wait_send()
        else:
            pl.when(holds)(share.copy(row.at[chip, 0], row.at[chip, 0], chip).wait_send)

    def swap_copy(i):
        return swap.copy(spare.at[i], spare.at[own_blocks + i], i)

    def grad_pieces(i):
        for side in range(plan.cores):
            spot, target = (line, side) if spread else (lax.rem(line, 2), line // 2)
            chip = own_blocks * core + i
            src = low.at[pl.ds(pl.multiple_of(i * KB + side * places, places), places)]
            dst = refs.grad_pieces.at[spot]
            stays = (chip == line) & (target == core)
            sem = sems.back_send.at[i, side]
            yield stays, remote(
                src, dst, sem, sems.back_recv.at[line, core], plan.device(coords, chip, target)
            ), pltpu.make_async_copy(src, dst, sem)

    def give(b):
        rows = pl.ds(pl.multiple_of(lax.rem(b * KB, half), KB), KB)
        part = b * KB // half
        span = pl.ds(pl.multiple_of(b * KB, KB), KB)
        i = lax.rem(b, own_blocks)
        d_queries[part, rows, :] = (jnp.transpose(dq_acc[:, span]) * 0.125).astype(bf16)
        term = mm_nt(d_queries[part, rows, :], weight(0, core))
        term = term + mm_nt(d_keys[part, rows, :], weight(1, core))
        term = term + mm_nt(d_values[part, rows, :], weight(2, core))
        owner = b // own_blocks

        @pl.when(core != owner)
        def _():
            spare[i] = term.astype(bf16).reshape(spare.shape[1:])
            swap_copy(i).start()

        @pl.when(core == owner)
        def _():
            own = term + acc[rows, :]
            swap_copy(i).wait_recv()
            low[rows, :] = (own + spare[own_blocks + i].reshape(KB, width).astype(f32)).astype(bf16)
            for stays, far, near in grad_pieces(i):
                pl.when(jnp.logical_not(stays))(far.start)
                pl.when(stays)(near.start)

    blocks = length // KB
    near_blocks = -(-(REACH - 1) // KB)
    turned = line < LINE // 2
    given = 0
    for o in range(blocks):
        first, final = max(0, o - near_blocks), min(blocks - 1, o + near_blocks)
        key_block(
            jnp.where(turned, blocks - 1 - o, o), jnp.where(turned, blocks - 1 - final, first), final - first + 1
        )
        prefix_sum.go_on(o)
        while given < blocks and min(blocks - 1, given + near_blocks) <= o:
            give(jnp.where(turned, blocks - 1 - given, given))
            given = given + 1
    prefix_sum.finish(blocks)

    lax.fori_loop(0, gather.count, lambda i, x: (gather.drain(i), x)[1], 0)
    token_line.drain()
    prefix_line.drain()
    grad_line.drain()
    if not spread:
        pl.when(holds)(meta_copy.wait_send)
    for p in range(pairs):
        att_copy(p).wait_send()
    for b in range(parts):
        d_copy(b).wait_send()
    for i in range(own_blocks):
        swap_copy(i).wait_send()
        for stays, far, near in grad_pieces(i):
            pl.when(jnp.logical_not(stays))(far.wait_send)
            pl.when(stays)(near.wait)
    out_back.settle()
    arrivals = Line(plan, place, sems.back_send, sems.back_recv)
    for j in range(held):
        chip = j if spread else 2 * core + j
        out_back.receive(refs.pieces.at[j], chip, line // 2)
        arrivals.receive(refs.grad_pieces.at[j], chip, line // 2)
    out_back.drain()


def forward_backward(plan, given):
    held, places, width = given.tokens.shape
    depth = given.w_query.shape[0]
    length = places * plan.tp
    half = length // 2
    pairs = WIDE // PAIR
    bf16, f32 = jnp.bfloat16, jnp.float32
    S = jax.ShapeDtypeStruct
    tasks, slots, part = given.prefix_keys.shape
    kept = -(-slots // 16) * 16
    steps = len(plan.axes)
    reach = max(plan.shape[a] for a in plan.axes) - 1
    outs = dict(
        pieces=S((held, places, width), bf16),
        grad_pieces=S((held, places, width), bf16),
        keys_grad=S((tasks, slots, part), f32),
        values_grad=S((tasks, slots, part), f32),
    )
    scratch = dict(
        source=((KINDS, plan.sides, depth, LANES), bf16),
        prefix=((held, plan.sides, 2, SLOTS, LANES), bf16),
        meta=((8, SLOTS + length), f32),
        whole=((KINDS, 2) + plan.shape + (depth, WIDE), bf16),
        row=((LINE, plan.cores, places, width), bf16),
        grad=((2, plan.cores, places, width), bf16),
        pre=((2, SLOTS, WIDE), bf16),
        q=((length, WIDE), bf16),
        k=((length, WIDE), bf16),
        v=((length, WIDE), bf16),
        att=((length, WIDE), bf16),
        lse=((pairs, 8, length), f32),
        att_other=((half, WIDE), bf16),
        keys=((SLOTS + length, PAIR), bf16),
        values=((SLOTS + length, PAIR), bf16),
        meta_cols=((SLOTS + length, 8), f32),
        normal_one=((half, width), f32),
        rstd_one=((half, LANES), f32),
        normed=((half, width), bf16),
        slope=((2 * GROUPS, half, WIDE), bf16),
        acted=((2 * GROUPS, half, WIDE), bf16),
        acc=((half, width), f32),
        low=((half, width), bf16),
        out=((half, width), bf16),
        d_att=((length, WIDE), bf16),
        d_att_away=((half, WIDE), bf16),
        d_pre=((2, SLOTS, WIDE), f32),
        terms=((LINE, 2, SLOTS, LANES), bf16),
        row_terms=((LINE, 2, SLOTS, LANES), bf16),
        total=((tasks, 2, kept, LANES), f32),
        total_other=((tasks, 2, kept, LANES), f32),
        gone=((steps, tasks, 2, kept, LANES), bf16),
        come=((steps, reach, tasks, 2, kept, LANES), bf16),
    )
    sems = gather_semaphores(plan)
    sems.update(
        token_send=semaphores(held),
        token_recv=semaphores(LINE, 2),
        prefix_send=semaphores(held * plan.sides),
        prefix_recv=semaphores(LINE, 2),
        grad_send=semaphores(held),
        grad_recv=semaphores(LINE, 2),
        share_send=semaphores(5),
        share_recv=semaphores(5),
        att_send=semaphores(pairs),
        att_recv=semaphores(pairs),
        d_send=semaphores(half // CHUNK),
        d_recv=semaphores(half // CHUNK),
        out_send=semaphores(4),
        out_recv=semaphores(LINE, 2),
        back_send=semaphores(half // KB, 2),
        back_recv=semaphores(LINE, 2),
        swap_send=semaphores(half // KB),
        swap_recv=semaphores(half // KB),
        terms_send=semaphores(LINE),
        terms_recv=semaphores(LINE, 2),
        total_send=semaphores(1),
        total_recv=semaphores(1),
        sum_send=semaphores(steps, reach),
        sum_recv=semaphores(steps, reach),
    )
    smem = pl.BlockSpec(memory_space=pltpu.SMEM)
    vmem = pl.BlockSpec(memory_space=pltpu.VMEM)
    hbm = pl.BlockSpec(memory_space=pl.ANY)
    results = pl.pallas_call(
        functools.partial(forward_backward_kernel, plan, (*vars(given), *outs, *scratch, *sems)),
        out_shape=list(outs.values()),
        in_specs=[smem, smem, smem, vmem, hbm, hbm] + [vmem] * 12,
        out_specs=[hbm, hbm, vmem, vmem],
        scratch_shapes=[pltpu.VMEM(*spec) for spec in scratch.values()] + list(sems.values()),
        compiler_params=pltpu.CompilerParams(
            collective_id=0, has_side_effects=True, vmem_limit_bytes=63 * 2**20
        ),
    )(*vars(given).values())
    return SimpleNamespace(**dict(zip(outs, results)))


def shards(
    plan, tokens, w_query, w_key, w_value, w_attn_out, w_up, w_down, first_gain, first_shift,
    second_gain, second_shift, prefix_keys, prefix_values, example_lengths, task_ids, prefix_lens,
    slot_masks, out_grad,
):
    done = forward_backward(
        plan,
        SimpleNamespace(
            task_ids=task_ids,
            lengths=example_lengths,
            prefix_lens=prefix_lens,
            slot_masks=slot_masks,
            tokens=tokens,
            out_grad=out_grad,
            w_query=w_query,
            w_key=w_key,
            w_value=w_value,
            w_attn_out=w_attn_out,
            w_up=w_up,
            w_down=w_down,
            gain_one=first_gain[None],
            shift_one=first_shift[None],
            gain_two=second_gain[None],
            shift_two=second_shift[None],
            prefix_keys=prefix_keys,
            prefix_values=prefix_values,
        ),
    )
    return done.pieces, done.grad_pieces.astype(jnp.float32), done.keys_grad, done.values_grad


def solution(mesh):
    placed = (
        P("rows", "tp", None),
        P("rows", "tp"),
        P("rows", "tp"),
        P("rows", "tp"),
        P("tp", "rows"),
        P("rows", "tp"),
        P("tp", "rows"),
        P(),
        P(),
        P(),
        P(),
        P(None, None, "tp"),
        P(None, None, "tp"),
        P("rows", None),
        P("rows"),
        P(),
        P(),
        P("rows", "tp", None),
    )
    plan = Plan(mesh.shape["rows"], mesh.shape["tp"])
    return jax.shard_map(
        functools.partial(shards, plan),
        mesh=mesh,
        in_specs=placed,
        out_specs=(
            P("rows", "tp", None),
            P("rows", "tp", None),
            P(None, None, "tp"),
            P(None, None, "tp"),
        ),
        check_vma=False,
    )
```

```python
import functools
import math
from types import SimpleNamespace

import jax
import jax.numpy as jnp
from jax import lax
from jax.experimental import pallas as pl
from jax.experimental.pallas import tpu as pltpu
from jax.sharding import PartitionSpec as P

HD = 64
PAIR = 2 * HD
SLOTS = 128
QB = 256
KB = 256
REACH = 512
NEG = -1e30
MARKS = 16
NT = (((1,), (1,)), ((), ()))


def mm(a, b):
    return jnp.dot(a, b, preferred_element_type=jnp.float32)


def mm_nt(a, b):
    return lax.dot_general(a, b, NT, preferred_element_type=jnp.float32)


def head_lanes(half):
    lane = lax.broadcasted_iota(jnp.int32, (1, PAIR), 1)
    return (lane >= half * HD) & (lane < (half + 1) * HD)


def only_head(a, half):
    return jnp.where(head_lanes(half), a, jnp.zeros_like(a))


def key_marks(meta):
    length = meta.shape[1]
    row = lax.broadcasted_iota(jnp.int32, (PAIR, length), 0)
    place = lax.broadcasted_iota(jnp.int32, (PAIR, length), 1)
    seg = meta[0:1, :]
    other = (place >= SLOTS) & (row < 8) & (row.astype(jnp.float32) != seg)
    dead = (place < SLOTS) & (row == 8) & (seg < 0.5)
    ones = (row >= 9) & (row < 12)
    marks = jnp.where(other | dead, NEG, jnp.where(ones, 1.0, 0.0))
    return jnp.transpose(marks).astype(jnp.bfloat16)


def query_marks(meta):
    length = meta.shape[1] - SLOTS
    row = lax.broadcasted_iota(jnp.int32, (MARKS, length), 0)
    seg = meta[0:1, SLOTS:]
    return jnp.where(((row < 8) & (row.astype(jnp.float32) == seg)) | (row == 8), 1.0, 0.0)


def attend_tile(q_t, marks, keys, values):
    scaled = q_t * jnp.asarray(0.125, jnp.bfloat16)
    blank = jnp.zeros((PAIR - MARKS, marks.shape[1]), jnp.bfloat16)
    low_marks = jnp.concatenate([marks.astype(jnp.bfloat16), blank], axis=0)
    mixed, totals = [], []
    zero = jnp.zeros((HD, q_t.shape[1]), jnp.bfloat16)
    ones = jnp.ones((16, keys.shape[0]), jnp.bfloat16)
    for half in range(2):
        rows = slice(half * HD, (half + 1) * HD)
        own = [scaled[rows, :], zero] if half == 0 else [zero, scaled[rows, :]]
        scores = mm(keys, jnp.concatenate([*own, low_marks], axis=0))
        top = jnp.max(scores, axis=0, keepdims=True)
        probs = jnp.exp(scores - top).astype(jnp.bfloat16)
        out = mm(jnp.concatenate([values[rows, :], ones], axis=0), probs)
        total = out[HD : HD + 1, :]
        mixed.append(out[:HD, :] * (1.0 / total))
        totals.append(top + jnp.log(total))
    return jnp.concatenate(mixed, axis=0), totals


def inner_rows(do, att):
    picks = lax.broadcasted_iota(jnp.int32, (8, PAIR), 0)
    lanes = lax.broadcasted_iota(jnp.int32, (8, PAIR), 1) // HD
    picker = jnp.where(picks == lanes, 1.0, 0.0).astype(jnp.bfloat16)
    prod = do.astype(jnp.float32) * att.astype(jnp.float32)
    high = prod.astype(jnp.bfloat16)
    return mm_nt(picker, high) + mm_nt(picker, (prod - high.astype(jnp.float32)).astype(jnp.bfloat16))


def gradient_tile(keys, values, q, do, rows, allowed):
    back = jnp.transpose(keys)
    d_keys = jnp.zeros(keys.shape, jnp.float32)
    d_values = jnp.zeros(keys.shape, jnp.float32)
    d_query = []
    scaled = q * jnp.asarray(0.125, jnp.bfloat16)
    for half in range(2):
        qh, dh = only_head(scaled, half), only_head(do, half)
        scores = jnp.where(allowed, mm_nt(keys, qh), NEG)
        probs = jnp.exp(scores - rows[half : half + 1, :])
        d_scores = (probs * (mm_nt(values, dh) - rows[2 + half : 3 + half, :])).astype(jnp.bfloat16)
        d_keys = d_keys + mm(d_scores, qh)
        d_values = d_values + mm(probs.astype(jnp.bfloat16), dh)
        d_query.append(mm(back[half * HD : (half + 1) * HD, :], d_scores))
    return d_keys, d_values, jnp.concatenate(d_query, axis=0)


MESH = pl.DeviceIdType.MESH
LINE = 4
LANES = 128
WIDE = LINE * LANES
KINDS = 12
FIRST_UP = 4
GROUPS = (KINDS - FIRST_UP) // 2
CHUNK = 256


class Plan:
    def __init__(self, rows, tp):
        self.rows = rows
        self.tp = tp
        self.core_in_tp = tp > LINE
        self.shape = (rows // 8, 2, 4) if self.core_in_tp else (rows // 4, 2, 2)
        self.axes = (0, 1, 2) if self.core_in_tp else (0, 1)
        self.cores = 2 if self.core_in_tp else 1
        self.sides = 2 // self.cores

    def here(self):
        r = lax.axis_index("rows")
        t = lax.axis_index("tp")
        a, b, c = self.shape
        coords = (r // (b * c), lax.rem(r // c, b), lax.rem(r, c))
        if self.core_in_tp:
            return coords, t // 2, lax.rem(t, 2)
        return coords, t, coords[2]

    def device(self, coords, line, core):
        a, b, c = self.shape
        if self.core_in_tp:
            return ((coords[0] * b + coords[1]) * c + coords[2], line * 2 + core)
        return ((coords[0] * b + coords[1]) * c + core, line)

    def row_core(self, chip):
        return None if self.core_in_tp else chip // 2


def shifted(coords, axis, by, size):
    moved = list(coords)
    moved[axis] = lax.rem(coords[axis] + by, size)
    return tuple(moved)


def sibling(plan, place):
    coords, line, core = place
    return plan.device(coords, line, 1 - core)


def greet(plan, place):
    coords, line, core = place
    others = [
        plan.device(coords, lax.rem(line + by, LINE), side) for by in range(1, LINE) for side in range(2)
    ]
    others.append(sibling(plan, place))
    for axis in plan.axes:
        for by in range(1, plan.shape[axis]):
            others.append(plan.device(shifted(coords, axis, by, plan.shape[axis]), line, core))
    barrier = pltpu.get_barrier_semaphore()
    for other in others:
        pl.semaphore_signal(barrier, inc=1, device_id=other, device_id_type=MESH)
    pl.semaphore_wait(barrier, len(others))


def remote(src, dst, send, recv, device):
    return pltpu.make_async_remote_copy(
        src_ref=src, dst_ref=dst, send_sem=send, recv_sem=recv, device_id=device, device_id_type=MESH
    )


class Gather:
    def __init__(self, plan, place, source, whole, sems):
        self.plan = plan
        self.place = place
        self.coords, self.line, self.core = place
        self.source = source
        self.whole = whole
        self.sems = sems
        self.count = KINDS * plan.sides
        self.depth = source.shape[-2]
        self.orders = (plan.axes, plan.axes[::-1])
        self.lanes = pl.ds(pl.multiple_of(self.line * LANES, LANES), LANES)

    def unit(self, i):
        if self.plan.core_in_tp:
            return (i, self.core)
        return (i // 2, lax.rem(i, 2))

    def own_copies(self):
        where = tuple(self.coords) + (slice(None), self.lanes)
        for at in range(self.plan.sides):
            side = self.core if self.plan.core_in_tp else at
            yield pltpu.make_async_copy(
                self.source.at[:, at], self.whole.at[(slice(None), side) + where], self.sems.own.at[at]
            )

    def block(self, i, chip):
        lanes = pl.ds(pl.multiple_of(chip * LANES, LANES), LANES)
        return self.whole.at[self.unit(i) + tuple(self.coords) + (slice(None), lanes)]

    def line_copies(self, i):
        src = self.source.at[(i, 0) if self.plan.core_in_tp else self.unit(i)]
        for at, by in enumerate((1, -1, 2, -2)):
            chip = self.line + by
            there = (chip >= 0) & (chip < LINE)
            yield there, remote(
                src, self.block(i, self.line), self.sems.line_send.at[i, at], self.sems.line_recv.at[i, self.line],
                self.plan.device(self.coords, jnp.clip(chip, 0, LINE - 1), self.core),
            )

    def pass_copies(self, i):
        for middle, first, target in ((2, 0, 3), (1, 3, 0)):
            block = self.block(i, first)
            yield self.line == middle, remote(
                block, block, self.sems.line_send.at[i, 4], self.sems.line_recv.at[i, first],
                self.plan.device(self.coords, target, self.core),
            )

    def line_arrived(self, i, chip):
        block = self.block(i, chip)
        remote(
            block, block, self.sems.line_send.at[i, 0], self.sems.line_recv.at[i, chip],
            self.plan.device(self.coords, chip, self.core),
        ).wait_recv()

    def axis_copies(self, i, step):
        rows = self.depth // 2
        for half in range(2):
            order = self.orders[half]
            axis = order[step]
            size = self.plan.shape[axis]
            index = [
                pl.ds(0, self.plan.shape[a]) if a in order[:step] else self.coords[a] for a in range(3)
            ]
            block = self.whole.at[self.unit(i) + tuple(index) + (pl.ds(half * rows, rows),)]
            for by in range(1, size):
                spot = (i, half, step, by - 1)
                yield remote(
                    block, block, self.sems.axis_send.at[spot], self.sems.axis_recv.at[spot],
                    self.plan.device(shifted(self.coords, axis, by, size), self.line, self.core),
                )

    def core_copy(self, i, side):
        if self.plan.core_in_tp:
            block = self.whole.at[i, side]
        else:
            block = self.whole.at[self.unit(i) + (slice(None), slice(None), side)]
        return remote(
            block, block, self.sems.core_send.at[i], self.sems.core_recv.at[i], sibling(self.plan, self.place)
        )

    def core_roles(self, i):
        if self.plan.core_in_tp:
            wide = i >= 3
            return wide, wide
        side = lax.rem(i, 2)
        wide = i >= 6
        return wide | (side != self.core), wide | (side == self.core)

    def start_line(self, i):
        for there, copy in self.line_copies(i):
            pl.when(there)(copy.start)

    def pass_on(self, i):
        for (here, copy), first in zip(self.pass_copies(i), (0, 3)):

            @pl.when(here)
            def _(copy=copy, first=first):
                self.line_arrived(i, first)
                copy.start()

    def start_axis(self, i, step):
        if step == 0:
            for chip in range(LINE):
                passed = ((chip == 0) & (self.line == 2)) | ((chip == 3) & (self.line == 1))
                pl.when((self.line != chip) & jnp.logical_not(passed))(functools.partial(self.line_arrived, i, chip))
        else:
            for copy in self.axis_copies(i, step - 1):
                copy.wait_recv()
        for copy in self.axis_copies(i, step):
            copy.start()

    def start_core(self, i):
        for copy in self.axis_copies(i, len(self.plan.axes) - 1):
            copy.wait_recv()
        sends, _ = self.core_roles(i)
        pl.when(sends)(lambda: self.core_copy(i, self.core).start())

    def finish(self, i):
        _, gets = self.core_roles(i)
        pl.when(gets)(lambda: self.core_copy(i, 1 - self.core).wait_recv())

    def drain(self, i):
        for there, copy in (*self.line_copies(i), *self.pass_copies(i)):
            pl.when(there)(copy.wait_send)
        for step in range(len(self.plan.axes)):
            for copy in self.axis_copies(i, step):
                copy.wait_send()
        sends, _ = self.core_roles(i)
        pl.when(sends)(lambda: self.core_copy(i, self.core).wait_send())

    def tick(self, i, ahead, lag):
        steps = len(self.plan.axes)

        def guarded(at, body):
            pl.when((at >= 0) & (at < self.count))(functools.partial(body, at))

        guarded(i + ahead, self.start_line)
        guarded(i + 1, self.pass_on)
        for step in range(steps):
            guarded(i - lag * step, lambda at, step=step: self.start_axis(at, step))
        guarded(i - lag * steps, self.start_core)

    def ticks(self, lag):
        return self.count + lag * len(self.plan.axes)


def semaphores(*shape):
    return pltpu.SemaphoreType.DMA(shape)


def gather_semaphores(plan):
    count = KINDS * plan.sides
    steps = len(plan.axes)
    reach = max(plan.shape[a] for a in plan.axes) - 1
    return dict(
        line_send=semaphores(count, 5),
        line_recv=semaphores(count, LINE),
        axis_send=semaphores(count, 2, steps, reach),
        axis_recv=semaphores(count, 2, steps, reach),
        core_send=semaphores(count),
        core_recv=semaphores(count),
        own=semaphores(2),
    )


class Line:
    def __init__(self, plan, place, send_sems, recv_sems):
        self.plan = plan
        self.coords, self.line, self.core = place
        self.send_sems = send_sems
        self.recv_sems = recv_sems
        self.pieces = []

    def here(self, chip, side):
        return (chip == self.line) & (side == self.core)

    def add(self, src, dst, chip, side):
        at = len(self.pieces)
        device = self.plan.device(self.coords, chip, side)

        def far(src, dst):
            return remote(src, dst, self.send_sems.at[at], self.recv_sems.at[self.line, self.core], device)

        near = pltpu.make_async_copy(src, dst, self.send_sems.at[at])
        self.pieces.append((self.here(chip, side), src, dst, far, near))

    def start(self, part=0, parts=1):
        for stays, src, dst, far, near in self.pieces:
            rows = src.shape[0] // parts
            cut = pl.ds(pl.multiple_of(part * rows, rows), rows) if parts > 1 else slice(None)
            pl.when(jnp.logical_not(stays))(far(src.at[cut], dst.at[cut]).start)
            pl.when(stays & (part == 0))(near.start)

    def send(self, src, dst, chip, side):
        self.add(src, dst, chip, side)
        stays, src, dst, far, near = self.pieces[-1]
        pl.when(jnp.logical_not(stays))(far(src, dst).start)
        pl.when(stays)(near.start)

    def settle(self):
        for stays, *_, near in self.pieces:
            pl.when(stays)(near.wait)

    def drain(self):
        for stays, src, dst, far, _ in self.pieces:
            pl.when(jnp.logical_not(stays))(far(src, dst).wait_send)

    def receive(self, dst, chip, side):
        copy = remote(
            dst, dst, self.send_sems.at[0], self.recv_sems.at[chip, side],
            self.plan.device(self.coords, chip, side),
        )
        pl.when(jnp.logical_not(self.here(chip, side)))(copy.wait_recv)


class Sibling:
    def __init__(self, plan, place, send_sems, recv_sems):
        self.send_sems = send_sems
        self.recv_sems = recv_sems
        self.device = sibling(plan, place)

    def copy(self, src, dst, at):
        return remote(src, dst, self.send_sems.at[at], self.recv_sems.at[at], self.device)


class PrefixSum:
    def __init__(self, plan, place, refs):
        self.plan = plan
        self.place = place
        self.refs = refs
        self.coords, self.line, self.core = place
        self.terms = Line(plan, place, refs.terms_send, refs.terms_recv)
        self.last = Sibling(plan, place, refs.total_send, refs.total_recv)

    def start(self):
        refs = self.refs
        for chip in range(LINE):
            lanes = slice(chip * LANES, (chip + 1) * LANES)
            for which in range(2):
                refs.terms[chip, which] = refs.d_pre[which, :, lanes].astype(jnp.bfloat16)
            refs.terms[chip, 0, SLOTS - 16 :, :] = jnp.broadcast_to(refs.meta[1:2, 0:SLOTS], (16, SLOTS)).astype(
                jnp.bfloat16
            )
        for chip in range(LINE):
            self.terms.send(refs.terms.at[chip], refs.row_terms.at[self.line], chip, self.core)

    def copies(self, step):
        refs = self.refs
        axis = self.plan.axes[step]
        size = self.plan.shape[axis]
        return [
            remote(
                refs.gone.at[step], refs.come.at[step, by - 1], refs.sum_send.at[step, by - 1],
                refs.sum_recv.at[step, by - 1],
                self.plan.device(shifted(self.coords, axis, by, size), self.line, self.core),
            )
            for by in range(1, size)
        ]

    def send(self, step):
        self.refs.gone[step] = self.refs.total[...].astype(jnp.bfloat16)
        for copy in self.copies(step):
            copy.start()

    def line_sum(self):
        refs = self.refs
        total = refs.total
        tasks, _, kept = total.shape[:3]
        self.terms.settle()
        for chip in range(LINE):
            self.terms.receive(refs.row_terms.at[chip], chip, self.core)
            marks = refs.row_terms[chip, 0, SLOTS - 16 :, :].astype(jnp.float32)
            for task in range(tasks):
                for which in range(2):
                    more = refs.row_terms[chip, which, 0:kept, :].astype(jnp.float32) * marks[0:1, task : task + 1]
                    total[task, which] = more if chip == 0 else total[task, which] + more

    def receive(self, step):
        for by, copy in enumerate(self.copies(step)):
            copy.wait_recv()
            self.refs.total[...] += self.refs.come[step, by].astype(jnp.float32)

    def go_on(self, beat):
        steps = len(self.plan.axes)
        if beat == 0:
            self.line_sum()
        elif beat <= steps:
            self.receive(beat - 1)
        if beat < steps:
            self.send(beat)
        elif beat == steps and not self.plan.core_in_tp:
            self.last.copy(self.refs.total, self.refs.total_other, 0).start()

    def put(self, block, lanes):
        refs = self.refs
        tasks, slots = refs.keys_grad.shape[:2]
        for task in range(tasks):
            refs.keys_grad[task, :, lanes] = block[task, 0, 0:slots, :]
            refs.values_grad[task, :, lanes] = block[task, 1, 0:slots, :]

    def finish(self, beats):
        refs = self.refs
        steps = len(self.plan.axes)
        for beat in range(beats, steps + 1):
            self.go_on(beat)
        if self.plan.core_in_tp:
            self.put(refs.total, slice(None))
        else:
            self.last.copy(refs.total, refs.total_other, 0).wait_recv()
            sides = slice(0, LANES), slice(LANES, 2 * LANES)
            for side in range(2):

                @pl.when(self.core == side)
                def _(side=side):
                    self.put(refs.total, sides[side])
                    self.put(refs.total_other, sides[1 - side])

            self.last.copy(refs.total, refs.total_other, 0).wait_send()
        self.terms.drain()
        for step in range(steps):
            for copy in self.copies(step):
                copy.wait_send()


def normalise(z):
    mean = jnp.mean(z, axis=1, keepdims=True)
    centred = z - mean
    rstd = lax.rsqrt(jnp.mean(centred * centred, axis=1, keepdims=True) + 1e-05)
    return centred * rstd, rstd


def normalise_grad(normal, rstd, gain, grad):
    g = grad * gain
    return rstd * (
        g - jnp.mean(g, axis=1, keepdims=True) - normal * jnp.mean(g * normal, axis=1, keepdims=True)
    )


def up_kind(j):
    return FIRST_UP + j + jnp.maximum(j - 1, 0) if not isinstance(j, int) else FIRST_UP + j + max(j - 1, 0)


def down_kind(j):
    return jnp.minimum(FIRST_UP + 2 + 2 * j, KINDS - 1) if not isinstance(j, int) else min(FIRST_UP + 2 + 2 * j, KINDS - 1)


def forward_inputs(plan, place, refs, scratch):
    coords, line, core = place
    source, prefix, meta = scratch.source, scratch.prefix, scratch.meta
    sides = plan.sides

    def put(kind, block, first):
        for side in range(sides):
            at = (first + side) * LANES
            source[kind, side] = block[:, at : at + LANES]

    put(0, refs.w_query, 0)
    put(1, refs.w_key, 0)
    put(2, refs.w_value, 0)
    put(3, jnp.transpose(refs.w_attn_out[...]), 0)
    down = jnp.transpose(refs.w_down[...])
    for j in range(GROUPS):
        put(up_kind(j), refs.w_up, j * sides)
        put(down_kind(j), down, j * sides)

    slots = refs.prefix_keys.shape[1]
    prefix[...] = jnp.zeros_like(prefix)
    for j in range(refs.tokens.shape[0]):
        task = refs.task_ids[j]
        for which, table in enumerate((refs.prefix_keys, refs.prefix_values)):
            rows = table[task]
            for side in range(sides):
                prefix[j, side, which, 0:slots, :] = rows[:, side * LANES : (side + 1) * LANES]

    mine = line if plan.core_in_tp else lax.rem(line, 2)
    task = refs.task_ids[mine]
    meta[...] = jnp.zeros_like(meta)
    length = meta.shape[1] - SLOTS
    spots = lax.broadcasted_iota(jnp.int32, (1, length), 1)
    lane = lax.broadcasted_iota(jnp.int32, (1, SLOTS), 1)
    segment = jnp.zeros((1, length), jnp.float32)
    ends = jnp.zeros((1, SLOTS), jnp.float32)
    end = jnp.int32(0)
    for j in range(refs.lengths.shape[1]):
        end = end + refs.lengths[mine, j]
        segment = segment + jnp.where(spots >= end, 1.0, 0.0)
        ends = jnp.where(lane == j, end.astype(jnp.float32), ends)
    masks = refs.slot_masks
    used = jnp.zeros((1, slots), jnp.int32)
    limit = jnp.int32(0)
    for t in range(masks.shape[0]):
        used = jnp.where(task == t, masks[t : t + 1, :], used)
        limit = jnp.where(task == t, refs.prefix_lens[t], limit)
    live = jnp.where((used == 1) & (lane[:, :slots] < limit), 1.0, 0.0)
    meta[0:1, 0:slots] = live
    meta[0:1, SLOTS:] = segment
    meta[1:2, 0:SLOTS] = jnp.where(lane == task, 1.0, 0.0)
    meta[2:3, 0:SLOTS] = ends


AHEAD = 3
LAG = 2
CUTS = 8
TOKENS = 4
ATT_BEATS = 1
QKV_BEATS = 3
MIX_BEATS = 2
ACT_BEATS = 1
SPAN = 1024
GRADS = 14


def forward_backward_kernel(plan, names, *args):
    refs = SimpleNamespace(**dict(zip(names, args)))
    sems = refs
    place = plan.here()
    coords, line, core = place
    bf16, f32 = jnp.bfloat16, jnp.float32
    spread = plan.core_in_tp
    tokens, row, grad, pre = refs.tokens, refs.row, refs.grad, refs.pre
    whole, meta = refs.whole, refs.meta
    q, k, v, att, lse = refs.q, refs.k, refs.v, refs.att, refs.lse
    held = tokens.shape[0]
    width = row.shape[-1]
    length = q.shape[0]
    half = length // 2
    base = 0 if spread else 2 * core
    slot = core if spread else 0
    holds = None if spread else line // 2 == core

    forward_inputs(plan, place, refs, refs)
    greet(plan, place)

    gather = Gather(plan, place, refs.source, whole, sems)
    gather.start_line(0)
    gather.start_line(1)
    token_line = Line(plan, place, sems.token_send, sems.token_recv)
    for j in range(held):
        token_line.add(tokens.at[j], row.at[line, slot], base + j, core)
    grad_line = Line(plan, place, sems.grad_send, sems.grad_recv)
    for j in range(held):
        grad_line.add(refs.out_grad.at[j], grad.at[lax.rem(line, 2), slot], base + j, line // 2)
    for copy in gather.own_copies():
        copy.start()
    for i in range(2, AHEAD):
        gather.start_line(i)
    share = Sibling(plan, place, sems.share_send, sems.share_recv)
    meta_copy = share.copy(meta, meta, 4)
    if not spread:
        pl.when(holds)(meta_copy.start)
    for copy in gather.own_copies():
        copy.wait()

    last = gather.ticks(LAG)

    grads = min(GRADS, last - CUTS)

    def beat(i, x=0):
        gather.tick(i, AHEAD, LAG)
        pl.when((i >= TOKENS) & (i < TOKENS + CUTS))(lambda: token_line.start(i - TOKENS, CUTS))
        pl.when((i >= grads) & (i < grads + CUTS))(lambda: grad_line.start(i - grads, CUTS))
        return x

    gather.pass_on(0)
    steps = LAG * len(plan.axes) + 1
    done = TOKENS + CUTS
    lax.fori_loop(0, done, beat, 0)
    prefix_line = Line(plan, place, sems.prefix_send, sems.prefix_recv)
    for j in range(held):
        for side in range(plan.sides):
            prefix_line.send(
                refs.prefix.at[j, side], pre.at[:, :, gather.lanes], base + j, core if spread else side
            )

    token_line.settle()

    def share_token(chip):
        if spread:
            token_line.receive(row.at[chip, core], chip, core)
            share.copy(row.at[chip, core], row.at[chip, core], chip).start()
        else:
            @pl.when(holds)
            def _():
                token_line.receive(row.at[chip, 0], chip, core)
                share.copy(row.at[chip, 0], row.at[chip, 0], chip).start()

    for chip in range(LINE):
        share_token(chip)
    for chip in range(LINE):
        if spread:
            share.copy(row.at[chip, 1 - core], row.at[chip, 1 - core], chip).wait_recv()
        else:
            pl.when(jnp.logical_not(holds))(share.copy(row.at[chip, 0], row.at[chip, 0], chip).wait_recv)
    if not spread:
        pl.when(jnp.logical_not(holds))(meta_copy.wait_recv)
    prefix_line.settle()
    for chip in range(LINE):
        prefix_line.receive(pre.at[:, :, pl.ds(chip * LANES, LANES)], chip, core if spread else line // 2)
    refs.meta_cols[...] = jnp.transpose(meta[...])

    def ready(first, amount, done):
        until = min(last, first + amount - 1 + steps)
        if until > done:
            lax.fori_loop(done, until, beat, 0)
        for i in range(first, first + amount):
            gather.finish(i)
        return max(done, until)

    for kind, target in enumerate((q, k, v)):
        done = ready(kind * plan.sides, plan.sides, done)
        weight = whole.at[kind, core]

        def project(b, x, weight=weight, target=target):
            block = row[b].reshape(CHUNK, width)
            target[pl.ds(pl.multiple_of(b * CHUNK, CHUNK), CHUNK), :] = mm(
                block, weight[...].reshape(width, WIDE)
            ).astype(bf16)
            return x

        lax.fori_loop(0, LINE, project, 0)
        if kind < QKV_BEATS:
            beat(done)
            done = done + 1
    att_share = Sibling(plan, place, sems.att_send, sems.att_recv)
    here = pl.ds(pl.multiple_of(core * half, half), half)
    there = pl.ds(pl.multiple_of((1 - core) * half, half), half)
    keys, values, queries = refs.keys, refs.values, refs.queries
    keys[:, PAIR:] = key_marks(meta)

    def pair_lanes(p):
        return pl.ds(pl.multiple_of(p * PAIR, PAIR), PAIR)

    def att_copy(p):
        lanes = pair_lanes(p)
        return att_share.copy(att.at[there, lanes], refs.att_other.at[:, lanes], p)

    def pair(p, x):
        lanes = pair_lanes(p)
        queries[...] = jnp.transpose(q[:, lanes])
        keys[0:SLOTS, 0:PAIR] = pre[0, :, lanes]
        keys[SLOTS:, 0:PAIR] = k[:, lanes]
        values[:, 0:SLOTS] = jnp.transpose(pre[1, :, lanes])
        values[:, SLOTS:] = jnp.transpose(v[:, lanes])
        if ATT_BEATS > 0:
            beat(done + ATT_BEATS * p)
        for first in range(0, length, SPAN):
            rows = slice(first, first + SPAN)
            mixed, totals = attend_tile(queries[:, rows], query_marks(meta)[:, rows], keys[...], values[...])
            att[rows, lanes] = jnp.transpose(mixed).astype(bf16)
            lse[p, 0:1, rows] = totals[0]
            lse[p, 1:2, rows] = totals[1]
        if ATT_BEATS > 1:
            beat(done + ATT_BEATS * p + 1)
        att_copy(p).start()
        return x

    pairs = WIDE // PAIR
    lax.fori_loop(0, pairs, pair, 0)
    done = done + ATT_BEATS * pairs
    for p in range(pairs):
        att_copy(p).wait_recv()

    done = ready(3 * plan.sides, plan.sides, done)
    normal_one, rstd_one, normed, acc = refs.normal_one, refs.rstd_one, refs.normed, refs.acc
    low, slope, out = refs.normed, refs.slope, refs.out
    parts = half // CHUNK

    def weight(kind, side):
        return whole[kind, side].reshape(width, WIDE)

    def mix(b):
        rows = pl.ds(pl.multiple_of(b * CHUNK, CHUNK), CHUNK)
        own = att[pl.ds(pl.multiple_of(core * half + b * CHUNK, CHUNK), CHUNK), :]
        total = row[2 * core + b].reshape(CHUNK, width).astype(f32)
        total = total + mm_nt(own, weight(3, core)) + mm_nt(refs.att_other[rows, :], weight(3, 1 - core))
        normal, rstd = normalise(total)
        normal_one[rows, :] = normal
        rstd_one[rows, :] = jnp.broadcast_to(rstd, (CHUNK, LANES))
        low_normed = (normal * refs.gain_one[...] + refs.shift_one[...]).astype(bf16)
        normed[rows, :] = low_normed
        acc[rows, :] = low_normed.astype(f32)
        if b < MIX_BEATS:
            beat(done + b)

    for b in range(parts):
        mix(b)
    done = done + min(parts, MIX_BEATS)

    acted = refs.acted
    chunks = [slice(b * CHUNK, (b + 1) * CHUNK) for b in range(parts)]

    def act(j, done):
        def unit(side, x):
            for rows in chunks:
                upper = mm(normed[rows, :], weight(up_kind(j), side))
                bell = (1.0 + lax.erf(upper * (0.5**0.5))) * 0.5
                acted[2 * j + side, rows, :] = (upper * bell).astype(bf16)
                slope[2 * j + side, rows, :] = (
                    bell + upper * jnp.exp(upper * upper * -0.5) * (1.0 / (2.0 * math.pi) ** 0.5)
                ).astype(bf16)
            if ACT_BEATS > 0:
                beat(done + side)
            return x

        lax.fori_loop(0, 2, unit, 0)

    def add(j, done):
        for rows in chunks:
            acc[rows, :] += mm_nt(acted[2 * j, rows, :], weight(down_kind(j), 0)) + mm_nt(
                acted[2 * j + 1, rows, :], weight(down_kind(j), 1)
            )

    steps_of = sorted([(up_kind(j), act, j) for j in range(GROUPS)] + [(down_kind(j), add, j) for j in range(GROUPS)], key=lambda s: s[0])
    for kind, body, j in steps_of:
        done = ready(kind * plan.sides, plan.sides, done)
        body(j, done)
        done = done + 2 if body is act and ACT_BEATS > 0 else done

    grad_line.settle()
    for part in range(2):
        for side in range(plan.cores):
            grad_line.receive(grad.at[part, side], 2 * core + part, side if spread else line // 2)

    def close(b, x):
        rows = pl.ds(pl.multiple_of(b * CHUNK, CHUNK), CHUNK)
        normal, rstd = normalise(acc[rows, :])
        out[rows, :] = (normal * refs.gain_two[...] + refs.shift_two[...]).astype(bf16)
        d_second = normalise_grad(
            normal, rstd, refs.gain_two[...], grad[b].reshape(CHUNK, width).astype(f32)
        )
        acc[rows, :] = d_second
        low[rows, :] = d_second.astype(bf16)
        return x

    lax.fori_loop(0, parts, close, 0)
    places = tokens.shape[1]
    out_back = Line(plan, place, sems.out_send, sems.out_recv)
    for b in range(2):
        for side in range(plan.cores):
            spot, target = (line, side) if spread else (lax.rem(line, 2), line // 2)
            out_back.send(
                out.at[pl.ds((b * plan.cores + side) * places, places)], refs.pieces.at[spot],
                2 * core + b, target,
            )

    def feed_back(j, x):
        d_upper = [
            (mm(low[...], weight(down_kind(j), side)) * slope[2 * j + side].astype(f32)).astype(bf16)
            for side in range(2)
        ]
        acc[...] += mm_nt(d_upper[0], weight(up_kind(j), 0)) + mm_nt(d_upper[1], weight(up_kind(j), 1))
        return x

    lax.fori_loop(0, GROUPS, feed_back, 0)

    d_att, away = refs.d_att, refs.d_att_away
    d_share = Sibling(plan, place, sems.d_send, sems.d_recv)

    def d_copy(b):
        mine = pl.ds(pl.multiple_of(core * half + b * CHUNK, CHUNK), CHUNK)
        return d_share.copy(away.at[pl.ds(pl.multiple_of(b * CHUNK, CHUNK), CHUNK)], d_att.at[mine], b)

    def open_(b, x):
        rows = pl.ds(pl.multiple_of(b * CHUNK, CHUNK), CHUNK)
        d_first = normalise_grad(normal_one[rows, :], rstd_one[rows, 0:1], refs.gain_one[...], acc[rows, :])
        acc[rows, :] = d_first
        d_low = d_first.astype(bf16)
        away[rows, :] = mm(d_low, weight(3, 1 - core)).astype(bf16)
        d_copy(b).start()
        mine = pl.ds(pl.multiple_of(core * half + b * CHUNK, CHUNK), CHUNK)
        d_att[mine, :] = mm(d_low, weight(3, core)).astype(bf16)
        return x

    lax.fori_loop(0, parts, open_, 0)
    for b in range(parts):
        d_copy(b).wait_recv()

    def pair_inner(p, x):
        lanes = pair_lanes(p)
        lse[p, 2:4, :] = inner_rows(d_att[:, lanes], att[:, lanes])[0:2]
        return x

    lax.fori_loop(0, pairs, pair_inner, 0)
    columns, dq_acc = refs.meta_cols, normal_one
    d_queries, d_keys, d_values = (
        acted.at[pl.ds(n * length // half, length // half)] for n in range(3)
    )
    d_pre = refs.d_pre

    def prefix_pair(p, x):
        lanes = pair_lanes(p)
        live = columns[0:SLOTS, 0:1] > 0.5
        a, g, dq = gradient_tile(pre[0, :, lanes], pre[1, :, lanes], q[:, lanes], d_att[:, lanes], lse[p], live)
        d_pre[0, :, lanes] = a
        d_pre[1, :, lanes] = g
        dq_acc[lanes, :] = dq
        return x

    lax.fori_loop(0, pairs, prefix_pair, 0)
    prefix_sum = PrefixSum(plan, place, refs)
    prefix_sum.start()

    def key_block(kb, first, count):
        rows = pl.ds(pl.multiple_of(kb * KB, KB), KB)
        span = pl.ds(pl.multiple_of(first * KB, KB), count * KB)
        seg_k = columns[pl.ds(pl.multiple_of(SLOTS + kb * KB, SLOTS), KB), 0:1]
        part, at = kb * KB // half, pl.ds(pl.multiple_of(lax.rem(kb * KB, half), KB), KB)

        def one(p, x):
            lanes = pair_lanes(p)
            allowed = seg_k == meta[0:1, pl.ds(pl.multiple_of(SLOTS + first * KB, SLOTS), count * KB)]
            a, g, dq = gradient_tile(
                k[rows, lanes], v[rows, lanes], q[span, lanes], d_att[span, lanes], lse[p, :, span], allowed
            )
            d_keys[part, at, lanes] = a.astype(bf16)
            d_values[part, at, lanes] = g.astype(bf16)
            dq_acc[lanes, span] += dq
            return x

        lax.fori_loop(0, pairs, one, 0)

    swap = Sibling(plan, place, sems.swap_send, sems.swap_recv)
    spare = row
    own_blocks = half // KB
    for chip in range(LINE):
        if spread:
            share.copy(row.at[chip, core], row.at[chip, core], chip).wait_send()
        else:
            pl.when(holds)(share.copy(row.at[chip, 0], row.at[chip, 0], chip).wait_send)

    def swap_copy(i):
        return swap.copy(spare.at[i], spare.at[own_blocks + i], i)

    def grad_pieces(i):
        for side in range(plan.cores):
            spot, target = (line, side) if spread else (lax.rem(line, 2), line // 2)
            chip = own_blocks * core + i
            src = low.at[pl.ds(pl.multiple_of(i * KB + side * places, places), places)]
            dst = refs.grad_pieces.at[spot]
            stays = (chip == line) & (target == core)
            sem = sems.back_send.at[i, side]
            yield stays, remote(
                src, dst, sem, sems.back_recv.at[line, core], plan.device(coords, chip, target)
            ), pltpu.make_async_copy(src, dst, sem)

    def give(b):
        rows = pl.ds(pl.multiple_of(lax.rem(b * KB, half), KB), KB)
        part = b * KB // half
        span = pl.ds(pl.multiple_of(b * KB, KB), KB)
        i = lax.rem(b, own_blocks)
        d_queries[part, rows, :] = (jnp.transpose(dq_acc[:, span]) * 0.125).astype(bf16)
        term = mm_nt(d_queries[part, rows, :], weight(0, core))
        term = term + mm_nt(d_keys[part, rows, :], weight(1, core))
        term = term + mm_nt(d_values[part, rows, :], weight(2, core))
        owner = b // own_blocks

        @pl.when(core != owner)
        def _():
            spare[i] = term.astype(bf16).reshape(spare.shape[1:])
            swap_copy(i).start()

        @pl.when(core == owner)
        def _():
            own = term + acc[rows, :]
            swap_copy(i).wait_recv()
            low[rows, :] = (own + spare[own_blocks + i].reshape(KB, width).astype(f32)).astype(bf16)
            for stays, far, near in grad_pieces(i):
                pl.when(jnp.logical_not(stays))(far.start)
                pl.when(stays)(near.start)

    blocks = length // KB
    near_blocks = -(-(REACH - 1) // KB)
    turned = line < LINE // 2
    given = 0
    for o in range(blocks):
        first, final = max(0, o - near_blocks), min(blocks - 1, o + near_blocks)
        key_block(
            jnp.where(turned, blocks - 1 - o, o), jnp.where(turned, blocks - 1 - final, first), final - first + 1
        )
        prefix_sum.go_on(o)
        while given < blocks and min(blocks - 1, given + near_blocks) <= o:
            give(jnp.where(turned, blocks - 1 - given, given))
            given = given + 1
    prefix_sum.finish(blocks)

    lax.fori_loop(0, gather.count, lambda i, x: (gather.drain(i), x)[1], 0)
    token_line.drain()
    prefix_line.drain()
    grad_line.drain()
    if not spread:
        pl.when(holds)(meta_copy.wait_send)
    for p in range(pairs):
        att_copy(p).wait_send()
    for b in range(parts):
        d_copy(b).wait_send()
    for i in range(own_blocks):
        swap_copy(i).wait_send()
        for stays, far, near in grad_pieces(i):
            pl.when(jnp.logical_not(stays))(far.wait_send)
            pl.when(stays)(near.wait)
    out_back.settle()
    arrivals = Line(plan, place, sems.back_send, sems.back_recv)
    for j in range(held):
        chip = j if spread else 2 * core + j
        out_back.receive(refs.pieces.at[j], chip, line // 2)
        arrivals.receive(refs.grad_pieces.at[j], chip, line // 2)
    out_back.drain()


def forward_backward(plan, given):
    held, places, width = given.tokens.shape
    depth = given.w_query.shape[0]
    length = places * plan.tp
    half = length // 2
    pairs = WIDE // PAIR
    bf16, f32 = jnp.bfloat16, jnp.float32
    S = jax.ShapeDtypeStruct
    tasks, slots, part = given.prefix_keys.shape
    kept = -(-slots // 16) * 16
    steps = len(plan.axes)
    reach = max(plan.shape[a] for a in plan.axes) - 1
    outs = dict(
        pieces=S((held, places, width), bf16),
        grad_pieces=S((held, places, width), bf16),
        keys_grad=S((tasks, slots, part), f32),
        values_grad=S((tasks, slots, part), f32),
    )
    scratch = dict(
        source=((KINDS, plan.sides, depth, LANES), bf16),
        prefix=((held, plan.sides, 2, SLOTS, LANES), bf16),
        meta=((8, SLOTS + length), f32),
        whole=((KINDS, 2) + plan.shape + (depth, WIDE), bf16),
        row=((LINE, plan.cores, places, width), bf16),
        grad=((2, plan.cores, places, width), bf16),
        pre=((2, SLOTS, WIDE), bf16),
        q=((length, WIDE), bf16),
        k=((length, WIDE), bf16),
        v=((length, WIDE), bf16),
        att=((length, WIDE), bf16),
        lse=((pairs, 8, length), f32),
        att_other=((half, WIDE), bf16),
        keys=((SLOTS + length, 2 * PAIR), bf16),
        values=((PAIR, SLOTS + length), bf16),
        queries=((PAIR, length), bf16),
        meta_cols=((SLOTS + length, 8), f32),
        normal_one=((half, width), f32),
        rstd_one=((half, LANES), f32),
        normed=((half, width), bf16),
        slope=((2 * GROUPS, half, WIDE), bf16),
        acted=((2 * GROUPS, half, WIDE), bf16),
        acc=((half, width), f32),
        out=((half, width), bf16),
        d_att=((length, WIDE), bf16),
        d_att_away=((half, WIDE), bf16),
        d_pre=((2, SLOTS, WIDE), f32),
        terms=((LINE, 2, SLOTS, LANES), bf16),
        row_terms=((LINE, 2, SLOTS, LANES), bf16),
        total=((tasks, 2, kept, LANES), f32),
        total_other=((tasks, 2, kept, LANES), f32),
        gone=((steps, tasks, 2, kept, LANES), bf16),
        come=((steps, reach, tasks, 2, kept, LANES), bf16),
    )
    sems = gather_semaphores(plan)
    sems.update(
        token_send=semaphores(held),
        token_recv=semaphores(LINE, 2),
        prefix_send=semaphores(held * plan.sides),
        prefix_recv=semaphores(LINE, 2),
        grad_send=semaphores(held),
        grad_recv=semaphores(LINE, 2),
        share_send=semaphores(5),
        share_recv=semaphores(5),
        att_send=semaphores(pairs),
        att_recv=semaphores(pairs),
        d_send=semaphores(half // CHUNK),
        d_recv=semaphores(half // CHUNK),
        out_send=semaphores(4),
        out_recv=semaphores(LINE, 2),
        back_send=semaphores(half // KB, 2),
        back_recv=semaphores(LINE, 2),
        swap_send=semaphores(half // KB),
        swap_recv=semaphores(half // KB),
        terms_send=semaphores(LINE),
        terms_recv=semaphores(LINE, 2),
        total_send=semaphores(1),
        total_recv=semaphores(1),
        sum_send=semaphores(steps, reach),
        sum_recv=semaphores(steps, reach),
    )
    smem = pl.BlockSpec(memory_space=pltpu.SMEM)
    vmem = pl.BlockSpec(memory_space=pltpu.VMEM)
    hbm = pl.BlockSpec(memory_space=pl.ANY)
    results = pl.pallas_call(
        functools.partial(forward_backward_kernel, plan, (*vars(given), *outs, *scratch, *sems)),
        out_shape=list(outs.values()),
        in_specs=[smem, smem, smem, vmem, hbm, hbm] + [vmem] * 12,
        out_specs=[hbm, hbm, vmem, vmem],
        scratch_shapes=[pltpu.VMEM(*spec) for spec in scratch.values()] + list(sems.values()),
        compiler_params=pltpu.CompilerParams(
            collective_id=0, has_side_effects=True, vmem_limit_bytes=63 * 2**20
        ),
    )(*vars(given).values())
    return SimpleNamespace(**dict(zip(outs, results)))


def shards(
    plan, tokens, w_query, w_key, w_value, w_attn_out, w_up, w_down, first_gain, first_shift,
    second_gain, second_shift, prefix_keys, prefix_values, example_lengths, task_ids, prefix_lens,
    slot_masks, out_grad,
):
    done = forward_backward(
        plan,
        SimpleNamespace(
            task_ids=task_ids,
            lengths=example_lengths,
            prefix_lens=prefix_lens,
            slot_masks=slot_masks,
            tokens=tokens,
            out_grad=out_grad,
            w_query=w_query,
            w_key=w_key,
            w_value=w_value,
            w_attn_out=w_attn_out,
            w_up=w_up,
            w_down=w_down,
            gain_one=first_gain[None],
            shift_one=first_shift[None],
            gain_two=second_gain[None],
            shift_two=second_shift[None],
            prefix_keys=prefix_keys,
            prefix_values=prefix_values,
        ),
    )
    return done.pieces, done.grad_pieces.astype(jnp.float32), done.keys_grad, done.values_grad


def solution(mesh):
    placed = (
        P("rows", "tp", None),
        P("rows", "tp"),
        P("rows", "tp"),
        P("rows", "tp"),
        P("tp", "rows"),
        P("rows", "tp"),
        P("tp", "rows"),
        P(),
        P(),
        P(),
        P(),
        P(None, None, "tp"),
        P(None, None, "tp"),
        P("rows", None),
        P("rows"),
        P(),
        P(),
        P("rows", "tp", None),
    )
    plan = Plan(mesh.shape["rows"], mesh.shape["tp"])
    return jax.shard_map(
        functools.partial(shards, plan),
        mesh=mesh,
        in_specs=placed,
        out_specs=(
            P("rows", "tp", None),
            P("rows", "tp", None),
            P(None, None, "tp"),
            P(None, None, "tp"),
        ),
        check_vma=False,
    )
```

```python
import functools
import math
from types import SimpleNamespace

import jax
import jax.numpy as jnp
from jax import lax
from jax.experimental import pallas as pl
from jax.experimental.pallas import tpu as pltpu
from jax.sharding import PartitionSpec as P

HD = 64
PAIR = 2 * HD
SLOTS = 128
QB = 256
KB = 256
REACH = 512
NEG = -1e30
MARKS = 16
NT = (((1,), (1,)), ((), ()))


def mm(a, b):
    return jnp.dot(a, b, preferred_element_type=jnp.float32)


def mm_nt(a, b):
    return lax.dot_general(a, b, NT, preferred_element_type=jnp.float32)


def head_lanes(half):
    lane = lax.broadcasted_iota(jnp.int32, (1, PAIR), 1)
    return (lane >= half * HD) & (lane < (half + 1) * HD)


def only_head(a, half):
    return jnp.where(head_lanes(half), a, jnp.zeros_like(a))


def key_marks(meta):
    length = meta.shape[1]
    row = lax.broadcasted_iota(jnp.int32, (PAIR, length), 0)
    place = lax.broadcasted_iota(jnp.int32, (PAIR, length), 1)
    seg = meta[0:1, :]
    other = (place >= SLOTS) & (row < 8) & (row.astype(jnp.float32) != seg)
    dead = (place < SLOTS) & (row == 8) & (seg < 0.5)
    ones = (row >= 9) & (row < 12)
    marks = jnp.where(other | dead, NEG, jnp.where(ones, 1.0, 0.0))
    return jnp.transpose(marks).astype(jnp.bfloat16)


def query_marks(meta):
    length = meta.shape[1] - SLOTS
    row = lax.broadcasted_iota(jnp.int32, (MARKS, length), 0)
    seg = meta[0:1, SLOTS:]
    return jnp.where(((row < 8) & (row.astype(jnp.float32) == seg)) | (row == 8), 1.0, 0.0)


def attend_tile(q_t, marks, keys, values):
    scaled = q_t * jnp.asarray(0.125, jnp.bfloat16)
    blank = jnp.zeros((PAIR - MARKS, marks.shape[1]), jnp.bfloat16)
    low_marks = jnp.concatenate([marks.astype(jnp.bfloat16), blank], axis=0)
    mixed, totals = [], []
    zero = jnp.zeros((HD, q_t.shape[1]), jnp.bfloat16)
    ones = jnp.ones((16, keys.shape[0]), jnp.bfloat16)
    for half in range(2):
        rows = slice(half * HD, (half + 1) * HD)
        own = [scaled[rows, :], zero] if half == 0 else [zero, scaled[rows, :]]
        scores = mm(keys, jnp.concatenate([*own, low_marks], axis=0))
        top = jnp.max(scores, axis=0, keepdims=True)
        probs = jnp.exp(scores - top).astype(jnp.bfloat16)
        out = mm(jnp.concatenate([values[rows, :], ones], axis=0), probs)
        total = out[HD : HD + 1, :]
        mixed.append(out[:HD, :] * (1.0 / total))
        totals.append(top + jnp.log(total))
    return jnp.concatenate(mixed, axis=0), totals


def inner_rows(do, att):
    picks = lax.broadcasted_iota(jnp.int32, (8, PAIR), 0)
    lanes = lax.broadcasted_iota(jnp.int32, (8, PAIR), 1) // HD
    picker = jnp.where(picks == lanes, 1.0, 0.0).astype(jnp.bfloat16)
    prod = do.astype(jnp.float32) * att.astype(jnp.float32)
    high = prod.astype(jnp.bfloat16)
    return mm_nt(picker, high) + mm_nt(picker, (prod - high.astype(jnp.float32)).astype(jnp.bfloat16))


def gradient_tile(keys, values, q, do, rows, allowed):
    back = jnp.transpose(keys)
    d_keys = jnp.zeros(keys.shape, jnp.float32)
    d_values = jnp.zeros(keys.shape, jnp.float32)
    d_query = []
    scaled = q * jnp.asarray(0.125, jnp.bfloat16)
    for half in range(2):
        qh, dh = only_head(scaled, half), only_head(do, half)
        scores = jnp.where(allowed, mm_nt(keys, qh), NEG)
        probs = jnp.exp(scores - rows[half : half + 1, :])
        d_scores = (probs * (mm_nt(values, dh) - rows[2 + half : 3 + half, :])).astype(jnp.bfloat16)
        d_keys = d_keys + mm(d_scores, qh)
        d_values = d_values + mm(probs.astype(jnp.bfloat16), dh)
        d_query.append(mm(back[half * HD : (half + 1) * HD, :], d_scores))
    return d_keys, d_values, jnp.concatenate(d_query, axis=0)


MESH = pl.DeviceIdType.MESH
LINE = 4
LANES = 128
WIDE = LINE * LANES
KINDS = 12
FIRST_UP = 4
GROUPS = (KINDS - FIRST_UP) // 2
CHUNK = 256


class Plan:
    def __init__(self, rows, tp):
        self.rows = rows
        self.tp = tp
        self.core_in_tp = tp > LINE
        self.shape = (rows // 8, 2, 4) if self.core_in_tp else (rows // 4, 2, 2)
        self.axes = (0, 1, 2) if self.core_in_tp else (0, 1)
        self.cores = 2 if self.core_in_tp else 1
        self.sides = 2 // self.cores

    def here(self):
        r = lax.axis_index("rows")
        t = lax.axis_index("tp")
        a, b, c = self.shape
        coords = (r // (b * c), lax.rem(r // c, b), lax.rem(r, c))
        if self.core_in_tp:
            return coords, t // 2, lax.rem(t, 2)
        return coords, t, coords[2]

    def device(self, coords, line, core):
        a, b, c = self.shape
        if self.core_in_tp:
            return ((coords[0] * b + coords[1]) * c + coords[2], line * 2 + core)
        return ((coords[0] * b + coords[1]) * c + core, line)

    def row_core(self, chip):
        return None if self.core_in_tp else chip // 2


def shifted(coords, axis, by, size):
    moved = list(coords)
    moved[axis] = lax.rem(coords[axis] + by, size)
    return tuple(moved)


def sibling(plan, place):
    coords, line, core = place
    return plan.device(coords, line, 1 - core)


def greet(plan, place):
    coords, line, core = place
    others = [
        plan.device(coords, lax.rem(line + by, LINE), side) for by in range(1, LINE) for side in range(2)
    ]
    others.append(sibling(plan, place))
    for axis in plan.axes:
        for by in range(1, plan.shape[axis]):
            others.append(plan.device(shifted(coords, axis, by, plan.shape[axis]), line, core))
    barrier = pltpu.get_barrier_semaphore()
    for other in others:
        pl.semaphore_signal(barrier, inc=1, device_id=other, device_id_type=MESH)
    return lambda: pl.semaphore_wait(barrier, len(others))


def remote(src, dst, send, recv, device):
    return pltpu.make_async_remote_copy(
        src_ref=src, dst_ref=dst, send_sem=send, recv_sem=recv, device_id=device, device_id_type=MESH
    )


class Gather:
    def __init__(self, plan, place, source, whole, sems):
        self.plan = plan
        self.place = place
        self.coords, self.line, self.core = place
        self.source = source
        self.whole = whole
        self.sems = sems
        self.count = KINDS * plan.sides
        self.depth = source.shape[-2]
        self.orders = (plan.axes, plan.axes[::-1])
        self.lanes = pl.ds(pl.multiple_of(self.line * LANES, LANES), LANES)

    def unit(self, i):
        if self.plan.core_in_tp:
            return (i, self.core)
        return (i // 2, lax.rem(i, 2))

    def own_copies(self):
        where = tuple(self.coords) + (slice(None), self.lanes)
        for at in range(self.plan.sides):
            side = self.core if self.plan.core_in_tp else at
            yield pltpu.make_async_copy(
                self.source.at[:, at], self.whole.at[(slice(None), side) + where], self.sems.own.at[at]
            )

    def block(self, i, chip):
        lanes = pl.ds(pl.multiple_of(chip * LANES, LANES), LANES)
        return self.whole.at[self.unit(i) + tuple(self.coords) + (slice(None), lanes)]

    def line_copies(self, i):
        src = self.source.at[(i, 0) if self.plan.core_in_tp else self.unit(i)]
        for at, by in enumerate((1, -1, 2, -2)):
            chip = self.line + by
            there = (chip >= 0) & (chip < LINE)
            yield there, remote(
                src, self.block(i, self.line), self.sems.line_send.at[i, at], self.sems.line_recv.at[i, self.line],
                self.plan.device(self.coords, jnp.clip(chip, 0, LINE - 1), self.core),
            )

    def pass_copies(self, i):
        for middle, first, target in ((2, 0, 3), (1, 3, 0)):
            block = self.block(i, first)
            yield self.line == middle, remote(
                block, block, self.sems.line_send.at[i, 4], self.sems.line_recv.at[i, first],
                self.plan.device(self.coords, target, self.core),
            )

    def line_arrived(self, i, chip):
        block = self.block(i, chip)
        remote(
            block, block, self.sems.line_send.at[i, 0], self.sems.line_recv.at[i, chip],
            self.plan.device(self.coords, chip, self.core),
        ).wait_recv()

    def axis_copies(self, i, step):
        rows = self.depth // 2
        for half in range(2):
            order = self.orders[half]
            axis = order[step]
            size = self.plan.shape[axis]
            index = [
                pl.ds(0, self.plan.shape[a]) if a in order[:step] else self.coords[a] for a in range(3)
            ]
            block = self.whole.at[self.unit(i) + tuple(index) + (pl.ds(half * rows, rows),)]
            for by in range(1, size):
                spot = (i, half, step, by - 1)
                yield remote(
                    block, block, self.sems.axis_send.at[spot], self.sems.axis_recv.at[spot],
                    self.plan.device(shifted(self.coords, axis, by, size), self.line, self.core),
                )

    def core_copy(self, i, side):
        if self.plan.core_in_tp:
            block = self.whole.at[i, side]
        else:
            block = self.whole.at[self.unit(i) + (slice(None), slice(None), side)]
        return remote(
            block, block, self.sems.core_send.at[i], self.sems.core_recv.at[i], sibling(self.plan, self.place)
        )

    def core_roles(self, i):
        if self.plan.core_in_tp:
            wide = i >= 3
            return wide, wide
        side = lax.rem(i, 2)
        wide = i >= 6
        return wide | (side != self.core), wide | (side == self.core)

    def start_line(self, i):
        for there, copy in self.line_copies(i):
            pl.when(there)(copy.start)

    def pass_on(self, i):
        for (here, copy), first in zip(self.pass_copies(i), (0, 3)):

            @pl.when(here)
            def _(copy=copy, first=first):
                self.line_arrived(i, first)
                copy.start()

    def start_axis(self, i, step):
        if step == 0:
            for chip in range(LINE):
                passed = ((chip == 0) & (self.line == 2)) | ((chip == 3) & (self.line == 1))
                pl.when((self.line != chip) & jnp.logical_not(passed))(functools.partial(self.line_arrived, i, chip))
        else:
            for copy in self.axis_copies(i, step - 1):
                copy.wait_recv()
        for copy in self.axis_copies(i, step):
            copy.start()

    def start_core(self, i):
        for copy in self.axis_copies(i, len(self.plan.axes) - 1):
            copy.wait_recv()
        sends, _ = self.core_roles(i)
        pl.when(sends)(lambda: self.core_copy(i, self.core).start())

    def finish(self, i):
        _, gets = self.core_roles(i)
        pl.when(gets)(lambda: self.core_copy(i, 1 - self.core).wait_recv())

    def drain(self, i):
        for there, copy in (*self.line_copies(i), *self.pass_copies(i)):
            pl.when(there)(copy.wait_send)
        for step in range(len(self.plan.axes)):
            for copy in self.axis_copies(i, step):
                copy.wait_send()
        sends, _ = self.core_roles(i)
        pl.when(sends)(lambda: self.core_copy(i, self.core).wait_send())

    def tick(self, i, ahead, lag):
        steps = len(self.plan.axes)

        def guarded(at, body):
            pl.when((at >= 0) & (at < self.count))(functools.partial(body, at))

        guarded(i + ahead, self.start_line)
        guarded(i + 1, self.pass_on)
        for step in range(steps):
            guarded(i - lag * step, lambda at, step=step: self.start_axis(at, step))
        guarded(i - lag * steps, self.start_core)

    def ticks(self, lag):
        return self.count + lag * len(self.plan.axes)


def semaphores(*shape):
    return pltpu.SemaphoreType.DMA(shape)


def gather_semaphores(plan):
    count = KINDS * plan.sides
    steps = len(plan.axes)
    reach = max(plan.shape[a] for a in plan.axes) - 1
    return dict(
        line_send=semaphores(count, 5),
        line_recv=semaphores(count, LINE),
        axis_send=semaphores(count, 2, steps, reach),
        axis_recv=semaphores(count, 2, steps, reach),
        core_send=semaphores(count),
        core_recv=semaphores(count),
        own=semaphores(2),
    )


class Line:
    def __init__(self, plan, place, send_sems, recv_sems):
        self.plan = plan
        self.coords, self.line, self.core = place
        self.send_sems = send_sems
        self.recv_sems = recv_sems
        self.pieces = []

    def here(self, chip, side):
        return (chip == self.line) & (side == self.core)

    def add(self, src, dst, chip, side):
        at = len(self.pieces)
        device = self.plan.device(self.coords, chip, side)

        def far(src, dst):
            return remote(src, dst, self.send_sems.at[at], self.recv_sems.at[self.line, self.core], device)

        near = pltpu.make_async_copy(src, dst, self.send_sems.at[at])
        self.pieces.append((self.here(chip, side), src, dst, far, near))

    def start(self, part=0, parts=1):
        for stays, src, dst, far, near in self.pieces:
            rows = src.shape[0] // parts
            cut = pl.ds(pl.multiple_of(part * rows, rows), rows) if parts > 1 else slice(None)
            pl.when(jnp.logical_not(stays))(far(src.at[cut], dst.at[cut]).start)
            pl.when(stays & (part == 0))(near.start)

    def send(self, src, dst, chip, side):
        self.add(src, dst, chip, side)
        stays, src, dst, far, near = self.pieces[-1]
        pl.when(jnp.logical_not(stays))(far(src, dst).start)
        pl.when(stays)(near.start)

    def settle(self):
        for stays, *_, near in self.pieces:
            pl.when(stays)(near.wait)

    def drain(self):
        for stays, src, dst, far, _ in self.pieces:
            pl.when(jnp.logical_not(stays))(far(src, dst).wait_send)

    def receive(self, dst, chip, side):
        copy = remote(
            dst, dst, self.send_sems.at[0], self.recv_sems.at[chip, side],
            self.plan.device(self.coords, chip, side),
        )
        pl.when(jnp.logical_not(self.here(chip, side)))(copy.wait_recv)


class Sibling:
    def __init__(self, plan, place, send_sems, recv_sems):
        self.send_sems = send_sems
        self.recv_sems = recv_sems
        self.device = sibling(plan, place)

    def copy(self, src, dst, at):
        return remote(src, dst, self.send_sems.at[at], self.recv_sems.at[at], self.device)


class PrefixSum:
    def __init__(self, plan, place, refs):
        self.plan = plan
        self.place = place
        self.refs = refs
        self.coords, self.line, self.core = place
        self.terms = Line(plan, place, refs.terms_send, refs.terms_recv)
        self.last = Sibling(plan, place, refs.total_send, refs.total_recv)

    def start(self):
        refs = self.refs
        for chip in range(LINE):
            lanes = slice(chip * LANES, (chip + 1) * LANES)
            for which in range(2):
                refs.terms[chip, which] = refs.d_pre[which, :, lanes].astype(jnp.bfloat16)
            refs.terms[chip, 0, SLOTS - 16 :, :] = jnp.broadcast_to(refs.meta[1:2, 0:SLOTS], (16, SLOTS)).astype(
                jnp.bfloat16
            )
        for chip in range(LINE):
            self.terms.send(refs.terms.at[chip], refs.row_terms.at[self.line], chip, self.core)

    def copies(self, step):
        refs = self.refs
        axis = self.plan.axes[step]
        size = self.plan.shape[axis]
        return [
            remote(
                refs.gone.at[step], refs.come.at[step, by - 1], refs.sum_send.at[step, by - 1],
                refs.sum_recv.at[step, by - 1],
                self.plan.device(shifted(self.coords, axis, by, size), self.line, self.core),
            )
            for by in range(1, size)
        ]

    def send(self, step):
        self.refs.gone[step] = self.refs.total[...].astype(jnp.bfloat16)
        for copy in self.copies(step):
            copy.start()

    def line_sum(self):
        refs = self.refs
        total = refs.total
        tasks, _, kept = total.shape[:3]
        self.terms.settle()
        for chip in range(LINE):
            self.terms.receive(refs.row_terms.at[chip], chip, self.core)
            marks = refs.row_terms[chip, 0, SLOTS - 16 :, :].astype(jnp.float32)
            for task in range(tasks):
                for which in range(2):
                    more = refs.row_terms[chip, which, 0:kept, :].astype(jnp.float32) * marks[0:1, task : task + 1]
                    total[task, which] = more if chip == 0 else total[task, which] + more

    def receive(self, step):
        for by, copy in enumerate(self.copies(step)):
            copy.wait_recv()
            self.refs.total[...] += self.refs.come[step, by].astype(jnp.float32)

    def go_on(self, beat):
        steps = len(self.plan.axes)
        if beat == 0:
            self.line_sum()
        elif beat <= steps:
            self.receive(beat - 1)
        if beat < steps:
            self.send(beat)
        elif beat == steps and not self.plan.core_in_tp:
            self.last.copy(self.refs.total, self.refs.total_other, 0).start()

    def put(self, block, lanes):
        refs = self.refs
        slots, tasks = refs.keys_grad.shape[:2]
        for task in range(tasks):
            refs.keys_grad[:, task, lanes] = block[task, 0, 0:slots, :]
            refs.values_grad[:, task, lanes] = block[task, 1, 0:slots, :]

    def finish(self, beats):
        refs = self.refs
        steps = len(self.plan.axes)
        for beat in range(beats, steps + 1):
            self.go_on(beat)
        if self.plan.core_in_tp:
            self.put(refs.total, slice(None))
        else:
            self.last.copy(refs.total, refs.total_other, 0).wait_recv()
            sides = slice(0, LANES), slice(LANES, 2 * LANES)
            for side in range(2):

                @pl.when(self.core == side)
                def _(side=side):
                    self.put(refs.total, sides[side])
                    self.put(refs.total_other, sides[1 - side])

            self.last.copy(refs.total, refs.total_other, 0).wait_send()
        self.terms.drain()
        for step in range(steps):
            for copy in self.copies(step):
                copy.wait_send()


def normalise(z):
    mean = jnp.mean(z, axis=1, keepdims=True)
    centred = z - mean
    rstd = lax.rsqrt(jnp.mean(centred * centred, axis=1, keepdims=True) + 1e-05)
    return centred * rstd, rstd


def normalise_grad(normal, rstd, gain, grad):
    g = grad * gain
    return rstd * (
        g - jnp.mean(g, axis=1, keepdims=True) - normal * jnp.mean(g * normal, axis=1, keepdims=True)
    )


def up_kind(j):
    return FIRST_UP + j + jnp.maximum(j - 1, 0) if not isinstance(j, int) else FIRST_UP + j + max(j - 1, 0)


def down_kind(j):
    return jnp.minimum(FIRST_UP + 2 + 2 * j, KINDS - 1) if not isinstance(j, int) else min(FIRST_UP + 2 + 2 * j, KINDS - 1)


def put_blocks(plan, source, kind, block, first):
    for side in range(plan.sides):
        at = (first + side) * LANES
        source[kind, side] = block[:, at : at + LANES]


def first_inputs(plan, refs):
    for kind, block in enumerate((refs.w_query, refs.w_key, refs.w_value)):
        put_blocks(plan, refs.source, kind, block, 0)


def other_inputs(plan, place, refs):
    coords, line, core = place
    source, prefix, meta = refs.source, refs.prefix, refs.meta
    sides = plan.sides
    put_blocks(plan, source, 3, jnp.transpose(refs.w_attn_out[...]), 0)
    down = jnp.transpose(refs.w_down[...])
    for j in range(GROUPS):
        put_blocks(plan, source, up_kind(j), refs.w_up, j * sides)
        put_blocks(plan, source, down_kind(j), down, j * sides)

    slots, tasks = refs.prefix_keys.shape[:2]
    prefix[...] = jnp.zeros_like(prefix)
    tables = [ref[...].astype(jnp.float32) for ref in (refs.prefix_keys, refs.prefix_values)]
    for j in range(refs.tokens.shape[0]):
        task = refs.task_ids[j]
        for which, table in enumerate(tables):
            rows = table[:, 0, :]
            for t in range(1, tasks):
                rows = jnp.where(task == t, table[:, t, :], rows)
            rows = rows.astype(jnp.bfloat16)
            for side in range(sides):
                prefix[j, side, which, 0:slots, :] = rows[:, side * LANES : (side + 1) * LANES]

    def tables():
        mine = line if plan.core_in_tp else lax.rem(line, 2)
        task = refs.task_ids[mine]
        meta[...] = jnp.zeros_like(meta)
        length = meta.shape[1] - SLOTS
        spots = lax.broadcasted_iota(jnp.int32, (1, length), 1)
        lane = lax.broadcasted_iota(jnp.int32, (1, SLOTS), 1)
        segment = jnp.zeros((1, length), jnp.float32)
        ends = jnp.zeros((1, SLOTS), jnp.float32)
        end = jnp.int32(0)
        for j in range(refs.lengths.shape[1]):
            end = end + refs.lengths[mine, j]
            segment = segment + jnp.where(spots >= end, 1.0, 0.0)
            ends = jnp.where(lane == j, end.astype(jnp.float32), ends)
        masks = refs.slot_masks
        used = jnp.zeros((1, slots), jnp.int32)
        limit = jnp.int32(0)
        for t in range(masks.shape[0]):
            used = jnp.where(task == t, masks[t : t + 1, :], used)
            limit = jnp.where(task == t, refs.prefix_lens[t], limit)
        live = jnp.where((used == 1) & (lane[:, :slots] < limit), 1.0, 0.0)
        meta[0:1, 0:slots] = live
        meta[0:1, SLOTS:] = segment
        meta[1:2, 0:SLOTS] = jnp.where(lane == task, 1.0, 0.0)
        meta[2:3, 0:SLOTS] = ends

    if plan.core_in_tp:
        tables()
    else:
        pl.when(line // 2 == core)(tables)


AHEAD = 3
LAG = 2
CUTS = 8
TOKENS = 4
ATT_BEATS = 1
QKV_BEATS = 3
MIX_BEATS = 2
ACT_BEATS = 1
SPAN = 1024
UNROLL = 2
GRADS = 14


def forward_backward_kernel(plan, names, *args):
    refs = SimpleNamespace(**dict(zip(names, args)))
    sems = refs
    place = plan.here()
    coords, line, core = place
    bf16, f32 = jnp.bfloat16, jnp.float32
    spread = plan.core_in_tp
    tokens, row, grad, pre = refs.tokens, refs.row, refs.grad, refs.pre
    whole, meta = refs.whole, refs.meta
    q, k, v, att, lse = refs.q, refs.k, refs.v, refs.att, refs.lse
    held = tokens.shape[0]
    width = row.shape[-1]
    length = q.shape[0]
    half = length // 2
    base = 0 if spread else 2 * core
    slot = core if spread else 0
    holds = None if spread else line // 2 == core

    greeted = greet(plan, place)
    first_inputs(plan, refs)
    greeted()

    gather = Gather(plan, place, refs.source, whole, sems)
    for i in range(AHEAD):
        gather.start_line(i)
    other_inputs(plan, place, refs)
    token_line = Line(plan, place, sems.token_send, sems.token_recv)
    for j in range(held):
        token_line.add(tokens.at[j], row.at[line, slot], base + j, core)
    grad_line = Line(plan, place, sems.grad_send, sems.grad_recv)
    for j in range(held):
        grad_line.add(refs.out_grad.at[j], grad.at[lax.rem(line, 2), slot], base + j, line // 2)
    for copy in gather.own_copies():
        copy.start()
    share = Sibling(plan, place, sems.share_send, sems.share_recv)
    meta_copy = share.copy(meta, meta, 4)
    if not spread:
        pl.when(holds)(meta_copy.start)
    for copy in gather.own_copies():
        copy.wait()

    last = gather.ticks(LAG)

    grads = min(GRADS, last - CUTS)

    def beat(i, x=0):
        gather.tick(i, AHEAD, LAG)
        pl.when((i >= TOKENS) & (i < TOKENS + CUTS))(lambda: token_line.start(i - TOKENS, CUTS))
        pl.when((i >= grads) & (i < grads + CUTS))(lambda: grad_line.start(i - grads, CUTS))
        return x

    gather.pass_on(0)
    steps = LAG * len(plan.axes) + 1
    done = TOKENS + CUTS
    lax.fori_loop(0, done, beat, 0)
    prefix_line = Line(plan, place, sems.prefix_send, sems.prefix_recv)
    for j in range(held):
        for side in range(plan.sides):
            prefix_line.send(
                refs.prefix.at[j, side], pre.at[:, :, gather.lanes], base + j, core if spread else side
            )

    token_line.settle()

    def share_token(chip):
        if spread:
            token_line.receive(row.at[chip, core], chip, core)
            share.copy(row.at[chip, core], row.at[chip, core], chip).start()
        else:
            @pl.when(holds)
            def _():
                token_line.receive(row.at[chip, 0], chip, core)
                share.copy(row.at[chip, 0], row.at[chip, 0], chip).start()

    for chip in range(LINE):
        share_token(chip)
    for chip in range(LINE):
        if spread:
            share.copy(row.at[chip, 1 - core], row.at[chip, 1 - core], chip).wait_recv()
        else:
            pl.when(jnp.logical_not(holds))(share.copy(row.at[chip, 0], row.at[chip, 0], chip).wait_recv)
    if not spread:
        pl.when(jnp.logical_not(holds))(meta_copy.wait_recv)
    prefix_line.settle()
    for chip in range(LINE):
        prefix_line.receive(pre.at[:, :, pl.ds(chip * LANES, LANES)], chip, core if spread else line // 2)
    refs.meta_cols[...] = jnp.transpose(meta[...])

    def ready(first, amount, done):
        until = min(last, first + amount - 1 + steps)
        if until > done:
            lax.fori_loop(done, until, beat, 0)
        for i in range(first, first + amount):
            gather.finish(i)
        return max(done, until)

    for kind, target in enumerate((q, k, v)):
        done = ready(kind * plan.sides, plan.sides, done)
        weight = whole.at[kind, core]

        def project(b, x, weight=weight, target=target):
            block = row[b].reshape(CHUNK, width)
            target[pl.ds(pl.multiple_of(b * CHUNK, CHUNK), CHUNK), :] = mm(
                block, weight[...].reshape(width, WIDE)
            ).astype(bf16)
            return x

        lax.fori_loop(0, LINE, project, 0)
        if kind < QKV_BEATS:
            beat(done)
            done = done + 1
    att_share = Sibling(plan, place, sems.att_send, sems.att_recv)
    here = pl.ds(pl.multiple_of(core * half, half), half)
    there = pl.ds(pl.multiple_of((1 - core) * half, half), half)
    keys, values, queries = refs.keys, refs.values, refs.queries
    keys[:, PAIR:] = key_marks(meta)

    def pair_lanes(p):
        return pl.ds(pl.multiple_of(p * PAIR, PAIR), PAIR)

    def att_copy(p):
        lanes = pair_lanes(p)
        return att_share.copy(att.at[there, lanes], refs.att_other.at[:, lanes], p)

    def pair(p, x):
        lanes = pair_lanes(p)
        queries[...] = jnp.transpose(q[:, lanes])
        keys[0:SLOTS, 0:PAIR] = pre[0, :, lanes]
        keys[SLOTS:, 0:PAIR] = k[:, lanes]
        values[:, 0:SLOTS] = jnp.transpose(pre[1, :, lanes])
        values[:, SLOTS:] = jnp.transpose(v[:, lanes])
        if ATT_BEATS > 0:
            beat(done + ATT_BEATS * p)
        for first in range(0, length, SPAN):
            rows = slice(first, first + SPAN)
            mixed, totals = attend_tile(queries[:, rows], query_marks(meta)[:, rows], keys[...], values[...])
            att[rows, lanes] = jnp.transpose(mixed).astype(bf16)
            lse[p, 0:1, rows] = totals[0]
            lse[p, 1:2, rows] = totals[1]
        if ATT_BEATS > 1:
            beat(done + ATT_BEATS * p + 1)
        att_copy(p).start()
        return x

    pairs = WIDE // PAIR
    lax.fori_loop(0, pairs, pair, 0)
    done = done + ATT_BEATS * pairs
    for p in range(pairs):
        att_copy(p).wait_recv()

    done = ready(3 * plan.sides, plan.sides, done)
    normal_one, rstd_one, normed, acc = refs.normal_one, refs.rstd_one, refs.normed, refs.acc
    low, slope, out = refs.normed, refs.slope, refs.out
    parts = half // CHUNK

    def weight(kind, side):
        return whole[kind, side].reshape(width, WIDE)

    def mix(b):
        rows = pl.ds(pl.multiple_of(b * CHUNK, CHUNK), CHUNK)
        own = att[pl.ds(pl.multiple_of(core * half + b * CHUNK, CHUNK), CHUNK), :]
        total = row[2 * core + b].reshape(CHUNK, width).astype(f32)
        total = total + mm_nt(own, weight(3, core)) + mm_nt(refs.att_other[rows, :], weight(3, 1 - core))
        normal, rstd = normalise(total)
        normal_one[rows, :] = normal
        rstd_one[rows, :] = jnp.broadcast_to(rstd, (CHUNK, LANES))
        low_normed = (normal * refs.gain_one[...] + refs.shift_one[...]).astype(bf16)
        normed[rows, :] = low_normed
        acc[rows, :] = low_normed.astype(f32)
        if b < MIX_BEATS:
            beat(done + b)

    for b in range(parts):
        mix(b)
    done = done + min(parts, MIX_BEATS)

    acted = refs.acted
    chunks = [slice(b * CHUNK, (b + 1) * CHUNK) for b in range(parts)]

    def act(j, done):
        def unit(side, x):
            for rows in chunks:
                upper = mm(normed[rows, :], weight(up_kind(j), side))
                bell = (1.0 + lax.erf(upper * (0.5**0.5))) * 0.5
                acted[2 * j + side, rows, :] = (upper * bell).astype(bf16)
                slope[2 * j + side, rows, :] = (
                    bell + upper * jnp.exp(upper * upper * -0.5) * (1.0 / (2.0 * math.pi) ** 0.5)
                ).astype(bf16)
            if ACT_BEATS > 0:
                beat(done + side)
            return x

        lax.fori_loop(0, 2, unit, 0)

    def add(j, done):
        for rows in chunks:
            acc[rows, :] += mm_nt(acted[2 * j, rows, :], weight(down_kind(j), 0)) + mm_nt(
                acted[2 * j + 1, rows, :], weight(down_kind(j), 1)
            )

    steps_of = sorted([(up_kind(j), act, j) for j in range(GROUPS)] + [(down_kind(j), add, j) for j in range(GROUPS)], key=lambda s: s[0])
    for kind, body, j in steps_of:
        done = ready(kind * plan.sides, plan.sides, done)
        body(j, done)
        done = done + 2 if body is act and ACT_BEATS > 0 else done

    grad_line.settle()
    for part in range(2):
        for side in range(plan.cores):
            grad_line.receive(grad.at[part, side], 2 * core + part, side if spread else line // 2)

    def close(b, x):
        rows = pl.ds(pl.multiple_of(b * CHUNK, CHUNK), CHUNK)
        normal, rstd = normalise(acc[rows, :])
        out[rows, :] = (normal * refs.gain_two[...] + refs.shift_two[...]).astype(bf16)
        d_second = normalise_grad(
            normal, rstd, refs.gain_two[...], grad[b].reshape(CHUNK, width).astype(f32)
        )
        acc[rows, :] = d_second
        low[rows, :] = d_second.astype(bf16)
        return x

    lax.fori_loop(0, parts, close, 0)
    places = tokens.shape[1]
    out_back = Line(plan, place, sems.out_send, sems.out_recv)
    for b in range(2):
        for side in range(plan.cores):
            spot, target = (line, side) if spread else (lax.rem(line, 2), line // 2)
            out_back.send(
                out.at[pl.ds((b * plan.cores + side) * places, places)], refs.pieces.at[spot],
                2 * core + b, target,
            )

    def feed_back(j, x):
        d_upper = [
            (mm(low[...], weight(down_kind(j), side)) * slope[2 * j + side].astype(f32)).astype(bf16)
            for side in range(2)
        ]
        acc[...] += mm_nt(d_upper[0], weight(up_kind(j), 0)) + mm_nt(d_upper[1], weight(up_kind(j), 1))
        return x

    lax.fori_loop(0, GROUPS, feed_back, 0)

    d_att, away = refs.d_att, refs.d_att_away
    d_share = Sibling(plan, place, sems.d_send, sems.d_recv)

    def d_copy(b):
        mine = pl.ds(pl.multiple_of(core * half + b * CHUNK, CHUNK), CHUNK)
        return d_share.copy(away.at[pl.ds(pl.multiple_of(b * CHUNK, CHUNK), CHUNK)], d_att.at[mine], b)

    def open_(b, x):
        rows = pl.ds(pl.multiple_of(b * CHUNK, CHUNK), CHUNK)
        d_first = normalise_grad(normal_one[rows, :], rstd_one[rows, 0:1], refs.gain_one[...], acc[rows, :])
        acc[rows, :] = d_first
        d_low = d_first.astype(bf16)
        away[rows, :] = mm(d_low, weight(3, 1 - core)).astype(bf16)
        d_copy(b).start()
        mine = pl.ds(pl.multiple_of(core * half + b * CHUNK, CHUNK), CHUNK)
        d_att[mine, :] = mm(d_low, weight(3, core)).astype(bf16)
        return x

    for chip in range(LINE):
        if spread:
            share.copy(row.at[chip, core], row.at[chip, core], chip).wait_send()
        else:
            pl.when(holds)(share.copy(row.at[chip, 0], row.at[chip, 0], chip).wait_send)
    lax.fori_loop(0, parts, open_, 0)
    for b in range(parts):
        d_copy(b).wait_recv()

    def pair_inner(p, x):
        lanes = pair_lanes(p)
        lse[p, 2:4, :] = inner_rows(d_att[:, lanes], att[:, lanes])[0:2]
        return x

    lax.fori_loop(0, pairs, pair_inner, 0)
    columns, dq_acc = refs.meta_cols, normal_one
    d_queries, d_keys, d_values = (
        acted.at[pl.ds(n * length // half, length // half)] for n in range(3)
    )
    d_pre = refs.d_pre

    def prefix_pair(p, x):
        lanes = pair_lanes(p)
        live = columns[0:SLOTS, 0:1] > 0.5
        a, g, dq = gradient_tile(pre[0, :, lanes], pre[1, :, lanes], q[:, lanes], d_att[:, lanes], lse[p], live)
        d_pre[0, :, lanes] = a
        d_pre[1, :, lanes] = g
        dq_acc[lanes, :] = dq
        return x

    lax.fori_loop(0, pairs, prefix_pair, 0, unroll=UNROLL)
    prefix_sum = PrefixSum(plan, place, refs)
    prefix_sum.start()

    def key_block(kb, first, count):
        rows = pl.ds(pl.multiple_of(kb * KB, KB), KB)
        span = pl.ds(pl.multiple_of(first * KB, KB), count * KB)
        seg_k = columns[pl.ds(pl.multiple_of(SLOTS + kb * KB, SLOTS), KB), 0:1]
        part, at = kb * KB // half, pl.ds(pl.multiple_of(lax.rem(kb * KB, half), KB), KB)

        def one(p, x):
            lanes = pair_lanes(p)
            allowed = seg_k == meta[0:1, pl.ds(pl.multiple_of(SLOTS + first * KB, SLOTS), count * KB)]
            a, g, dq = gradient_tile(
                k[rows, lanes], v[rows, lanes], q[span, lanes], d_att[span, lanes], lse[p, :, span], allowed
            )
            d_keys[part, at, lanes] = a.astype(bf16)
            d_values[part, at, lanes] = g.astype(bf16)
            dq_acc[lanes, span] += dq
            return x

        lax.fori_loop(0, pairs, one, 0, unroll=UNROLL)

    swap = Sibling(plan, place, sems.swap_send, sems.swap_recv)
    spare = row
    own_blocks = half // KB

    def swap_copy(i):
        return swap.copy(spare.at[i], spare.at[own_blocks + i], i)

    def grad_pieces(i):
        for side in range(plan.cores):
            spot, target = (line, side) if spread else (lax.rem(line, 2), line // 2)
            chip = own_blocks * core + i
            src = low.at[pl.ds(pl.multiple_of(i * KB + side * places, places), places)]
            dst = refs.grad_pieces.at[spot]
            stays = (chip == line) & (target == core)
            sem = sems.back_send.at[i, side]
            yield stays, remote(
                src, dst, sem, sems.back_recv.at[line, core], plan.device(coords, chip, target)
            ), pltpu.make_async_copy(src, dst, sem)

    def give(b):
        rows = pl.ds(pl.multiple_of(lax.rem(b * KB, half), KB), KB)
        part = b * KB // half
        span = pl.ds(pl.multiple_of(b * KB, KB), KB)
        i = lax.rem(b, own_blocks)
        d_queries[part, rows, :] = (jnp.transpose(dq_acc[:, span]) * 0.125).astype(bf16)
        term = mm_nt(d_queries[part, rows, :], weight(0, core))
        term = term + mm_nt(d_keys[part, rows, :], weight(1, core))
        term = term + mm_nt(d_values[part, rows, :], weight(2, core))
        owner = b // own_blocks

        @pl.when(core != owner)
        def _():
            spare[i] = term.astype(bf16).reshape(spare.shape[1:])
            swap_copy(i).start()

        @pl.when(core == owner)
        def _():
            own = term + acc[rows, :]
            swap_copy(i).wait_recv()
            low[rows, :] = (own + spare[own_blocks + i].reshape(KB, width).astype(f32)).astype(bf16)
            for stays, far, near in grad_pieces(i):
                pl.when(jnp.logical_not(stays))(far.start)
                pl.when(stays)(near.start)

    blocks = length // KB
    near_blocks = -(-(REACH - 1) // KB)
    turned = line < LINE // 2
    given = 0
    for o in range(blocks):
        first, final = max(0, o - near_blocks), min(blocks - 1, o + near_blocks)
        key_block(
            jnp.where(turned, blocks - 1 - o, o), jnp.where(turned, blocks - 1 - final, first), final - first + 1
        )
        while given < blocks and min(blocks - 1, given + near_blocks) <= o:
            give(jnp.where(turned, blocks - 1 - given, given))
            given = given + 1
    prefix_sum.finish(0)

    lax.fori_loop(0, gather.count, lambda i, x: (gather.drain(i), x)[1], 0)
    token_line.drain()
    prefix_line.drain()
    grad_line.drain()
    if not spread:
        pl.when(holds)(meta_copy.wait_send)
    for p in range(pairs):
        att_copy(p).wait_send()
    for b in range(parts):
        d_copy(b).wait_send()
    for i in range(own_blocks):
        swap_copy(i).wait_send()
        for stays, far, near in grad_pieces(i):
            pl.when(jnp.logical_not(stays))(far.wait_send)
            pl.when(stays)(near.wait)
    out_back.settle()
    arrivals = Line(plan, place, sems.back_send, sems.back_recv)
    for j in range(held):
        chip = j if spread else 2 * core + j
        out_back.receive(refs.pieces.at[j], chip, line // 2)
        arrivals.receive(refs.grad_pieces.at[j], chip, line // 2)
    out_back.drain()


def forward_backward(plan, given):
    held, places, width = given.tokens.shape
    depth = given.w_query.shape[0]
    length = places * plan.tp
    half = length // 2
    pairs = WIDE // PAIR
    bf16, f32 = jnp.bfloat16, jnp.float32
    S = jax.ShapeDtypeStruct
    slots, tasks, part = given.prefix_keys.shape
    kept = -(-slots // 16) * 16
    steps = len(plan.axes)
    reach = max(plan.shape[a] for a in plan.axes) - 1
    outs = dict(
        pieces=S((held, places, width), bf16),
        grad_pieces=S((held, places, width), bf16),
        keys_grad=S((slots, tasks, part), f32),
        values_grad=S((slots, tasks, part), f32),
    )
    scratch = dict(
        source=((KINDS, plan.sides, depth, LANES), bf16),
        prefix=((held, plan.sides, 2, SLOTS, LANES), bf16),
        meta=((8, SLOTS + length), f32),
        whole=((KINDS, 2) + plan.shape + (depth, WIDE), bf16),
        row=((LINE, plan.cores, places, width), bf16),
        grad=((2, plan.cores, places, width), bf16),
        pre=((2, SLOTS, WIDE), bf16),
        q=((length, WIDE), bf16),
        k=((length, WIDE), bf16),
        v=((length, WIDE), bf16),
        att=((length, WIDE), bf16),
        lse=((pairs, 8, length), f32),
        att_other=((half, WIDE), bf16),
        keys=((SLOTS + length, 2 * PAIR), bf16),
        values=((PAIR, SLOTS + length), bf16),
        queries=((PAIR, length), bf16),
        meta_cols=((SLOTS + length, 8), f32),
        normal_one=((half, width), f32),
        rstd_one=((half, LANES), f32),
        normed=((half, width), bf16),
        slope=((2 * GROUPS, half, WIDE), bf16),
        acted=((2 * GROUPS, half, WIDE), bf16),
        acc=((half, width), f32),
        out=((half, width), bf16),
        d_att=((length, WIDE), bf16),
        d_att_away=((half, WIDE), bf16),
        d_pre=((2, SLOTS, WIDE), f32),
        terms=((LINE, 2, SLOTS, LANES), bf16),
        row_terms=((LINE, 2, SLOTS, LANES), bf16),
        total=((tasks, 2, kept, LANES), f32),
        total_other=((tasks, 2, kept, LANES), f32),
        gone=((steps, tasks, 2, kept, LANES), bf16),
        come=((steps, reach, tasks, 2, kept, LANES), bf16),
    )
    sems = gather_semaphores(plan)
    sems.update(
        token_send=semaphores(held),
        token_recv=semaphores(LINE, 2),
        prefix_send=semaphores(held * plan.sides),
        prefix_recv=semaphores(LINE, 2),
        grad_send=semaphores(held),
        grad_recv=semaphores(LINE, 2),
        share_send=semaphores(5),
        share_recv=semaphores(5),
        att_send=semaphores(pairs),
        att_recv=semaphores(pairs),
        d_send=semaphores(half // CHUNK),
        d_recv=semaphores(half // CHUNK),
        out_send=semaphores(4),
        out_recv=semaphores(LINE, 2),
        back_send=semaphores(half // KB, 2),
        back_recv=semaphores(LINE, 2),
        swap_send=semaphores(half // KB),
        swap_recv=semaphores(half // KB),
        terms_send=semaphores(LINE),
        terms_recv=semaphores(LINE, 2),
        total_send=semaphores(1),
        total_recv=semaphores(1),
        sum_send=semaphores(steps, reach),
        sum_recv=semaphores(steps, reach),
    )
    smem = pl.BlockSpec(memory_space=pltpu.SMEM)
    vmem = pl.BlockSpec(memory_space=pltpu.VMEM)
    hbm = pl.BlockSpec(memory_space=pl.ANY)
    results = pl.pallas_call(
        functools.partial(forward_backward_kernel, plan, (*vars(given), *outs, *scratch, *sems)),
        out_shape=list(outs.values()),
        in_specs=[smem, smem, smem, vmem, hbm, hbm] + [vmem] * 12,
        out_specs=[hbm, hbm, vmem, vmem],
        scratch_shapes=[pltpu.VMEM(*spec) for spec in scratch.values()] + list(sems.values()),
        compiler_params=pltpu.CompilerParams(
            collective_id=0, has_side_effects=True, vmem_limit_bytes=63 * 2**20
        ),
    )(*vars(given).values())
    return SimpleNamespace(**dict(zip(outs, results)))


def by_slot(a):
    return jnp.transpose(a, (1, 0, 2))


def shards(
    plan, tokens, w_query, w_key, w_value, w_attn_out, w_up, w_down, first_gain, first_shift,
    second_gain, second_shift, prefix_keys, prefix_values, example_lengths, task_ids, prefix_lens,
    slot_masks, out_grad,
):
    done = forward_backward(
        plan,
        SimpleNamespace(
            task_ids=task_ids,
            lengths=example_lengths,
            prefix_lens=prefix_lens,
            slot_masks=slot_masks,
            tokens=tokens,
            out_grad=out_grad,
            w_query=w_query,
            w_key=w_key,
            w_value=w_value,
            w_attn_out=w_attn_out,
            w_up=w_up,
            w_down=w_down,
            gain_one=first_gain[None],
            shift_one=first_shift[None],
            gain_two=second_gain[None],
            shift_two=second_shift[None],
            prefix_keys=by_slot(prefix_keys),
            prefix_values=by_slot(prefix_values),
        ),
    )
    return done.pieces, done.grad_pieces.astype(jnp.float32), by_slot(done.keys_grad), by_slot(done.values_grad)


def solution(mesh):
    placed = (
        P("rows", "tp", None),
        P("rows", "tp"),
        P("rows", "tp"),
        P("rows", "tp"),
        P("tp", "rows"),
        P("rows", "tp"),
        P("tp", "rows"),
        P(),
        P(),
        P(),
        P(),
        P(None, None, "tp"),
        P(None, None, "tp"),
        P("rows", None),
        P("rows"),
        P(),
        P(),
        P("rows", "tp", None),
    )
    plan = Plan(mesh.shape["rows"], mesh.shape["tp"])
    return jax.shard_map(
        functools.partial(shards, plan),
        mesh=mesh,
        in_specs=placed,
        out_specs=(
            P("rows", "tp", None),
            P("rows", "tp", None),
            P(None, None, "tp"),
            P(None, None, "tp"),
        ),
        check_vma=False,
    )
```

```python
import functools
import math
from types import SimpleNamespace

import jax
import jax.numpy as jnp
from jax import lax
from jax.experimental import pallas as pl
from jax.experimental.pallas import tpu as pltpu
from jax.sharding import PartitionSpec as P

HD = 64
PAIR = 2 * HD
SLOTS = 128
QB = 256
KB = 256
REACH = 512
NEG = -1e30
MARKS = 16
NT = (((1,), (1,)), ((), ()))


def mm(a, b):
    return jnp.dot(a, b, preferred_element_type=jnp.float32)


def mm_nt(a, b):
    return lax.dot_general(a, b, NT, preferred_element_type=jnp.float32)


def head_lanes(half):
    lane = lax.broadcasted_iota(jnp.int32, (1, PAIR), 1)
    return (lane >= half * HD) & (lane < (half + 1) * HD)


def only_head(a, half):
    return jnp.where(head_lanes(half), a, jnp.zeros_like(a))


def key_marks(meta):
    length = meta.shape[1]
    row = lax.broadcasted_iota(jnp.int32, (PAIR, length), 0)
    place = lax.broadcasted_iota(jnp.int32, (PAIR, length), 1)
    seg = meta[0:1, :]
    other = (place >= SLOTS) & (row < 8) & (row.astype(jnp.float32) != seg)
    dead = (place < SLOTS) & (row == 8) & (seg < 0.5)
    ones = (row >= 9) & (row < 12)
    marks = jnp.where(other | dead, NEG, jnp.where(ones, 1.0, 0.0))
    return jnp.transpose(marks).astype(jnp.bfloat16)


def query_marks(meta):
    length = meta.shape[1] - SLOTS
    row = lax.broadcasted_iota(jnp.int32, (MARKS, length), 0)
    seg = meta[0:1, SLOTS:]
    return jnp.where(((row < 8) & (row.astype(jnp.float32) == seg)) | (row == 8), 1.0, 0.0)


def attend_tile(q_t, marks, keys, values):
    scaled = q_t * jnp.asarray(0.125, jnp.bfloat16)
    blank = jnp.zeros((PAIR - MARKS, marks.shape[1]), jnp.bfloat16)
    low_marks = jnp.concatenate([marks.astype(jnp.bfloat16), blank], axis=0)
    mixed, totals = [], []
    zero = jnp.zeros((HD, q_t.shape[1]), jnp.bfloat16)
    ones = jnp.ones((16, keys.shape[0]), jnp.bfloat16)
    for half in range(2):
        rows = slice(half * HD, (half + 1) * HD)
        own = [scaled[rows, :], zero] if half == 0 else [zero, scaled[rows, :]]
        scores = mm(keys, jnp.concatenate([*own, low_marks], axis=0))
        top = jnp.max(scores, axis=0, keepdims=True)
        probs = jnp.exp(scores - top).astype(jnp.bfloat16)
        out = mm(jnp.concatenate([values[rows, :], ones], axis=0), probs)
        total = out[HD : HD + 1, :]
        mixed.append(out[:HD, :] * (1.0 / total))
        totals.append(top + jnp.log(total))
    return jnp.concatenate(mixed, axis=0), totals


def inner_rows(do, att):
    picks = lax.broadcasted_iota(jnp.int32, (8, PAIR), 0)
    lanes = lax.broadcasted_iota(jnp.int32, (8, PAIR), 1) // HD
    picker = jnp.where(picks == lanes, 1.0, 0.0).astype(jnp.bfloat16)
    prod = do.astype(jnp.float32) * att.astype(jnp.float32)
    high = prod.astype(jnp.bfloat16)
    return mm_nt(picker, high) + mm_nt(picker, (prod - high.astype(jnp.float32)).astype(jnp.bfloat16))


def gradient_tile(keys, values, q, do, rows, allowed):
    back = jnp.transpose(keys)
    d_keys = jnp.zeros(keys.shape, jnp.float32)
    d_values = jnp.zeros(keys.shape, jnp.float32)
    d_query = []
    scaled = q * jnp.asarray(0.125, jnp.bfloat16)
    for half in range(2):
        qh, dh = only_head(scaled, half), only_head(do, half)
        scores = jnp.where(allowed, mm_nt(keys, qh), NEG)
        probs = jnp.exp(scores - rows[half : half + 1, :])
        d_scores = (probs * (mm_nt(values, dh) - rows[2 + half : 3 + half, :])).astype(jnp.bfloat16)
        d_keys = d_keys + mm(d_scores, qh)
        d_values = d_values + mm(probs.astype(jnp.bfloat16), dh)
        d_query.append(mm(back[half * HD : (half + 1) * HD, :], d_scores))
    return d_keys, d_values, jnp.concatenate(d_query, axis=0)


MESH = pl.DeviceIdType.MESH
LINE = 4
LANES = 128
WIDE = LINE * LANES
KINDS = 12
FIRST_UP = 4
GROUPS = (KINDS - FIRST_UP) // 2
CHUNK = 256


class Plan:
    def __init__(self, rows, tp):
        self.rows = rows
        self.tp = tp
        self.core_in_tp = tp > LINE
        self.shape = (rows // 8, 2, 4) if self.core_in_tp else (rows // 4, 2, 2)
        self.axes = (0, 1, 2) if self.core_in_tp else (0, 1)
        self.cores = 2 if self.core_in_tp else 1
        self.sides = 2 // self.cores

    def here(self):
        r = lax.axis_index("rows")
        t = lax.axis_index("tp")
        a, b, c = self.shape
        coords = (r // (b * c), lax.rem(r // c, b), lax.rem(r, c))
        if self.core_in_tp:
            return coords, t // 2, lax.rem(t, 2)
        return coords, t, coords[2]

    def device(self, coords, line, core):
        a, b, c = self.shape
        if self.core_in_tp:
            return ((coords[0] * b + coords[1]) * c + coords[2], line * 2 + core)
        return ((coords[0] * b + coords[1]) * c + core, line)

    def row_core(self, chip):
        return None if self.core_in_tp else chip // 2


def shifted(coords, axis, by, size):
    moved = list(coords)
    moved[axis] = lax.rem(coords[axis] + by, size)
    return tuple(moved)


def sibling(plan, place):
    coords, line, core = place
    return plan.device(coords, line, 1 - core)


def greet(plan, place):
    coords, line, core = place
    others = [
        plan.device(coords, lax.rem(line + by, LINE), side) for by in range(1, LINE) for side in range(2)
    ]
    others.append(sibling(plan, place))
    for axis in plan.axes:
        for by in range(1, plan.shape[axis]):
            others.append(plan.device(shifted(coords, axis, by, plan.shape[axis]), line, core))
    barrier = pltpu.get_barrier_semaphore()
    for other in others:
        pl.semaphore_signal(barrier, inc=1, device_id=other, device_id_type=MESH)
    return lambda: pl.semaphore_wait(barrier, len(others))


def remote(src, dst, send, recv, device):
    return pltpu.make_async_remote_copy(
        src_ref=src, dst_ref=dst, send_sem=send, recv_sem=recv, device_id=device, device_id_type=MESH
    )


class Gather:
    def __init__(self, plan, place, source, whole, sems):
        self.plan = plan
        self.place = place
        self.coords, self.line, self.core = place
        self.source = source
        self.whole = whole
        self.sems = sems
        self.count = KINDS * plan.sides
        self.depth = source.shape[-2]
        self.orders = (plan.axes, plan.axes[::-1])
        self.lanes = pl.ds(pl.multiple_of(self.line * LANES, LANES), LANES)

    def unit(self, i):
        if self.plan.core_in_tp:
            return (i, self.core)
        return (i // 2, lax.rem(i, 2))

    def own_copies(self):
        where = tuple(self.coords) + (slice(None), self.lanes)
        for at in range(self.plan.sides):
            side = self.core if self.plan.core_in_tp else at
            yield pltpu.make_async_copy(
                self.source.at[:, at], self.whole.at[(slice(None), side) + where], self.sems.own.at[at]
            )

    def block(self, i, chip):
        lanes = pl.ds(pl.multiple_of(chip * LANES, LANES), LANES)
        return self.whole.at[self.unit(i) + tuple(self.coords) + (slice(None), lanes)]

    def line_copies(self, i):
        src = self.source.at[(i, 0) if self.plan.core_in_tp else self.unit(i)]
        for at, by in enumerate((1, -1, 2, -2)):
            chip = self.line + by
            there = (chip >= 0) & (chip < LINE)
            yield there, remote(
                src, self.block(i, self.line), self.sems.line_send.at[i, at], self.sems.line_recv.at[i, self.line],
                self.plan.device(self.coords, jnp.clip(chip, 0, LINE - 1), self.core),
            )

    def pass_copies(self, i):
        for middle, first, target in ((2, 0, 3), (1, 3, 0)):
            block = self.block(i, first)
            yield self.line == middle, remote(
                block, block, self.sems.line_send.at[i, 4], self.sems.line_recv.at[i, first],
                self.plan.device(self.coords, target, self.core),
            )

    def line_arrived(self, i, chip):
        block = self.block(i, chip)
        remote(
            block, block, self.sems.line_send.at[i, 0], self.sems.line_recv.at[i, chip],
            self.plan.device(self.coords, chip, self.core),
        ).wait_recv()

    def axis_copies(self, i, step):
        rows = self.depth // 2
        for half in range(2):
            order = self.orders[half]
            axis = order[step]
            size = self.plan.shape[axis]
            index = [
                pl.ds(0, self.plan.shape[a]) if a in order[:step] else self.coords[a] for a in range(3)
            ]
            block = self.whole.at[self.unit(i) + tuple(index) + (pl.ds(half * rows, rows),)]
            for by in range(1, size):
                spot = (i, half, step, by - 1)
                yield remote(
                    block, block, self.sems.axis_send.at[spot], self.sems.axis_recv.at[spot],
                    self.plan.device(shifted(self.coords, axis, by, size), self.line, self.core),
                )

    def core_copy(self, i, side):
        if self.plan.core_in_tp:
            block = self.whole.at[i, side]
        else:
            block = self.whole.at[self.unit(i) + (slice(None), slice(None), side)]
        return remote(
            block, block, self.sems.core_send.at[i], self.sems.core_recv.at[i], sibling(self.plan, self.place)
        )

    def core_roles(self, i):
        if self.plan.core_in_tp:
            wide = i >= 3
            return wide, wide
        side = lax.rem(i, 2)
        wide = i >= 6
        return wide | (side != self.core), wide | (side == self.core)

    def start_line(self, i):
        for there, copy in self.line_copies(i):
            pl.when(there)(copy.start)

    def pass_on(self, i):
        for (here, copy), first in zip(self.pass_copies(i), (0, 3)):

            @pl.when(here)
            def _(copy=copy, first=first):
                self.line_arrived(i, first)
                copy.start()

    def start_axis(self, i, step):
        if step == 0:
            for chip in range(LINE):
                passed = ((chip == 0) & (self.line == 2)) | ((chip == 3) & (self.line == 1))
                pl.when((self.line != chip) & jnp.logical_not(passed))(functools.partial(self.line_arrived, i, chip))
        else:
            for copy in self.axis_copies(i, step - 1):
                copy.wait_recv()
        for copy in self.axis_copies(i, step):
            copy.start()

    def start_core(self, i):
        for copy in self.axis_copies(i, len(self.plan.axes) - 1):
            copy.wait_recv()
        sends, _ = self.core_roles(i)
        pl.when(sends)(lambda: self.core_copy(i, self.core).start())

    def finish(self, i):
        _, gets = self.core_roles(i)
        pl.when(gets)(lambda: self.core_copy(i, 1 - self.core).wait_recv())

    def drain(self, i):
        for there, copy in (*self.line_copies(i), *self.pass_copies(i)):
            pl.when(there)(copy.wait_send)
        for step in range(len(self.plan.axes)):
            for copy in self.axis_copies(i, step):
                copy.wait_send()
        sends, _ = self.core_roles(i)
        pl.when(sends)(lambda: self.core_copy(i, self.core).wait_send())

    def tick(self, i, ahead, lag):
        steps = len(self.plan.axes)

        def guarded(at, body):
            pl.when((at >= 0) & (at < self.count))(functools.partial(body, at))

        guarded(i + ahead, self.start_line)
        guarded(i + 1, self.pass_on)
        for step in range(steps):
            guarded(i - lag * step, lambda at, step=step: self.start_axis(at, step))
        guarded(i - lag * steps, self.start_core)

    def ticks(self, lag):
        return self.count + lag * len(self.plan.axes)


def semaphores(*shape):
    return pltpu.SemaphoreType.DMA(shape)


def gather_semaphores(plan):
    count = KINDS * plan.sides
    steps = len(plan.axes)
    reach = max(plan.shape[a] for a in plan.axes) - 1
    return dict(
        line_send=semaphores(count, 5),
        line_recv=semaphores(count, LINE),
        axis_send=semaphores(count, 2, steps, reach),
        axis_recv=semaphores(count, 2, steps, reach),
        core_send=semaphores(count),
        core_recv=semaphores(count),
        own=semaphores(2),
    )


class Line:
    def __init__(self, plan, place, send_sems, recv_sems):
        self.plan = plan
        self.coords, self.line, self.core = place
        self.send_sems = send_sems
        self.recv_sems = recv_sems
        self.pieces = []

    def here(self, chip, side):
        return (chip == self.line) & (side == self.core)

    def add(self, src, dst, chip, side):
        at = len(self.pieces)
        device = self.plan.device(self.coords, chip, side)

        def far(src, dst):
            return remote(src, dst, self.send_sems.at[at], self.recv_sems.at[self.line, self.core], device)

        near = pltpu.make_async_copy(src, dst, self.send_sems.at[at])
        self.pieces.append((self.here(chip, side), src, dst, far, near))

    def start(self, part=0, parts=1):
        for stays, src, dst, far, near in self.pieces:
            rows = src.shape[0] // parts
            cut = pl.ds(pl.multiple_of(part * rows, rows), rows) if parts > 1 else slice(None)
            pl.when(jnp.logical_not(stays))(far(src.at[cut], dst.at[cut]).start)
            pl.when(stays & (part == 0))(near.start)

    def send(self, src, dst, chip, side):
        self.add(src, dst, chip, side)
        stays, src, dst, far, near = self.pieces[-1]
        pl.when(jnp.logical_not(stays))(far(src, dst).start)
        pl.when(stays)(near.start)

    def settle(self):
        for stays, *_, near in self.pieces:
            pl.when(stays)(near.wait)

    def drain(self):
        for stays, src, dst, far, _ in self.pieces:
            pl.when(jnp.logical_not(stays))(far(src, dst).wait_send)

    def receive(self, dst, chip, side):
        copy = remote(
            dst, dst, self.send_sems.at[0], self.recv_sems.at[chip, side],
            self.plan.device(self.coords, chip, side),
        )
        pl.when(jnp.logical_not(self.here(chip, side)))(copy.wait_recv)


class Sibling:
    def __init__(self, plan, place, send_sems, recv_sems):
        self.send_sems = send_sems
        self.recv_sems = recv_sems
        self.device = sibling(plan, place)

    def copy(self, src, dst, at):
        return remote(src, dst, self.send_sems.at[at], self.recv_sems.at[at], self.device)


class PrefixSum:
    def __init__(self, plan, place, refs):
        self.plan = plan
        self.place = place
        self.refs = refs
        self.coords, self.line, self.core = place
        self.terms = Line(plan, place, refs.terms_send, refs.terms_recv)
        self.last = Sibling(plan, place, refs.total_send, refs.total_recv)

    def start(self):
        refs = self.refs
        for chip in range(LINE):
            lanes = slice(chip * LANES, (chip + 1) * LANES)
            for which in range(2):
                refs.terms[chip, which] = refs.d_pre[which, :, lanes].astype(jnp.bfloat16)
            refs.terms[chip, 0, SLOTS - 16 :, :] = jnp.broadcast_to(refs.meta[1:2, 0:SLOTS], (16, SLOTS)).astype(
                jnp.bfloat16
            )
        for chip in range(LINE):
            self.terms.send(refs.terms.at[chip], refs.row_terms.at[self.line], chip, self.core)

    def copies(self, step):
        refs = self.refs
        axis = self.plan.axes[step]
        size = self.plan.shape[axis]
        return [
            remote(
                refs.gone.at[step], refs.come.at[step, by - 1], refs.sum_send.at[step, by - 1],
                refs.sum_recv.at[step, by - 1],
                self.plan.device(shifted(self.coords, axis, by, size), self.line, self.core),
            )
            for by in range(1, size)
        ]

    def send(self, step):
        self.refs.gone[step] = self.refs.total[...].astype(jnp.bfloat16)
        for copy in self.copies(step):
            copy.start()

    def line_sum(self):
        refs = self.refs
        total = refs.total
        tasks, _, kept = total.shape[:3]
        self.terms.settle()
        for chip in range(LINE):
            self.terms.receive(refs.row_terms.at[chip], chip, self.core)
            marks = refs.row_terms[chip, 0, SLOTS - 16 :, :].astype(jnp.float32)
            for task in range(tasks):
                for which in range(2):
                    more = refs.row_terms[chip, which, 0:kept, :].astype(jnp.float32) * marks[0:1, task : task + 1]
                    total[task, which] = more if chip == 0 else total[task, which] + more

    def receive(self, step):
        for by, copy in enumerate(self.copies(step)):
            copy.wait_recv()
            self.refs.total[...] += self.refs.come[step, by].astype(jnp.float32)

    def go_on(self, beat):
        steps = len(self.plan.axes)
        if beat == 0:
            self.line_sum()
        elif beat <= steps:
            self.receive(beat - 1)
        if beat < steps:
            self.send(beat)
        elif beat == steps and not self.plan.core_in_tp:
            self.last.copy(self.refs.total, self.refs.total_other, 0).start()

    def put(self, block, lanes):
        refs = self.refs
        slots, tasks = refs.keys_grad.shape[:2]
        for task in range(tasks):
            refs.keys_grad[:, task, lanes] = block[task, 0, 0:slots, :]
            refs.values_grad[:, task, lanes] = block[task, 1, 0:slots, :]

    def finish(self, beats):
        refs = self.refs
        steps = len(self.plan.axes)
        for beat in range(beats, steps + 1):
            self.go_on(beat)
        if self.plan.core_in_tp:
            self.put(refs.total, slice(None))
        else:
            self.last.copy(refs.total, refs.total_other, 0).wait_recv()
            sides = slice(0, LANES), slice(LANES, 2 * LANES)
            for side in range(2):

                @pl.when(self.core == side)
                def _(side=side):
                    self.put(refs.total, sides[side])
                    self.put(refs.total_other, sides[1 - side])

            self.last.copy(refs.total, refs.total_other, 0).wait_send()
        self.terms.drain()
        for step in range(steps):
            for copy in self.copies(step):
                copy.wait_send()


def normalise(z):
    mean = jnp.mean(z, axis=1, keepdims=True)
    centred = z - mean
    rstd = lax.rsqrt(jnp.mean(centred * centred, axis=1, keepdims=True) + 1e-05)
    return centred * rstd, rstd


def normalise_grad(normal, rstd, gain, grad):
    g = grad * gain
    return rstd * (
        g - jnp.mean(g, axis=1, keepdims=True) - normal * jnp.mean(g * normal, axis=1, keepdims=True)
    )


def up_kind(j):
    return FIRST_UP + j + jnp.maximum(j - 1, 0) if not isinstance(j, int) else FIRST_UP + j + max(j - 1, 0)


def down_kind(j):
    return jnp.minimum(FIRST_UP + 2 + 2 * j, KINDS - 1) if not isinstance(j, int) else min(FIRST_UP + 2 + 2 * j, KINDS - 1)


def put_blocks(plan, source, kind, block, first):
    for side in range(plan.sides):
        at = (first + side) * LANES
        source[kind, side] = block[:, at : at + LANES]


def first_inputs(plan, refs):
    for kind, block in enumerate((refs.w_query, refs.w_key, refs.w_value)):
        put_blocks(plan, refs.source, kind, block, 0)


def other_inputs(plan, place, refs):
    coords, line, core = place
    source, prefix, meta = refs.source, refs.prefix, refs.meta
    sides = plan.sides
    put_blocks(plan, source, 3, jnp.transpose(refs.w_attn_out[...]), 0)
    down = jnp.transpose(refs.w_down[...])
    for j in range(GROUPS):
        put_blocks(plan, source, up_kind(j), refs.w_up, j * sides)
        put_blocks(plan, source, down_kind(j), down, j * sides)

    slots, tasks = refs.prefix_keys.shape[:2]
    prefix[...] = jnp.zeros_like(prefix)
    tables = [ref[...].astype(jnp.float32) for ref in (refs.prefix_keys, refs.prefix_values)]
    for j in range(refs.tokens.shape[0]):
        task = refs.task_ids[j]
        for which, table in enumerate(tables):
            rows = table[:, 0, :]
            for t in range(1, tasks):
                rows = jnp.where(task == t, table[:, t, :], rows)
            rows = rows.astype(jnp.bfloat16)
            for side in range(sides):
                prefix[j, side, which, 0:slots, :] = rows[:, side * LANES : (side + 1) * LANES]

    def tables():
        mine = line if plan.core_in_tp else lax.rem(line, 2)
        task = refs.task_ids[mine]
        meta[...] = jnp.zeros_like(meta)
        length = meta.shape[1] - SLOTS
        spots = lax.broadcasted_iota(jnp.int32, (1, length), 1)
        lane = lax.broadcasted_iota(jnp.int32, (1, SLOTS), 1)
        segment = jnp.zeros((1, length), jnp.float32)
        ends = jnp.zeros((1, SLOTS), jnp.float32)
        end = jnp.int32(0)
        for j in range(refs.lengths.shape[1]):
            end = end + refs.lengths[mine, j]
            segment = segment + jnp.where(spots >= end, 1.0, 0.0)
            ends = jnp.where(lane == j, end.astype(jnp.float32), ends)
        masks = refs.slot_masks
        used = jnp.zeros((1, slots), jnp.int32)
        limit = jnp.int32(0)
        for t in range(masks.shape[0]):
            used = jnp.where(task == t, masks[t : t + 1, :], used)
            limit = jnp.where(task == t, refs.prefix_lens[t], limit)
        live = jnp.where((used == 1) & (lane[:, :slots] < limit), 1.0, 0.0)
        meta[0:1, 0:slots] = live
        meta[0:1, SLOTS:] = segment
        meta[1:2, 0:SLOTS] = jnp.where(lane == task, 1.0, 0.0)
        meta[2:3, 0:SLOTS] = ends

    if plan.core_in_tp:
        tables()
    else:
        pl.when(line // 2 == core)(tables)


AHEAD = 3
LAG = 2
CUTS = 8
TOKENS = 4
ATT_BEATS = 1
QKV_BEATS = 3
MIX_BEATS = 2
ACT_BEATS = 1
SPAN = 1024
UNROLL = 2
GRADS = 14


def forward_backward_kernel(plan, names, *args):
    refs = SimpleNamespace(**dict(zip(names, args)))
    sems = refs
    place = plan.here()
    coords, line, core = place
    bf16, f32 = jnp.bfloat16, jnp.float32
    spread = plan.core_in_tp
    tokens, row, grad, pre = refs.tokens, refs.row, refs.grad, refs.pre
    whole, meta = refs.whole, refs.meta
    q, k, v, att, lse = refs.q, refs.k, refs.v, refs.att, refs.lse
    held = tokens.shape[0]
    width = row.shape[-1]
    length = q.shape[0]
    half = length // 2
    base = 0 if spread else 2 * core
    slot = core if spread else 0
    holds = None if spread else line // 2 == core

    greeted = greet(plan, place)
    first_inputs(plan, refs)
    greeted()

    gather = Gather(plan, place, refs.source, whole, sems)
    for i in range(AHEAD):
        gather.start_line(i)
    other_inputs(plan, place, refs)
    token_line = Line(plan, place, sems.token_send, sems.token_recv)
    for j in range(held):
        token_line.add(tokens.at[j], row.at[line, slot], base + j, core)
    grad_line = Line(plan, place, sems.grad_send, sems.grad_recv)
    for j in range(held):
        grad_line.add(refs.out_grad.at[j], grad.at[lax.rem(line, 2), slot], base + j, line // 2)
    for copy in gather.own_copies():
        copy.start()
    share = Sibling(plan, place, sems.share_send, sems.share_recv)
    meta_copy = share.copy(meta, meta, 4)
    if not spread:
        pl.when(holds)(meta_copy.start)
    for copy in gather.own_copies():
        copy.wait()

    last = gather.ticks(LAG)

    grads = min(GRADS, last - CUTS)

    def beat(i, x=0):
        gather.tick(i, AHEAD, LAG)
        pl.when((i >= TOKENS) & (i < TOKENS + CUTS))(lambda: token_line.start(i - TOKENS, CUTS))
        pl.when((i >= grads) & (i < grads + CUTS))(lambda: grad_line.start(i - grads, CUTS))
        return x

    gather.pass_on(0)
    steps = LAG * len(plan.axes) + 1
    done = TOKENS + CUTS
    lax.fori_loop(0, done, beat, 0)
    prefix_line = Line(plan, place, sems.prefix_send, sems.prefix_recv)
    for j in range(held):
        for side in range(plan.sides):
            prefix_line.send(
                refs.prefix.at[j, side], pre.at[:, :, gather.lanes], base + j, core if spread else side
            )

    token_line.settle()

    def share_token(chip):
        if spread:
            token_line.receive(row.at[chip, core], chip, core)
            share.copy(row.at[chip, core], row.at[chip, core], chip).start()
        else:
            @pl.when(holds)
            def _():
                token_line.receive(row.at[chip, 0], chip, core)
                share.copy(row.at[chip, 0], row.at[chip, 0], chip).start()

    for chip in range(LINE):
        share_token(chip)
    for chip in range(LINE):
        if spread:
            share.copy(row.at[chip, 1 - core], row.at[chip, 1 - core], chip).wait_recv()
        else:
            pl.when(jnp.logical_not(holds))(share.copy(row.at[chip, 0], row.at[chip, 0], chip).wait_recv)
    if not spread:
        pl.when(jnp.logical_not(holds))(meta_copy.wait_recv)
    prefix_line.settle()
    for chip in range(LINE):
        prefix_line.receive(pre.at[:, :, pl.ds(chip * LANES, LANES)], chip, core if spread else line // 2)
    refs.meta_cols[...] = jnp.transpose(meta[...])

    def ready(first, amount, done):
        until = min(last, first + amount - 1 + steps)
        if until > done:
            lax.fori_loop(done, until, beat, 0)
        for i in range(first, first + amount):
            gather.finish(i)
        return max(done, until)

    for kind, target in enumerate((q, k, v)):
        done = ready(kind * plan.sides, plan.sides, done)
        weight = whole.at[kind, core]

        def project(b, x, weight=weight, target=target):
            block = row[b].reshape(CHUNK, width)
            target[pl.ds(pl.multiple_of(b * CHUNK, CHUNK), CHUNK), :] = mm(
                block, weight[...].reshape(width, WIDE)
            ).astype(bf16)
            return x

        lax.fori_loop(0, LINE, project, 0)
        if kind < QKV_BEATS:
            beat(done)
            done = done + 1
    att_share = Sibling(plan, place, sems.att_send, sems.att_recv)
    here = pl.ds(pl.multiple_of(core * half, half), half)
    there = pl.ds(pl.multiple_of((1 - core) * half, half), half)
    keys, values, queries = refs.keys, refs.values, refs.queries
    keys[:, PAIR:] = key_marks(meta)

    def pair_lanes(p):
        return pl.ds(pl.multiple_of(p * PAIR, PAIR), PAIR)

    def att_copy(p):
        lanes = pair_lanes(p)
        return att_share.copy(att.at[there, lanes], refs.att_other.at[:, lanes], p)

    def pair(p, x):
        lanes = pair_lanes(p)
        queries[...] = jnp.transpose(q[:, lanes])
        keys[0:SLOTS, 0:PAIR] = pre[0, :, lanes]
        keys[SLOTS:, 0:PAIR] = k[:, lanes]
        values[:, 0:SLOTS] = jnp.transpose(pre[1, :, lanes])
        values[:, SLOTS:] = jnp.transpose(v[:, lanes])
        if ATT_BEATS > 0:
            beat(done + ATT_BEATS * p)
        for first in range(0, length, SPAN):
            rows = slice(first, first + SPAN)
            mixed, totals = attend_tile(queries[:, rows], query_marks(meta)[:, rows], keys[...], values[...])
            att[rows, lanes] = jnp.transpose(mixed).astype(bf16)
            lse[p, 0:1, rows] = totals[0]
            lse[p, 1:2, rows] = totals[1]
        if ATT_BEATS > 1:
            beat(done + ATT_BEATS * p + 1)
        att_copy(p).start()
        return x

    pairs = WIDE // PAIR
    lax.fori_loop(0, pairs, pair, 0)
    done = done + ATT_BEATS * pairs
    for p in range(pairs):
        att_copy(p).wait_recv()

    done = ready(3 * plan.sides, plan.sides, done)
    normal_one, rstd_one, normed, acc = refs.normal_one, refs.rstd_one, refs.normed, refs.acc
    low, slope, out = refs.normed, refs.slope, refs.out
    parts = half // CHUNK

    def weight(kind, side):
        return whole[kind, side].reshape(width, WIDE)

    def mix(b):
        rows = pl.ds(pl.multiple_of(b * CHUNK, CHUNK), CHUNK)
        own = att[pl.ds(pl.multiple_of(core * half + b * CHUNK, CHUNK), CHUNK), :]
        total = row[2 * core + b].reshape(CHUNK, width).astype(f32)
        total = total + mm_nt(own, weight(3, core)) + mm_nt(refs.att_other[rows, :], weight(3, 1 - core))
        normal, rstd = normalise(total)
        normal_one[rows, :] = normal
        rstd_one[rows, :] = jnp.broadcast_to(rstd, (CHUNK, LANES))
        low_normed = (normal * refs.gain_one[...] + refs.shift_one[...]).astype(bf16)
        normed[rows, :] = low_normed
        acc[rows, :] = low_normed.astype(f32)
        if b < MIX_BEATS:
            beat(done + b)

    for b in range(parts):
        mix(b)
    done = done + min(parts, MIX_BEATS)

    acted = refs.acted
    chunks = [slice(b * CHUNK, (b + 1) * CHUNK) for b in range(parts)]

    def act(j, done):
        def unit(side, x):
            for rows in chunks:
                upper = mm(normed[rows, :], weight(up_kind(j), side))
                bell = (1.0 + lax.erf(upper * (0.5**0.5))) * 0.5
                acted[2 * j + side, rows, :] = (upper * bell).astype(bf16)
                slope[2 * j + side, rows, :] = (
                    bell + upper * jnp.exp(upper * upper * -0.5) * (1.0 / (2.0 * math.pi) ** 0.5)
                ).astype(bf16)
            if ACT_BEATS > 0:
                beat(done + side)
            return x

        lax.fori_loop(0, 2, unit, 0)

    def add(j, done):
        for rows in chunks:
            acc[rows, :] += mm_nt(acted[2 * j, rows, :], weight(down_kind(j), 0)) + mm_nt(
                acted[2 * j + 1, rows, :], weight(down_kind(j), 1)
            )

    steps_of = sorted([(up_kind(j), act, j) for j in range(GROUPS)] + [(down_kind(j), add, j) for j in range(GROUPS)], key=lambda s: s[0])
    for kind, body, j in steps_of:
        done = ready(kind * plan.sides, plan.sides, done)
        body(j, done)
        done = done + 2 if body is act and ACT_BEATS > 0 else done

    grad_line.settle()
    for part in range(2):
        for side in range(plan.cores):
            grad_line.receive(grad.at[part, side], 2 * core + part, side if spread else line // 2)

    def close(b, x):
        rows = pl.ds(pl.multiple_of(b * CHUNK, CHUNK), CHUNK)
        normal, rstd = normalise(acc[rows, :])
        out[rows, :] = (normal * refs.gain_two[...] + refs.shift_two[...]).astype(bf16)
        d_second = normalise_grad(
            normal, rstd, refs.gain_two[...], grad[b].reshape(CHUNK, width).astype(f32)
        )
        acc[rows, :] = d_second
        low[rows, :] = d_second.astype(bf16)
        return x

    lax.fori_loop(0, parts, close, 0)
    places = tokens.shape[1]
    out_back = Line(plan, place, sems.out_send, sems.out_recv)
    for b in range(2):
        for side in range(plan.cores):
            spot, target = (line, side) if spread else (lax.rem(line, 2), line // 2)
            out_back.send(
                out.at[pl.ds((b * plan.cores + side) * places, places)], refs.pieces.at[spot],
                2 * core + b, target,
            )

    def feed_back(j, x):
        d_upper = [
            (mm(low[...], weight(down_kind(j), side)) * slope[2 * j + side].astype(f32)).astype(bf16)
            for side in range(2)
        ]
        acc[...] += mm_nt(d_upper[0], weight(up_kind(j), 0)) + mm_nt(d_upper[1], weight(up_kind(j), 1))
        return x

    lax.fori_loop(0, GROUPS, feed_back, 0, unroll=2)

    d_att, away = refs.d_att, refs.d_att_away
    d_share = Sibling(plan, place, sems.d_send, sems.d_recv)

    def d_copy(b):
        mine = pl.ds(pl.multiple_of(core * half + b * CHUNK, CHUNK), CHUNK)
        return d_share.copy(away.at[pl.ds(pl.multiple_of(b * CHUNK, CHUNK), CHUNK)], d_att.at[mine], b)

    def open_(b, x):
        rows = pl.ds(pl.multiple_of(b * CHUNK, CHUNK), CHUNK)
        d_first = normalise_grad(normal_one[rows, :], rstd_one[rows, 0:1], refs.gain_one[...], acc[rows, :])
        acc[rows, :] = d_first
        d_low = d_first.astype(bf16)
        away[rows, :] = mm(d_low, weight(3, 1 - core)).astype(bf16)
        d_copy(b).start()
        mine = pl.ds(pl.multiple_of(core * half + b * CHUNK, CHUNK), CHUNK)
        d_att[mine, :] = mm(d_low, weight(3, core)).astype(bf16)
        return x

    for chip in range(LINE):
        if spread:
            share.copy(row.at[chip, core], row.at[chip, core], chip).wait_send()
        else:
            pl.when(holds)(share.copy(row.at[chip, 0], row.at[chip, 0], chip).wait_send)
    lax.fori_loop(0, parts, open_, 0)
    for b in range(parts):
        d_copy(b).wait_recv()

    def pair_inner(p, x):
        lanes = pair_lanes(p)
        lse[p, 2:4, :] = inner_rows(d_att[:, lanes], att[:, lanes])[0:2]
        return x

    lax.fori_loop(0, pairs, pair_inner, 0, unroll=True)
    columns, dq_acc = refs.meta_cols, normal_one
    d_queries, d_keys, d_values = (
        acted.at[pl.ds(n * length // half, length // half)] for n in range(3)
    )
    d_pre = refs.d_pre

    def prefix_pair(p, x):
        lanes = pair_lanes(p)
        live = columns[0:SLOTS, 0:1] > 0.5
        a, g, dq = gradient_tile(pre[0, :, lanes], pre[1, :, lanes], q[:, lanes], d_att[:, lanes], lse[p], live)
        d_pre[0, :, lanes] = a
        d_pre[1, :, lanes] = g
        dq_acc[lanes, :] = dq
        return x

    lax.fori_loop(0, pairs, prefix_pair, 0, unroll=UNROLL)
    prefix_sum = PrefixSum(plan, place, refs)
    prefix_sum.start()

    def key_block(kb, first, count):
        rows = pl.ds(pl.multiple_of(kb * KB, KB), KB)
        span = pl.ds(pl.multiple_of(first * KB, KB), count * KB)
        seg_k = columns[pl.ds(pl.multiple_of(SLOTS + kb * KB, SLOTS), KB), 0:1]
        part, at = kb * KB // half, pl.ds(pl.multiple_of(lax.rem(kb * KB, half), KB), KB)

        def one(p, x):
            lanes = pair_lanes(p)
            allowed = seg_k == meta[0:1, pl.ds(pl.multiple_of(SLOTS + first * KB, SLOTS), count * KB)]
            a, g, dq = gradient_tile(
                k[rows, lanes], v[rows, lanes], q[span, lanes], d_att[span, lanes], lse[p, :, span], allowed
            )
            d_keys[part, at, lanes] = a.astype(bf16)
            d_values[part, at, lanes] = g.astype(bf16)
            dq_acc[lanes, span] += dq
            return x

        lax.fori_loop(0, pairs, one, 0, unroll=UNROLL)

    swap = Sibling(plan, place, sems.swap_send, sems.swap_recv)
    spare = row
    own_blocks = half // KB

    def swap_copy(i):
        return swap.copy(spare.at[i], spare.at[own_blocks + i], i)

    def grad_pieces(i):
        for side in range(plan.cores):
            spot, target = (line, side) if spread else (lax.rem(line, 2), line // 2)
            chip = own_blocks * core + i
            src = low.at[pl.ds(pl.multiple_of(i * KB + side * places, places), places)]
            dst = refs.grad_pieces.at[spot]
            stays = (chip == line) & (target == core)
            sem = sems.back_send.at[i, side]
            yield stays, remote(
                src, dst, sem, sems.back_recv.at[line, core], plan.device(coords, chip, target)
            ), pltpu.make_async_copy(src, dst, sem)

    def give(b):
        rows = pl.ds(pl.multiple_of(lax.rem(b * KB, half), KB), KB)
        part = b * KB // half
        span = pl.ds(pl.multiple_of(b * KB, KB), KB)
        i = lax.rem(b, own_blocks)
        d_queries[part, rows, :] = (jnp.transpose(dq_acc[:, span]) * 0.125).astype(bf16)
        term = mm_nt(d_queries[part, rows, :], weight(0, core))
        term = term + mm_nt(d_keys[part, rows, :], weight(1, core))
        term = term + mm_nt(d_values[part, rows, :], weight(2, core))
        owner = b // own_blocks

        @pl.when(core != owner)
        def _():
            spare[i] = term.astype(bf16).reshape(spare.shape[1:])
            swap_copy(i).start()

        @pl.when(core == owner)
        def _():
            own = term + acc[rows, :]
            swap_copy(i).wait_recv()
            low[rows, :] = (own + spare[own_blocks + i].reshape(KB, width).astype(f32)).astype(bf16)
            for stays, far, near in grad_pieces(i):
                pl.when(jnp.logical_not(stays))(far.start)
                pl.when(stays)(near.start)

    blocks = length // KB
    near_blocks = -(-(REACH - 1) // KB)
    turned = line < LINE // 2
    given = 0
    for o in range(blocks):
        first, final = max(0, o - near_blocks), min(blocks - 1, o + near_blocks)
        key_block(
            jnp.where(turned, blocks - 1 - o, o), jnp.where(turned, blocks - 1 - final, first), final - first + 1
        )
        while given < blocks and min(blocks - 1, given + near_blocks) <= o:
            give(jnp.where(turned, blocks - 1 - given, given))
            given = given + 1
    prefix_sum.finish(0)

    lax.fori_loop(0, gather.count, lambda i, x: (gather.drain(i), x)[1], 0)
    token_line.drain()
    prefix_line.drain()
    grad_line.drain()
    if not spread:
        pl.when(holds)(meta_copy.wait_send)
    for p in range(pairs):
        att_copy(p).wait_send()
    for b in range(parts):
        d_copy(b).wait_send()
    for i in range(own_blocks):
        swap_copy(i).wait_send()
        for stays, far, near in grad_pieces(i):
            pl.when(jnp.logical_not(stays))(far.wait_send)
            pl.when(stays)(near.wait)
    out_back.settle()
    arrivals = Line(plan, place, sems.back_send, sems.back_recv)
    for j in range(held):
        chip = j if spread else 2 * core + j
        out_back.receive(refs.pieces.at[j], chip, line // 2)
        arrivals.receive(refs.grad_pieces.at[j], chip, line // 2)
    out_back.drain()


def forward_backward(plan, given):
    held, places, width = given.tokens.shape
    depth = given.w_query.shape[0]
    length = places * plan.tp
    half = length // 2
    pairs = WIDE // PAIR
    bf16, f32 = jnp.bfloat16, jnp.float32
    S = jax.ShapeDtypeStruct
    slots, tasks, part = given.prefix_keys.shape
    kept = -(-slots // 16) * 16
    steps = len(plan.axes)
    reach = max(plan.shape[a] for a in plan.axes) - 1
    outs = dict(
        pieces=S((held, places, width), bf16),
        grad_pieces=S((held, places, width), bf16),
        keys_grad=S((slots, tasks, part), f32),
        values_grad=S((slots, tasks, part), f32),
    )
    scratch = dict(
        source=((KINDS, plan.sides, depth, LANES), bf16),
        prefix=((held, plan.sides, 2, SLOTS, LANES), bf16),
        meta=((8, SLOTS + length), f32),
        whole=((KINDS, 2) + plan.shape + (depth, WIDE), bf16),
        row=((LINE, plan.cores, places, width), bf16),
        grad=((2, plan.cores, places, width), bf16),
        pre=((2, SLOTS, WIDE), bf16),
        q=((length, WIDE), bf16),
        k=((length, WIDE), bf16),
        v=((length, WIDE), bf16),
        att=((length, WIDE), bf16),
        lse=((pairs, 8, length), f32),
        att_other=((half, WIDE), bf16),
        keys=((SLOTS + length, 2 * PAIR), bf16),
        values=((PAIR, SLOTS + length), bf16),
        queries=((PAIR, length), bf16),
        meta_cols=((SLOTS + length, 8), f32),
        normal_one=((half, width), f32),
        rstd_one=((half, LANES), f32),
        normed=((half, width), bf16),
        slope=((2 * GROUPS, half, WIDE), bf16),
        acted=((2 * GROUPS, half, WIDE), bf16),
        acc=((half, width), f32),
        out=((half, width), bf16),
        d_att=((length, WIDE), bf16),
        d_att_away=((half, WIDE), bf16),
        d_pre=((2, SLOTS, WIDE), f32),
        terms=((LINE, 2, SLOTS, LANES), bf16),
        row_terms=((LINE, 2, SLOTS, LANES), bf16),
        total=((tasks, 2, kept, LANES), f32),
        total_other=((tasks, 2, kept, LANES), f32),
        gone=((steps, tasks, 2, kept, LANES), bf16),
        come=((steps, reach, tasks, 2, kept, LANES), bf16),
    )
    sems = gather_semaphores(plan)
    sems.update(
        token_send=semaphores(held),
        token_recv=semaphores(LINE, 2),
        prefix_send=semaphores(held * plan.sides),
        prefix_recv=semaphores(LINE, 2),
        grad_send=semaphores(held),
        grad_recv=semaphores(LINE, 2),
        share_send=semaphores(5),
        share_recv=semaphores(5),
        att_send=semaphores(pairs),
        att_recv=semaphores(pairs),
        d_send=semaphores(half // CHUNK),
        d_recv=semaphores(half // CHUNK),
        out_send=semaphores(4),
        out_recv=semaphores(LINE, 2),
        back_send=semaphores(half // KB, 2),
        back_recv=semaphores(LINE, 2),
        swap_send=semaphores(half // KB),
        swap_recv=semaphores(half // KB),
        terms_send=semaphores(LINE),
        terms_recv=semaphores(LINE, 2),
        total_send=semaphores(1),
        total_recv=semaphores(1),
        sum_send=semaphores(steps, reach),
        sum_recv=semaphores(steps, reach),
    )
    smem = pl.BlockSpec(memory_space=pltpu.SMEM)
    vmem = pl.BlockSpec(memory_space=pltpu.VMEM)
    hbm = pl.BlockSpec(memory_space=pl.ANY)
    results = pl.pallas_call(
        functools.partial(forward_backward_kernel, plan, (*vars(given), *outs, *scratch, *sems)),
        out_shape=list(outs.values()),
        in_specs=[smem, smem, smem, vmem, hbm, hbm] + [vmem] * 12,
        out_specs=[hbm, hbm, vmem, vmem],
        scratch_shapes=[pltpu.VMEM(*spec) for spec in scratch.values()] + list(sems.values()),
        compiler_params=pltpu.CompilerParams(
            collective_id=0, has_side_effects=True, vmem_limit_bytes=63 * 2**20
        ),
    )(*vars(given).values())
    return SimpleNamespace(**dict(zip(outs, results)))


def by_slot(a):
    return jnp.transpose(a, (1, 0, 2))


def shards(
    plan, tokens, w_query, w_key, w_value, w_attn_out, w_up, w_down, first_gain, first_shift,
    second_gain, second_shift, prefix_keys, prefix_values, example_lengths, task_ids, prefix_lens,
    slot_masks, out_grad,
):
    done = forward_backward(
        plan,
        SimpleNamespace(
            task_ids=task_ids,
            lengths=example_lengths,
            prefix_lens=prefix_lens,
            slot_masks=slot_masks,
            tokens=tokens,
            out_grad=out_grad,
            w_query=w_query,
            w_key=w_key,
            w_value=w_value,
            w_attn_out=w_attn_out,
            w_up=w_up,
            w_down=w_down,
            gain_one=first_gain[None],
            shift_one=first_shift[None],
            gain_two=second_gain[None],
            shift_two=second_shift[None],
            prefix_keys=by_slot(prefix_keys),
            prefix_values=by_slot(prefix_values),
        ),
    )
    return done.pieces, done.grad_pieces.astype(jnp.float32), by_slot(done.keys_grad), by_slot(done.values_grad)


def solution(mesh):
    placed = (
        P("rows", "tp", None),
        P("rows", "tp"),
        P("rows", "tp"),
        P("rows", "tp"),
        P("tp", "rows"),
        P("rows", "tp"),
        P("tp", "rows"),
        P(),
        P(),
        P(),
        P(),
        P(None, None, "tp"),
        P(None, None, "tp"),
        P("rows", None),
        P("rows"),
        P(),
        P(),
        P("rows", "tp", None),
    )
    plan = Plan(mesh.shape["rows"], mesh.shape["tp"])
    return jax.shard_map(
        functools.partial(shards, plan),
        mesh=mesh,
        in_specs=placed,
        out_specs=(
            P("rows", "tp", None),
            P("rows", "tp", None),
            P(None, None, "tp"),
            P(None, None, "tp"),
        ),
        check_vma=False,
    )
```
